32 devices in a mesh: shard: 4 (over y, core), context: 2 (over x), tensor: 4 (over z).
Axes of the slice: x: 2, y: 2, z: 4, core: 2. Of those that a mesh axis runs over, the one named last changes fastest.
Arguments:
- tokens: bfloat16 [16, 1024, 1024], P('shard', 'context'), may hold values from -6 to 6
- norm_gain: bfloat16 [1024], replicated, may hold values from 0.099609375 to 1.8984375
- w_in: bfloat16 [3, 1024, 1024], P(None, 'shard', 'tensor'), may hold values from -0.1875 to 0.1875
- conv_weight: bfloat16 [3, 1024], P(None, 'tensor'), may hold values from -3 to 3
- convolution_out_weight: bfloat16 [1024, 1024], P('tensor', 'shard'), may hold values from -0.1875 to 0.1875
- ffn_gain: bfloat16 [1024], replicated, may hold values from 0.099609375 to 1.8984375
- w_gate: bfloat16 [1024, 4608], P('shard', 'tensor'), may hold values from -0.1875 to 0.1875
- w_up: bfloat16 [1024, 4608], P('shard', 'tensor'), may hold values from -0.1875 to 0.1875
- w_down: bfloat16 [4608, 1024], P('tensor', 'shard'), may hold values from -0.09375 to 0.09375
- cotangent: bfloat16 [16, 1024, 1024], P('shard', 'context'), may hold values from -6 to 6
Outputs:
- block_out: bfloat16 [16, 1024, 1024], P('shard', 'context')
- grad_tokens: float32 [16, 1024, 1024], P('shard', 'context')
- grad_norm_gain: float32 [1024], replicated
- grad_w_in: float32 [3, 1024, 1024], P(None, 'shard', 'tensor')
- grad_conv: float32 [3, 1024], P(None, 'tensor')
- out_weight_gradient: float32 [1024, 1024], P('tensor', 'shard')
- grad_ffn_gain: float32 [1024], replicated
- grad_w_gate: float32 [1024, 4608], P('shard', 'tensor')
- up_weight_gradient: float32 [1024, 4608], P('shard', 'tensor')
- grad_w_down: float32 [4608, 1024], P('tensor', 'shard')
The draws below stay inside these ranges and needn't reach their ends.
All inputs are finite; a program needn't handle non-finite values.
Results may differ from the reference program's by a relative error of at most 0.014.
Values may be sent and summed in bfloat16 or wider, within the bound.
No kernel may reach another device: no remote copies, remote signals or barrier semaphores. Data moves between devices by JAX's collectives and lax.ppermute only.
A program may use at most 192 MiB of HBM per device.

```python
import math
import jax
import jax.numpy as jnp
from jax import lax

D = 1024
FF = 4608
KW = 3
LEN = 1024
SEQS = 16


def steps_of(stream_key, dims, split, least, largest):
    level, own = 1.0, jax.random.fold_in(stream_key, 6)
    for dim, parts in split:
        heights = jnp.exp(jax.random.uniform(jax.random.fold_in(own, dim), (parts,), jnp.float32, least / len(split), largest / len(split)))
        level = level * jnp.repeat(heights, dims[dim] // parts).reshape([-1 if axis == dim else 1 for axis in range(len(dims))])
    return level


def bell_draw(own_key, shape, deviation, limit, pieces=(), dtype=jnp.bfloat16):
    drawn = jax.random.normal(own_key, shape, jnp.float32) * deviation
    if len(pieces) > 0:
        drawn = steps_of(own_key, shape, pieces, -0.22, 0.18) * drawn
    return jnp.clip(drawn, min=-limit, max=limit).astype(dtype)


def setup_inputs(seed: int = 0) -> dict:
    streams_of = jax.random.split(jax.random.key(seed), 11)
    return {
        "tokens": bell_draw(streams_of[0], (SEQS, LEN, D), 1.0, 6.0, ((0, 4), (1, 2))),
        "norm_gain": jnp.clip(1.0 + 0.18 * jax.random.normal(streams_of[1], (D,), jnp.float32), 0.099609375, 1.8984375).astype(jnp.bfloat16),
        "w_in": bell_draw(streams_of[2], (3, D, D), D ** -0.5, 0.1875, ((1, 4), (2, 4))),
        "conv_weight": bell_draw(streams_of[3], (KW, D), 0.6, 3.0, ((1, 4),)),
        "convolution_out_weight": bell_draw(streams_of[4], (D, D), D ** -0.5, 0.1875, ((0, 4), (1, 4))),
        "ffn_gain": jnp.clip(1.0 + 0.18 * jax.random.normal(streams_of[5], (D,), jnp.float32), 0.099609375, 1.8984375).astype(jnp.bfloat16),
        "w_gate": bell_draw(streams_of[6], (D, FF), D ** -0.5, 0.1875, ((0, 4), (1, 4))),
        "w_up": bell_draw(streams_of[7], (D, FF), D ** -0.5, 0.1875, ((0, 4), (1, 4))),
        "w_down": bell_draw(streams_of[8], (FF, D), FF ** -0.5, 0.09375, ((0, 4), (1, 4))),
        "cotangent": bell_draw(streams_of[9], (SEQS, LEN, D), 1.0, 6.0, ((0, 4), (1, 2))),
    }


EPSILON = 1e-05
HIGH_PRECISION = lax.Precision.HIGHEST

@jax.custom_vjp
def low(v):
    return lax.optimization_barrier(v.astype(jnp.bfloat16)).astype(jnp.float32)

@jax.custom_vjp
def reduced_precision_backward(v):
    return v

def low_keep(v):
    return (low(v), None)

def low_pass(kept, grad):
    return (grad,)

def back_keep(v):
    return (v, None)

def back_low(kept, grad):
    return (low(grad),)
low.defvjp(low_keep, low_pass)
reduced_precision_backward.defvjp(back_keep, back_low)

def scaled(values, gain):
    return values * lax.rsqrt(lax.optimization_barrier(jnp.mean(values * values, axis=-1, keepdims=True)) + EPSILON) * gain

def delayed(values, steps):
    padded = jnp.pad(values, ((0, 0), (steps, 0), (0, 0)))
    return padded[:, :values.shape[1], :]

def forward(input_rows, norm_gain, w_in, conv_weight, convolution_out_weight, ffn_gain, w_gate, w_up, w_down):
    first_normalized = low(scaled(input_rows, norm_gain))
    projection = reduced_precision_backward(jnp.einsum('gld,kdc->kglc', first_normalized, w_in, precision=HIGH_PRECISION))
    in_gate = projection[0]
    out_gate = projection[1]
    conv_input = projection[2]
    product = low(in_gate * conv_input)
    convolved = conv_weight[0] * product + conv_weight[1] * delayed(product, 1) + conv_weight[2] * delayed(product, 2)
    convolved = reduced_precision_backward(convolved)
    gated_product = low(out_gate * convolved)
    residual_middle = input_rows + reduced_precision_backward(jnp.einsum('jsf,fp->jsp', gated_product, convolution_out_weight, precision=HIGH_PRECISION))
    second_normalized = low(scaled(residual_middle, ffn_gain))
    gate_branch = reduced_precision_backward(jnp.einsum('gld,df->glf', second_normalized, w_gate, precision=HIGH_PRECISION))
    up_projection_branch = reduced_precision_backward(jnp.einsum('gld,df->glf', second_normalized, w_up, precision=HIGH_PRECISION))
    hidden_state = low(jax.nn.silu(gate_branch) * up_projection_branch)
    return residual_middle + reduced_precision_backward(jnp.einsum('glf,fd->gld', hidden_state, w_down, precision=HIGH_PRECISION))

def reference(tokens, norm_gain, w_in, conv_weight, convolution_out_weight, ffn_gain, w_gate, w_up, w_down, cotangent):
    weights = tuple((item.astype(jnp.float32) for item in (norm_gain, w_in, conv_weight, convolution_out_weight, ffn_gain, w_gate, w_up, w_down)))
    group = math.gcd(SEQS, 4)
    blocks = SEQS // group
    input_rows = tokens.astype(jnp.float32).reshape(blocks, group, LEN, D)
    tangents = cotangent.astype(jnp.float32).reshape(blocks, group, LEN, D)

    def step(totals, pair):
        block, tangent = pair
        result, pullback = jax.vjp(forward, block, *weights)
        grads = pullback(tangent)
        summed = tuple((total + grad for total, grad in zip(totals, grads[1:])))
        return (summed, (result, grads[0]))
    zeros = tuple((jnp.zeros_like(item) for item in weights))
    totals, outputs = lax.scan(step, zeros, (input_rows, tangents))
    results, input_grads = outputs
    return (results.reshape(SEQS, LEN, D).astype(jnp.bfloat16), input_grads.reshape(SEQS, LEN, D), totals[0], totals[1], totals[2], totals[3], totals[4], totals[5], totals[6], totals[7])
```

```python
import functools

import jax
import jax.numpy as jnp
from jax import lax
from jax.experimental import pallas as pl
from jax.experimental.pallas import tpu as pltpu
from jax.sharding import PartitionSpec as P

EPSILON = 1e-05
F32 = jnp.float32
BF16 = jnp.bfloat16
VMEM_LIMIT = 56 * 1024 * 1024
LEAD = 16


def norm_forward(values):
    inverse = lax.rsqrt(jnp.mean(values * values, axis=-1, keepdims=True) + EPSILON)
    return (values * inverse, inverse)


def norm_backward(grad_normed, plain, inverse, gain):
    grad_plain = grad_normed * gain
    return inverse * (
        grad_plain - plain * jnp.mean(grad_plain * plain, axis=-1, keepdims=True)
    )


def dot_nn(a, b):
    return lax.dot_general(a, b, (((1,), (0,)), ((), ())), preferred_element_type=F32)


def dot_nt(a, b):
    return lax.dot_general(a, b, (((1,), (1,)), ((), ())), preferred_element_type=F32)


def dot_tn(a, b):
    return lax.dot_general(a, b, (((0,), (0,)), ((), ())), preferred_element_type=F32)


def rounded(value):
    return lax.optimization_barrier(value.astype(BF16))


def shifted(value, steps):
    count = lax.axis_size("tensor")
    return lax.ppermute(value, "tensor", [(i, (i + steps) % count) for i in range(count)])


def swapped(value, axis, bit):
    count = lax.axis_size(axis)
    return lax.ppermute(value, axis, [(i, i ^ bit) for i in range(count)])


def to_core(value):
    return swapped(value, "shard", 1)


def to_y(value):
    return swapped(value, "shard", 2)


def to_x(value):
    return swapped(value, "context", 1)


def inward(value):
    return lax.ppermute(value, "tensor", [(0, 1), (3, 2)])


def across(value):
    return lax.ppermute(value, "tensor", [(1, 2), (2, 1)])


def outward(value):
    return lax.ppermute(value, "tensor", [(1, 0), (2, 3)])


def together(*values):
    return lax.optimization_barrier(values)


def added(*values):
    return sum(value.astype(F32) for value in values).astype(BF16)


def mixer_forward_kernel(ids, rows, mine, other, *rest):
    gated, weights = rest[-2:]
    part = mine.shape[1]
    half = 2 * part + LEAD

    @pl.when(pl.program_id(0) == 0)
    def _():
        for bit, piece in enumerate((mine, other)):
            for far in range(2):
                start = pl.multiple_of((ids[0] ^ (bit + 2 * far)) * part, part)
                for side in range(2):
                    first = 2 * (ids[2] ^ side)
                    base = (2 * far + side) * half
                    for which in range(2):
                        weights[0, first + which, pl.ds(start, part), :] = piece[
                            base + which * part : base + (which + 1) * part, :
                        ]

    taps = mine[2 * part : half, :].astype(F32)
    values = rows[0]
    product = dot_nn(values, weights[0, 0]) * dot_nn(values, weights[0, 2])
    product = product.astype(BF16).astype(F32)
    convolved = (
        taps[0:1] * product
        + taps[1:2] * pltpu.roll(product, 1, 0)
        + taps[2:3] * pltpu.roll(product, 2, 0)
    )[LEAD:]
    gated[0] = (dot_nn(values[LEAD:], weights[0, 1]) * convolved).astype(BF16)


def mixer_forward(ids, rows, pieces, block, earlier):
    seqs, long, model = rows.shape
    width = long - LEAD
    part = pieces[0].shape[1]
    count = model // part
    specs = [pl.BlockSpec((1, long, model), lambda q, ids: (q, 0, 0))]
    specs += [pl.BlockSpec(piece.shape, lambda q, ids: (0, 0)) for piece in pieces]
    specs += [pl.BlockSpec(memory_space=pl.ANY)] * len(earlier)
    return pl.pallas_call(
        mixer_forward_kernel,
        grid_spec=pltpu.PrefetchScalarGridSpec(
            num_scalar_prefetch=1,
            grid=(seqs,),
            in_specs=specs,
            out_specs=[
                pl.BlockSpec((1, width, part), lambda q, ids: (q, 0, block)),
                pl.BlockSpec((1, 4, model, part), lambda q, ids: (block, 0, 0, 0)),
            ],
        ),
        out_shape=[
            jax.ShapeDtypeStruct((seqs, width, model), BF16),
            jax.ShapeDtypeStruct((count, 4, model, part), BF16),
        ],
        input_output_aliases={4: 0, 5: 1} if earlier else {},
        compiler_params=pltpu.CompilerParams(vmem_limit_bytes=VMEM_LIMIT),
        cost_estimate=pl.CostEstimate(
            flops=2 * seqs * long * model * 3 * part, bytes_accessed=10 * 2**20, transcendentals=0
        ),
        name="mixer_forward",
    )(ids, rows, *pieces, *earlier)


def middle_kernel(ids, gated, weights, tokens, gain, normed, own):
    seq, tile = pl.program_id(0), pl.program_id(1)
    count, _, _, part = weights.shape
    size = tokens.shape[1]
    values = tokens[0].astype(F32)
    for block in range(count):
        values += dot_nt(gated[0, :, block * part : (block + 1) * part], weights[block, 0])
    plain, _ = norm_forward(values)
    normed[0] = (plain * gain[...].astype(F32)).astype(BF16)

    @pl.when(seq == ids[1])
    def _():
        own[pl.ds(pl.multiple_of(tile * size, size), size), :] = values


def middle(ids, gated, weights, tokens, gain):
    seqs, width, model = tokens.shape
    count, _, _, part = weights.shape
    size = width // 2
    tile = pl.BlockSpec((1, size, model), lambda q, i, ids: (q, i, 0))
    return pl.pallas_call(
        middle_kernel,
        grid_spec=pltpu.PrefetchScalarGridSpec(
            num_scalar_prefetch=1,
            grid=(seqs, 2),
            in_specs=[
                tile,
                pl.BlockSpec((count, 1, model, part), lambda q, i, ids: (0, 3, 0, 0)),
                tile,
                pl.BlockSpec((1, model), lambda q, i, ids: (0, 0)),
            ],
            out_specs=[tile, pl.BlockSpec((width, model), lambda q, i, ids: (0, 0))],
        ),
        out_shape=[
            jax.ShapeDtypeStruct(tokens.shape, BF16),
            jax.ShapeDtypeStruct((width, model), F32),
        ],
        compiler_params=pltpu.CompilerParams(vmem_limit_bytes=VMEM_LIMIT),
        cost_estimate=pl.CostEstimate(
            flops=2 * seqs * width * model * model, bytes_accessed=16 * 2**20, transcendentals=0
        ),
        name="middle",
    )(ids, gated, weights, tokens, gain)


def feedforward_kernel(ids, normed, cotangent, piece0, piece1, piece2, piece3, *rest):
    down, grad_normed, hidden, grad_gate, grad_up, weights, arrived = rest[-7:]
    part = piece0.shape[0] // 3
    first = jnp.logical_and(pl.program_id(0) == 0, pl.program_id(1) == 0)

    def copies(which):
        for place, piece in enumerate((piece0, piece1, piece2, piece3)):
            start = pl.multiple_of((ids[0] ^ place) * part, part)
            yield pltpu.make_async_copy(
                piece.at[pl.ds(which * part, part), :],
                weights.at[which, pl.ds(start, part), :],
                arrived.at[which, place],
            )

    @pl.when(first)
    def _():
        for which in range(3):
            for copy in copies(which):
                copy.start()
        for copy in copies(0):
            copy.wait()

    values = normed[0]
    gate = dot_nn(values, weights[0])

    @pl.when(first)
    def _():
        for which in (1, 2):
            for copy in copies(which):
                copy.wait()

    up = dot_nn(values, weights[1])
    grad_hidden = dot_nn(cotangent[0], weights[2])
    sigmoid = jax.nn.sigmoid(gate)
    silu = gate * sigmoid
    hidden_now = (silu * up).astype(BF16)
    hidden[0] = hidden_now
    gate_now = (grad_hidden * up * sigmoid * (1.0 + gate * (1.0 - sigmoid))).astype(BF16)
    up_now = (grad_hidden * silu).astype(BF16)
    grad_gate[0] = gate_now
    grad_up[0] = up_now
    grad_normed[0] = (dot_nt(gate_now, weights[0]) + dot_nt(up_now, weights[1])).astype(BF16)
    down[0] = dot_nt(hidden_now, weights[2]).astype(BF16)


def feedforward(ids, normed, cotangent, pieces, first, blocks, earlier):
    seqs, width, model = normed.shape
    units = pieces[0].shape[1]
    size = width // 2

    def seq(b, i, ids):
        return (ids[3 + first + b], i, 0)

    def own(b, i, ids):
        return (b, i, 0)

    wide = jax.ShapeDtypeStruct((seqs, width, units), BF16)
    return pl.pallas_call(
        feedforward_kernel,
        grid_spec=pltpu.PrefetchScalarGridSpec(
            num_scalar_prefetch=1,
            grid=(blocks, 2),
            in_specs=[
                pl.BlockSpec((1, size, model), seq),
                pl.BlockSpec((1, size, model), seq),
            ]
            + [pl.BlockSpec(memory_space=pl.ANY)] * (4 + len(earlier)),
            out_specs=[
                pl.BlockSpec((1, size, model), own),
                pl.BlockSpec((1, size, model), own),
                pl.BlockSpec((1, size, units), seq),
                pl.BlockSpec((1, size, units), seq),
                pl.BlockSpec((1, size, units), seq),
            ],
            scratch_shapes=[
                pltpu.VMEM((3, model, units), BF16),
                pltpu.SemaphoreType.DMA((3, 4)),
            ],
        ),
        out_shape=[
            jax.ShapeDtypeStruct((blocks, width, model), BF16),
            jax.ShapeDtypeStruct((blocks, width, model), BF16),
            wide,
            wide,
            wide,
        ],
        input_output_aliases={7: 2, 8: 3, 9: 4} if earlier else {},
        compiler_params=pltpu.CompilerParams(vmem_limit_bytes=VMEM_LIMIT),
        cost_estimate=pl.CostEstimate(
            flops=12 * blocks * width * model * units,
            bytes_accessed=8 * 2**20 + blocks * 8 * 2**20,
            transcendentals=0,
        ),
        name="feedforward",
    )(ids, normed, cotangent, *pieces, *earlier)


def mixer_backward_kernel(
    ids, part0, part1, part2, part3, own, cotangent, gain, rows, weights, taps,
    grad_middle, grad_mixed, gain_grad, grad_convolved, grad_out_gate, in_gate, conv_input, tap_grads,
):
    @pl.when(pl.program_id(0) == 0)
    def _():
        incoming = sum(part[...].astype(F32) for part in (part0, part1, part2, part3))
        plain, inverse = norm_forward(own[...])
        gain_grad[...] = jnp.sum(incoming * plain, axis=0, keepdims=True)
        total = cotangent[0].astype(F32) + norm_backward(
            incoming, plain, inverse, gain[...].astype(F32)
        )
        grad_middle[...] = total
        grad_mixed[...] = total.astype(BF16)

    tap = taps[0].astype(F32)
    values = rows[0]
    first = dot_nn(values, weights[0, 0])
    third = dot_nn(values, weights[0, 2])
    out_gate = dot_nn(values[LEAD:], weights[0, 1])
    product = (first * third).astype(BF16).astype(F32)
    recent, previous, earlier = (
        product[LEAD:], pltpu.roll(product, 1, 0)[LEAD:], pltpu.roll(product, 2, 0)[LEAD:],
    )
    convolved = tap[0:1] * recent + tap[1:2] * previous + tap[2:3] * earlier
    in_gate[...] = first[LEAD:]
    conv_input[...] = third[LEAD:]
    grad_gated = dot_nn(grad_mixed[...], weights[0, 3])
    grad_out_gate[...] = (grad_gated * convolved).astype(BF16)
    low = (grad_gated * out_gate).astype(BF16)
    grad_convolved[...] = low
    low = low.astype(F32)
    tap_grads[0] = jnp.concatenate(
        [
            jnp.sum(low * recent, axis=0, keepdims=True),
            jnp.sum(low * previous, axis=0, keepdims=True),
            jnp.sum(low * earlier, axis=0, keepdims=True),
            jnp.zeros((5, low.shape[1]), F32),
        ]
    )


def mixer_backward(ids, parts, own, cotangent, gain, rows, weights, taps):
    width, model = own.shape
    long = rows.shape[1]
    count, _, _, part = weights.shape
    whole = pl.BlockSpec((width, model), lambda j, ids: (0, 0))
    line = pl.BlockSpec((1, model), lambda j, ids: (0, 0))
    column = pl.BlockSpec((width, part), lambda j, ids: (0, j))
    return pl.pallas_call(
        mixer_backward_kernel,
        grid_spec=pltpu.PrefetchScalarGridSpec(
            num_scalar_prefetch=1,
            grid=(count,),
            in_specs=[
                whole, whole, whole, whole, whole,
                pl.BlockSpec((1, width, model), lambda j, ids: (ids[1], 0, 0)),
                line,
                pl.BlockSpec((1, long, model), lambda j, ids: (ids[1], 0, 0)),
                pl.BlockSpec((1, 4, model, part), lambda j, ids: (j, 0, 0, 0)),
                pl.BlockSpec((1, LEAD, part), lambda j, ids: (j, 0, 0)),
            ],
            out_specs=[
                whole, whole, line, column, column, column, column,
                pl.BlockSpec((1, 8, part), lambda j, ids: (j, 0, 0)),
            ],
        ),
        out_shape=[
            jax.ShapeDtypeStruct((width, model), F32),
            jax.ShapeDtypeStruct((width, model), BF16),
            jax.ShapeDtypeStruct((1, model), F32),
            jax.ShapeDtypeStruct((width, model), BF16),
            jax.ShapeDtypeStruct((width, model), BF16),
            jax.ShapeDtypeStruct((width, model), F32),
            jax.ShapeDtypeStruct((width, model), F32),
            jax.ShapeDtypeStruct((count, 8, part), F32),
        ],
        compiler_params=pltpu.CompilerParams(vmem_limit_bytes=VMEM_LIMIT),
        cost_estimate=pl.CostEstimate(
            flops=8 * width * model * model, bytes_accessed=24 * 2**20, transcendentals=0
        ),
        name="mixer_backward",
    )(ids, *parts, own, cotangent, gain, rows, weights, taps)


def input_backward_kernel(
    ids, grad_convolved, edge, in_gate, conv_input, grad_out_gate, taps, weights, grad_middle, tokens, gain,
    grad_first, grad_third, grad_tokens, gain_grad, total,
):
    block = pl.program_id(0)
    width = grad_convolved.shape[0]
    tap = taps[0].astype(F32)
    longer = jnp.concatenate([grad_convolved[...], edge[...]]).astype(F32)
    count = longer.shape[0]
    grad_product = (
        tap[0:1] * longer
        + tap[1:2] * pltpu.roll(longer, count - 1, 0)
        + tap[2:3] * pltpu.roll(longer, count - 2, 0)
    )[:width]
    first = (grad_product * conv_input[...]).astype(BF16)
    third = (grad_product * in_gate[...]).astype(BF16)
    grad_first[...] = first
    grad_third[...] = third
    here = (
        dot_nt(first, weights[0, 0])
        + dot_nt(grad_out_gate[...], weights[0, 1])
        + dot_nt(third, weights[0, 2])
    )

    @pl.when(block == 0)
    def _():
        total[...] = here

    @pl.when(block > 0)
    def _():
        total[...] += here

    @pl.when(block == pl.num_programs(0) - 1)
    def _():
        incoming = total[...]
        plain, inverse = norm_forward(tokens[0].astype(F32))
        gain_grad[...] = jnp.sum(incoming * plain, axis=0, keepdims=True)
        grad_tokens[...] = (
            grad_middle[...] + norm_backward(incoming, plain, inverse, gain[...].astype(F32))
        ).astype(BF16)


def input_backward(
    ids, grad_convolved, edge, in_gate, conv_input, grad_out_gate, taps, weights, grad_middle, tokens, gain
):
    width, model = grad_middle.shape
    count, _, _, part = weights.shape
    whole = pl.BlockSpec((width, model), lambda j, ids: (0, 0))
    line = pl.BlockSpec((1, model), lambda j, ids: (0, 0))
    column = pl.BlockSpec((width, part), lambda j, ids: (0, j))
    return pl.pallas_call(
        input_backward_kernel,
        grid_spec=pltpu.PrefetchScalarGridSpec(
            num_scalar_prefetch=1,
            grid=(count,),
            in_specs=[
                column,
                pl.BlockSpec((edge.shape[0], part), lambda j, ids: (0, j)),
                column, column, column,
                pl.BlockSpec((1, LEAD, part), lambda j, ids: (j, 0, 0)),
                pl.BlockSpec((1, 4, model, part), lambda j, ids: (j, 0, 0, 0)),
                whole,
                pl.BlockSpec((1, width, model), lambda j, ids: (ids[1], 0, 0)),
                line,
            ],
            out_specs=[column, column, whole, line],
            scratch_shapes=[pltpu.VMEM((width, model), F32)],
        ),
        out_shape=[
            jax.ShapeDtypeStruct((width, model), BF16),
            jax.ShapeDtypeStruct((width, model), BF16),
            jax.ShapeDtypeStruct((width, model), BF16),
            jax.ShapeDtypeStruct((1, model), F32),
        ],
        compiler_params=pltpu.CompilerParams(vmem_limit_bytes=VMEM_LIMIT),
        cost_estimate=pl.CostEstimate(
            flops=6 * width * model * model, bytes_accessed=20 * 2**20, transcendentals=0
        ),
        name="input_backward",
    )(ids, grad_convolved, edge, in_gate, conv_input, grad_out_gate, taps, weights, grad_middle, tokens, gain)


def of_core(value, core, axis):
    size = value.shape[axis] // 4
    return jnp.concatenate(
        [lax.dynamic_slice_in_dim(value, (2 * y + core) * size, size, axis) for y in range(2)], axis
    )


def pick(value, index, axis):
    return lax.dynamic_index_in_dim(value, index, axis, keepdims=False)


def local_by_links(
    tokens, norm_gain, w_in, conv_weight, convolution_out_weight, ffn_gain, w_gate, w_up, w_down, cotangent
):
    seqs, width, model = tokens.shape
    part = w_in.shape[1]
    units = w_gate.shape[1]
    shard, side, level = (lax.axis_index(name) for name in ("shard", "context", "tensor"))
    core, y = shard % 2, shard // 2
    end = jnp.logical_or(level == 0, level == 3)
    order = [
        jnp.where(level < 2, 3, 0), jnp.where(level < 2, 2, 1), level ^ 1, level,
    ]
    ids = jnp.stack([shard, level, side] + order).astype(jnp.int32)
    gain_one = norm_gain.reshape(1, model)
    gain_two = ffn_gain.reshape(1, model)
    def from_others(in_one, in_two, in_three):
        (inside, over, out_one), (over_end, out_two), out_three = in_one, in_two, in_three
        return (
            jnp.where(end, out_one, inside),
            jnp.where(end, out_two, over_end),
            jnp.where(end, out_three, over),
        )

    def placed(own, others, dtype):
        out = jnp.zeros((seqs, width, model), dtype)
        for bits, block in enumerate((own,) + others):
            out = lax.dynamic_update_slice(out, block.astype(dtype)[None], (level ^ bits, 0, 0))
        return out

    taps_near = jnp.concatenate([conv_weight, jnp.zeros((LEAD - 3, part), BF16)])
    near = jnp.concatenate(
        [w_in[0], w_in[1], taps_near, w_in[2], convolution_out_weight.T, taps_near]
    )
    half = near.shape[0] // 2

    def sides(value):
        return [lax.dynamic_slice_in_dim(value, (side ^ bit) * half, half, 0) for bit in range(2)]

    near, near_side, near_else = together(near, *sides(near))
    far = to_y(near)
    near_right, near_left = shifted(near_side, -1), shifted(near_side, 1)
    edge = lax.ppermute(tokens[:, width - 2 :, :], "context", [(0, 1)])
    feed = jnp.concatenate([w_gate, w_up, w_down.T])
    far, near_right, near_left, edge, feed, near_side, near_else = together(
        far, near_right, near_left, edge, feed, near_side, near_else
    )

    far_side, far_else = together(*sides(far))
    far_right, far_left = shifted(far_side, -1), shifted(far_side, 1)
    near_over = to_x(jnp.concatenate([near_right, near_left]))
    feed_far = to_y(feed)
    mine = together(jnp.concatenate([near_side, near_else, far_side, far_else]))[0]
    other = to_core(mine)
    rows = jnp.concatenate([jnp.zeros((seqs, LEAD - 2, model), BF16), edge, tokens], axis=1).astype(F32)
    rows = (norm_forward(rows)[0] * gain_one.astype(F32)).astype(BF16)
    state = mixer_forward(ids, rows, (mine, other), 0, ())
    far_right, far_left, near_over, near_right, near_left, rows, feed, cotangent, *state = together(
        far_right, far_left, near_over, near_right, near_left, rows, feed, cotangent, *state
    )

    near_far, far_far = shifted(near_right, -1), shifted(far_left, 1)
    far_over = to_x(jnp.concatenate([far_right, far_left]))
    feed_core = to_core(feed)
    cotangent_flat = cotangent.reshape(seqs * width, model)
    cot_send, cot_keep = of_core(cotangent_flat, 1 - core, 1), of_core(cotangent_flat, core, 1)
    near_far, far_far, far_over, feed_core, cot_send, cot_keep, *state = together(
        near_far, far_far, far_over, feed_core, cot_send, cot_keep, *state
    )

    last_over = to_x(jnp.concatenate([near_far, far_far]))
    for block, rows_of, (a, b) in (
        (1, slice(None, half), (near_right, far_right)),
        (3, slice(half, None), (near_left, far_left)),
    ):
        mine = together(jnp.concatenate([a, near_over[rows_of], b, far_over[rows_of]]))[0]
        state = mixer_forward(ids, rows, (mine, to_core(mine)), block, state)
    last_over, feed_far, *state = together(last_over, feed_far, *state)

    mine = together(jnp.concatenate([near_far, last_over[:half], far_far, last_over[half:]]))[0]
    state = mixer_forward(ids, rows, (mine, to_core(mine)), 2, state)
    gated, weights = state
    feed_far_core = to_core(feed_far)
    pieces = (feed, feed_core, feed_far, feed_far_core)
    taps = jnp.stack([near_side[2 * part :], near_right[2 * part :], near_far[2 * part :], near_left[2 * part :]])
    normed, middle_own = middle(ids, gated, weights, tokens, gain_two)
    normed_flat = normed.reshape(seqs * width, model)

    down0, grad0, *wide = feedforward(ids, normed, cotangent, pieces, 0, 1, ())
    down0, grad0, *wide = together(down0[0], grad0[0], *wide)

    grad_in0 = inward(grad0)
    down12, grad12, *wide = feedforward(ids, normed, cotangent, pieces, 1, 2, tuple(wide))
    grad1, grad2, down1, down2 = grad12[0], grad12[1], down12[0], down12[1]
    grad_in0, grad1, grad2, down1, down2, normed_flat, *wide = together(
        grad_in0, grad1, grad2, down1, down2, normed_flat, *wide
    )

    def matrix_gradient(left, right):
        received = to_core(dot_tn(left[0], right).astype(BF16))
        return added(dot_tn(left[1], right).astype(BF16), received)

    def by_y(kept):
        kept = kept.reshape(2, -1, kept.shape[-1])
        return pick(kept, y, 0), pick(kept, 1 - y, 0)

    grad_in1 = inward(grad1)
    grad_over0 = across(added(grad0, grad_in0))
    down3, grad3, hidden, grad_gate, grad_up = feedforward(
        ids, normed, cotangent, pieces, 3, 1, tuple(wide)
    )
    hidden, grad_gate, grad_up = (v.reshape(seqs * width, units) for v in (hidden, grad_gate, grad_up))
    normed_pair = of_core(normed_flat, 1 - core, 1), of_core(normed_flat, core, 1)
    kept_down = matrix_gradient((cot_send, cot_keep), hidden)
    grad_in1, grad_over0, grad_gate, grad_up, kept_down, *normed_pair = together(
        grad_in1, grad_over0, grad_gate, grad_up, kept_down, *normed_pair
    )

    grad_in2 = inward(grad2)
    grad_over1 = across(added(grad1, grad_in1))
    grad_out = outward(added(grad2, grad_over0))
    own_down, send = by_y(kept_down)
    y_down = to_y(send)
    kept_gate = matrix_gradient(normed_pair, grad_gate)
    kept_up = matrix_gradient(normed_pair, grad_up)
    grad_in2, grad_over1, grad_out, y_down, kept_gate, kept_up, down0 = together(
        grad_in2, grad_over1, grad_out, y_down, kept_gate, kept_up, down0
    )

    down_in0 = inward(down0)
    mine_down = rounded(added(own_down, y_down))
    x_down = to_x(mine_down)
    own_gate, send_gate = by_y(kept_gate)
    own_up, send_up = by_y(kept_up)
    y_both = to_y(jnp.concatenate([send_gate, send_up]))
    (
        grad_middle, grad_mixed, gain_two_grad, grad_convolved, grad_out_gate, in_gate, conv_input, tap_grads,
    ) = mixer_backward(
        ids, (grad3[0], grad_in2, grad_over1, grad_out), middle_own, cotangent, gain_two, rows, weights, taps
    )
    behind = lax.ppermute(grad_convolved[:LEAD], "context", [(1, 0)])
    grad_zero, grad_third, tokens_own, gain_one_grad = input_backward(
        ids, grad_convolved, behind, in_gate, conv_input, grad_out_gate, taps, weights, grad_middle,
        tokens, gain_one,
    )
    total_down = (mine_down.astype(F32) + x_down.astype(F32)).T
    (
        down_in0, y_both, tokens_own, grad_zero, grad_third, grad_mixed, grad_out_gate, gated, rows, total_down,
    ) = together(
        down_in0, y_both, tokens_own, grad_zero, grad_third, grad_mixed, grad_out_gate, gated, rows, total_down,
    )

    tokens_in = inward(tokens_own)
    tokens_over = across(tokens_own)
    tokens_out1 = outward(tokens_own)
    mine_both = rounded(added(jnp.concatenate([own_gate, own_up]), y_both))
    rows_own = pick(rows, level, 0)[LEAD:]
    gated_own = pick(gated, level, 0)
    rows_send, rows_keep = of_core(rows_own, 1 - core, 1), of_core(rows_own, core, 1)
    mixed_send, mixed_keep = of_core(grad_mixed, 1 - core, 1), of_core(grad_mixed, core, 1)

    def mixer_gradients(pairs, *others):
        send = jnp.concatenate([dot_tn(left[0], right).astype(BF16) for left, right in pairs])
        received = to_core(together(send, *others)[0])
        kept = jnp.concatenate([dot_tn(left[1], right).astype(BF16) for left, right in pairs])
        return added(kept, received).reshape(2, 2, 2, part // 2, model)

    early = mixer_gradients(
        (((rows_send, rows_keep), grad_out_gate), ((mixed_send, mixed_keep), gated_own))
    )
    late = mixer_gradients(
        (((rows_send, rows_keep), grad_zero), ((rows_send, rows_keep), grad_third)), early
    )
    tokens_in, tokens_over, tokens_out1, early, late, mine_both, down1, down2 = together(
        tokens_in, tokens_over, tokens_out1, early, late, mine_both, down1, down2
    )

    down_in1 = inward(down1)
    x_both = to_x(mine_both)
    tokens_over_end = across(tokens_in)
    tokens_out2 = outward(tokens_over)
    early_y = to_y(pick(early, 1 - y, 1))
    total_both = mine_both.astype(F32) + x_both.astype(F32)
    total_gate, total_up = total_both[:part], total_both[part:]
    down_in1, tokens_over_end, tokens_out2, early_y, down2, total_gate, total_up = together(
        down_in1, tokens_over_end, tokens_out2, early_y, down2, total_gate, total_up
    )

    down_in2 = inward(down2)
    down_over0 = across(added(down0, down_in0))
    tokens_out3 = outward(tokens_over_end)
    late_y = to_y(pick(late, 1 - y, 1))
    early = added(pick(early, y, 1), early_y)
    early_x = to_x(pick(early, 1 - side, 1))
    down_in2, down_over0, tokens_out3, late_y, early_x = together(
        down_in2, down_over0, tokens_out3, late_y, early_x
    )

    down_over1 = across(added(down1, down_in1))
    down_out = outward(added(down2, down_over0))
    early = added(pick(early, side, 1), early_x)
    late = added(pick(late, y, 1), late_y)
    late_x = to_x(pick(late, 1 - side, 1))
    tap_rows = tap_grads[:, :3].transpose(1, 0, 2)
    tap_rows = jnp.roll(tap_rows, level, axis=1).reshape(3, model)
    small = jnp.concatenate([gain_one_grad, gain_two_grad, tap_rows, jnp.zeros((3, model), F32)])
    small = small + to_core(small)
    small = small + to_y(small)
    grad_tokens = placed(
        tokens_own,
        from_others((tokens_in, tokens_over, tokens_out1), (tokens_over_end, tokens_out2), tokens_out3),
        F32,
    )
    down_over1, down_out, late_x, small, grad_tokens = together(
        down_over1, down_out, late_x, small, grad_tokens
    )

    out_own = rounded(
        middle_own
        + sum(value.astype(F32) for value in (down3[0], down_in2, down_over1, down_out))
    )
    out_in = inward(out_own)
    out_over = across(out_own)
    out_out1 = outward(out_own)
    late = added(pick(late, side, 1), late_x)
    both = jnp.concatenate([early, late]).reshape(4, part // 2, 4, part)
    blocks = [pick(both, (place - level) % 4, 2) for place in order]
    small = small + to_x(small)
    out_in, out_over, out_out1, small, *blocks = together(out_in, out_over, out_out1, small, *blocks)

    out_over_end = across(out_in)
    out_out2 = outward(out_over)
    mixer_in = inward(jnp.stack(blocks[:3]))
    small = small + swapped(small, "tensor", 1)
    out_over_end, out_out2, mixer_in, small = together(out_over_end, out_out2, mixer_in, small)

    out_out3 = outward(out_over_end)
    mixer_over = across(added(jnp.stack(blocks[:2]), mixer_in[:2]))
    mixer_out = outward(added(blocks[2], mixer_over[0]))
    mine = rounded(
        sum(value.astype(F32) for value in (blocks[3], mixer_in[2], mixer_over[1], mixer_out))
    )
    other = to_x(mine)
    mixer = jnp.concatenate(
        [jnp.where(side == 0, mine, other), jnp.where(side == 0, other, mine)], axis=1
    ).astype(F32)
    total_in = jnp.stack([mixer[2], mixer[0], mixer[3]])
    total_out = mixer[1].T
    small = small + swapped(small, "tensor", 2)
    total_taps = lax.dynamic_slice(small, (2, level * part), (3, part))
    block_out = placed(
        out_own, from_others((out_in, out_over, out_out1), (out_over_end, out_out2), out_out3), BF16
    )
    return (
        block_out, grad_tokens, small[0], total_in, total_taps, total_out, small[1],
        total_gate, total_up, total_down,
    )


def from_behind(value, axis, steps):
    count = lax.axis_size(axis)
    initial, last = (max(0, -steps), min(count, count - steps))
    return lax.ppermute(value, axis, [(source, source + steps) for source in range(initial, last)])


def norm_backward_and_gain(grad_normed, plain, inverse, gain):
    grad_plain = grad_normed * gain
    grad_values = inverse * (
        grad_plain - plain * jnp.mean(grad_plain * plain, axis=-1, keepdims=True)
    )
    leading = tuple(range(grad_normed.ndim - 1))
    return (grad_values, jnp.sum(grad_normed * plain, axis=leading))


def local(
    tokens,
    norm_gain,
    w_in,
    conv_weight,
    convolution_out_weight,
    ffn_gain,
    w_gate,
    w_up,
    w_down,
    cotangent,
):
    input_rows = tokens.astype(jnp.float32)
    gain_one = norm_gain.astype(jnp.float32)
    gain_two = ffn_gain.astype(jnp.float32)
    taps = conv_weight.astype(jnp.float32)
    seqs, width, model = tokens.shape
    (
        complete_input_weight,
        complete_output_weight,
        feedforward_gate_weight,
        feedforward_up_weight,
        feedforward_down_weight,
    ) = (
        lax.all_gather(w_in, "shard", axis=1, tiled=True),
        lax.all_gather(convolution_out_weight, "shard", axis=1, tiled=True),
        lax.all_gather(w_gate, "shard", axis=0, tiled=True),
        lax.all_gather(w_up, "shard", axis=0, tiled=True),
        lax.all_gather(w_down, "shard", axis=1, tiled=True),
    )
    plain_one, inverse_one = norm_forward(input_rows)
    first_normalized = (plain_one * gain_one).astype(jnp.bfloat16)
    projection = jnp.einsum(
        "uiq,tqz->tuiz", first_normalized, complete_input_weight, preferred_element_type=jnp.float32
    )
    in_gate = projection[0]
    out_gate = projection[1]
    conv_input = projection[2]
    product = (in_gate * conv_input).astype(jnp.bfloat16)
    edge = from_behind(product[:, width - 2 :, :], "context", 1)
    extended = jnp.concatenate([edge, product], axis=1).astype(jnp.float32)
    recent = extended[:, 2:, :]
    previous = extended[:, 1 : width + 1, :]
    earlier = extended[:, :width, :]
    convolved = taps[0] * recent + taps[1] * previous + taps[2] * earlier
    gated_product = (out_gate * convolved).astype(jnp.bfloat16)
    partial_mixer_output = jnp.einsum(
        "zaw,wk->zak", gated_product, complete_output_weight, preferred_element_type=jnp.float32
    )
    residual_middle = input_rows + lax.psum(partial_mixer_output, "tensor")
    plain_two, inverse_two = norm_forward(residual_middle)
    second_normalized = (plain_two * gain_two).astype(jnp.bfloat16)
    gate_branch = jnp.einsum(
        "mut,tz->muz",
        second_normalized,
        feedforward_gate_weight,
        preferred_element_type=jnp.float32,
    )
    up_projection_branch = jnp.einsum(
        "mut,tz->muz", second_normalized, feedforward_up_weight, preferred_element_type=jnp.float32
    )
    sigmoid_gate = jax.nn.sigmoid(gate_branch)
    silu_gate = gate_branch * sigmoid_gate
    hidden_state = (silu_gate * up_projection_branch).astype(jnp.bfloat16)
    partial_feedforward = jnp.einsum(
        "eny,yv->env", hidden_state, feedforward_down_weight, preferred_element_type=jnp.float32
    )
    block_out = (
        residual_middle
        + lax.psum(partial_feedforward.astype(jnp.bfloat16), "tensor").astype(jnp.float32)
    ).astype(jnp.bfloat16)
    grad_out = cotangent.astype(jnp.float32)
    hidden_gradient = jnp.einsum(
        "qmn,pn->qmp", cotangent, feedforward_down_weight, preferred_element_type=jnp.float32
    )
    down_gradient = jnp.einsum(
        "eiu,eix->ux", hidden_state, cotangent, preferred_element_type=jnp.float32
    )
    gate_gradient = (
        hidden_gradient
        * up_projection_branch
        * sigmoid_gate
        * (1.0 + gate_branch * (1.0 - sigmoid_gate))
    ).astype(jnp.bfloat16)
    up_gradient = (hidden_gradient * silu_gate).astype(jnp.bfloat16)
    grad_w_gate = jnp.einsum(
        "rnj,rnt->jt", second_normalized, gate_gradient, preferred_element_type=jnp.float32
    )
    up_weight_gradient = jnp.einsum(
        "rnj,rnt->jt", second_normalized, up_gradient, preferred_element_type=jnp.float32
    )
    partial_normed_two = jnp.einsum(
        "wxo,qo->wxq", gate_gradient, feedforward_gate_weight, preferred_element_type=jnp.float32
    )
    partial_normed_two = partial_normed_two + jnp.einsum(
        "wxo,qo->wxq", up_gradient, feedforward_up_weight, preferred_element_type=jnp.float32
    )
    grad_normed_two = lax.psum(partial_normed_two, "tensor")
    grad_rows_two, gain_grad_two = norm_backward_and_gain(grad_normed_two, plain_two, inverse_two, gain_two)
    grad_middle = grad_out + grad_rows_two
    mixer_output_gradient = grad_middle.astype(jnp.bfloat16)
    grad_gated = jnp.einsum(
        "ymo,bo->ymb",
        mixer_output_gradient,
        complete_output_weight,
        preferred_element_type=jnp.float32,
    )
    out_weight_gradient = jnp.einsum(
        "miy,miq->yq", gated_product, mixer_output_gradient, preferred_element_type=jnp.float32
    )
    grad_convolved = (grad_gated * out_gate).astype(jnp.bfloat16)
    grad_out_gate = grad_gated * convolved
    grad_edge = from_behind(grad_convolved[:, :2, :], "context", -1)
    grad_extended = jnp.concatenate([grad_convolved, grad_edge], axis=1).astype(jnp.float32)
    grad_product = (
        taps[0] * grad_extended[:, :width, :]
        + taps[1] * grad_extended[:, 1 : width + 1, :]
        + taps[2] * grad_extended[:, 2:, :]
    )
    grad_local = grad_extended[:, :width, :]
    tap_grads = jnp.stack(
        [
            jnp.sum(grad_local * recent, axis=(0, 1)),
            jnp.sum(grad_local * previous, axis=(0, 1)),
            jnp.sum(grad_local * earlier, axis=(0, 1)),
        ]
    )
    projection_gradient = jnp.stack(
        [
            (grad_product * conv_input).astype(jnp.bfloat16),
            grad_out_gate.astype(jnp.bfloat16),
            (grad_product * in_gate).astype(jnp.bfloat16),
        ]
    )
    grad_w_in = jnp.einsum(
        "pxw,gpxt->gwt", first_normalized, projection_gradient, preferred_element_type=jnp.float32
    )
    partial_normed_one = jnp.einsum(
        "ireo,ivo->rev",
        projection_gradient,
        complete_input_weight,
        preferred_element_type=jnp.float32,
    )
    shard_in, shard_out, shard_gate, shard_up, shard_down = (
        lax.psum_scatter(
            grad_w_in.astype(jnp.bfloat16), "shard", scatter_dimension=1, tiled=True
        ).astype(jnp.float32),
        lax.psum_scatter(
            out_weight_gradient.astype(jnp.bfloat16), "shard", scatter_dimension=1, tiled=True
        ).astype(jnp.float32),
        lax.psum_scatter(
            grad_w_gate.astype(jnp.bfloat16), "shard", scatter_dimension=0, tiled=True
        ).astype(jnp.float32),
        lax.psum_scatter(
            up_weight_gradient.astype(jnp.bfloat16), "shard", scatter_dimension=0, tiled=True
        ).astype(jnp.float32),
        lax.psum_scatter(
            down_gradient.astype(jnp.bfloat16), "shard", scatter_dimension=1, tiled=True
        ).astype(jnp.float32),
    )
    total_in, total_out, total_gate, total_up, total_down = (
        lax.psum(shard_in.astype(jnp.bfloat16), "context").astype(jnp.float32),
        lax.psum(shard_out.astype(jnp.bfloat16), "context").astype(jnp.float32),
        lax.psum(shard_gate.astype(jnp.bfloat16), "context").astype(jnp.float32),
        lax.psum(shard_up.astype(jnp.bfloat16), "context").astype(jnp.float32),
        lax.psum(shard_down.astype(jnp.bfloat16), "context").astype(jnp.float32),
    )
    grad_normed_one = lax.psum(partial_normed_one.astype(jnp.bfloat16), "tensor").astype(
        jnp.float32
    )
    grad_rows_one, gain_grad_one = norm_backward_and_gain(grad_normed_one, plain_one, inverse_one, gain_one)
    grad_tokens = grad_middle + grad_rows_one
    total_gain_one, total_taps, total_gain_two = lax.psum(
        (gain_grad_one, tap_grads, gain_grad_two), ("shard", "context")
    )
    return (
        block_out,
        grad_tokens,
        total_gain_one,
        total_in,
        total_taps,
        total_out,
        total_gain_two,
        total_gate,
        total_up,
        total_down,
    )


def solution(mesh):
    in_specs = (
        P("shard", "context", None),
        P(),
        P(None, "shard", "tensor"),
        P(None, "tensor"),
        P("tensor", "shard"),
        P(),
        P("shard", "tensor"),
        P("shard", "tensor"),
        P("tensor", "shard"),
        P("shard", "context", None),
    )
    out_specs = (
        P("shard", "context", None),
        P("shard", "context", None),
        P(),
        P(None, "shard", "tensor"),
        P(None, "tensor"),
        P("tensor", "shard"),
        P(),
        P("shard", "tensor"),
        P("shard", "tensor"),
        P("tensor", "shard"),
    )
    sizes = mesh.shape
    by_links = (sizes["shard"], sizes["context"], sizes["tensor"]) == (4, 2, 4)
    body = local_by_links if by_links else local
    return jax.shard_map(body, mesh=mesh, in_specs=in_specs, out_specs=out_specs, check_vma=False)
```

```python
import functools

import jax
import jax.numpy as jnp
from jax import lax
from jax.experimental import pallas as pl
from jax.experimental.pallas import tpu as pltpu
from jax.sharding import PartitionSpec as P

EPSILON = 1e-05
F32 = jnp.float32
BF16 = jnp.bfloat16
MIB = 1024 * 1024
LEAD = 16


def norm_forward(values):
    inverse = lax.rsqrt(jnp.mean(values * values, axis=-1, keepdims=True) + EPSILON)
    return (values * inverse, inverse)


def norm_backward(grad_normed, plain, inverse, gain):
    grad_plain = grad_normed * gain
    return inverse * (
        grad_plain - plain * jnp.mean(grad_plain * plain, axis=-1, keepdims=True)
    )


def dot_nn(a, b):
    return lax.dot_general(a, b, (((1,), (0,)), ((), ())), preferred_element_type=F32)


def dot_nt(a, b):
    return lax.dot_general(a, b, (((1,), (1,)), ((), ())), preferred_element_type=F32)


def dot_tn(a, b):
    return lax.dot_general(a, b, (((0,), (0,)), ((), ())), preferred_element_type=F32)


def rounded(value):
    return lax.optimization_barrier(value.astype(BF16))


def shifted(value, steps):
    count = lax.axis_size("tensor")
    return lax.ppermute(value, "tensor", [(i, (i + steps) % count) for i in range(count)])


def swapped(value, axis, bit):
    count = lax.axis_size(axis)
    return lax.ppermute(value, axis, [(i, i ^ bit) for i in range(count)])


def to_core(value):
    return swapped(value, "shard", 1)


def to_y(value):
    return swapped(value, "shard", 2)


def to_x(value):
    return swapped(value, "context", 1)


def inward(value):
    return lax.ppermute(value, "tensor", [(0, 1), (3, 2)])


def across(value):
    return lax.ppermute(value, "tensor", [(1, 2), (2, 1)])


def outward(value):
    return lax.ppermute(value, "tensor", [(1, 0), (2, 3)])


def together(*values):
    return lax.optimization_barrier(values)


def added(*values):
    return sum(value.astype(F32) for value in values).astype(BF16)


def mixer_forward_kernel(ids, rows, mine, other, *rest):
    gated, weights = rest[-2:]
    part = mine.shape[1]
    half = 2 * part + LEAD

    @pl.when(pl.program_id(0) == 0)
    def _():
        for bit, piece in enumerate((mine, other)):
            for far in range(2):
                start = pl.multiple_of((ids[0] ^ (bit + 2 * far)) * part, part)
                for side in range(2):
                    first = 2 * (ids[2] ^ side)
                    base = (2 * far + side) * half
                    for which in range(2):
                        weights[0, first + which, pl.ds(start, part), :] = piece[
                            base + which * part : base + (which + 1) * part, :
                        ]

    taps = mine[2 * part : half, :].astype(F32)
    values = rows[0]
    product = dot_nn(values, weights[0, 0]) * dot_nn(values, weights[0, 2])
    product = product.astype(BF16).astype(F32)
    convolved = (
        taps[0:1] * product
        + taps[1:2] * pltpu.roll(product, 1, 0)
        + taps[2:3] * pltpu.roll(product, 2, 0)
    )[LEAD:]
    gated[0] = (dot_nn(values[LEAD:], weights[0, 1]) * convolved).astype(BF16)


def mixer_forward(ids, rows, pieces, block, earlier):
    seqs, long, model = rows.shape
    width = long - LEAD
    part = pieces[0].shape[1]
    count = model // part
    specs = [pl.BlockSpec((1, long, model), lambda q, ids: (q, 0, 0))]
    specs += [pl.BlockSpec(piece.shape, lambda q, ids: (0, 0)) for piece in pieces]
    specs += [pl.BlockSpec(memory_space=pl.ANY)] * len(earlier)
    return pl.pallas_call(
        mixer_forward_kernel,
        grid_spec=pltpu.PrefetchScalarGridSpec(
            num_scalar_prefetch=1,
            grid=(seqs,),
            in_specs=specs,
            out_specs=[
                pl.BlockSpec((1, width, part), lambda q, ids: (q, 0, block)),
                pl.BlockSpec((1, 4, model, part), lambda q, ids: (block, 0, 0, 0)),
            ],
        ),
        out_shape=[
            jax.ShapeDtypeStruct((seqs, width, model), BF16),
            jax.ShapeDtypeStruct((count, 4, model, part), BF16),
        ],
        input_output_aliases={4: 0, 5: 1} if earlier else {},
        compiler_params=pltpu.CompilerParams(vmem_limit_bytes=24 * MIB),
        cost_estimate=pl.CostEstimate(flops=0, bytes_accessed=0, transcendentals=0),
        name="mixer_forward",
    )(ids, rows, *pieces, *earlier)


def middle_kernel(ids, gated, weights, tokens, gain, normed, own):
    count, _, _, part = weights.shape
    values = tokens[0].astype(F32)
    for block in range(count):
        values += dot_nt(gated[0, :, block * part : (block + 1) * part], weights[block, 0])
    plain, _ = norm_forward(values)
    normed[0] = (plain * gain[...].astype(F32)).astype(BF16)

    @pl.when(pl.program_id(0) == ids[1])
    def _():
        own[...] = values


def middle(ids, gated, weights, tokens, gain):
    seqs, width, model = tokens.shape
    count, _, _, part = weights.shape
    row = pl.BlockSpec((1, width, model), lambda q, ids: (q, 0, 0))
    return pl.pallas_call(
        middle_kernel,
        grid_spec=pltpu.PrefetchScalarGridSpec(
            num_scalar_prefetch=1,
            grid=(seqs,),
            in_specs=[
                row,
                pl.BlockSpec((count, 1, model, part), lambda q, ids: (0, 3, 0, 0)),
                row,
                pl.BlockSpec((1, model), lambda q, ids: (0, 0)),
            ],
            out_specs=[row, pl.BlockSpec((width, model), lambda q, ids: (0, 0))],
        ),
        out_shape=[
            jax.ShapeDtypeStruct(tokens.shape, BF16),
            jax.ShapeDtypeStruct((width, model), F32),
        ],
        compiler_params=pltpu.CompilerParams(vmem_limit_bytes=32 * MIB),
        cost_estimate=pl.CostEstimate(flops=0, bytes_accessed=0, transcendentals=0),
        name="middle",
    )(ids, gated, weights, tokens, gain)


def feedforward_kernel(ids, normed, cotangent, piece0, piece1, piece2, piece3, *rest):
    down, grad_normed, hidden, grad_gate, grad_up, weights, arrived = rest[-7:]
    part = piece0.shape[0] // 3
    first = jnp.logical_and(pl.program_id(0) == 0, pl.program_id(1) == 0)

    def copies(which):
        for place, piece in enumerate((piece0, piece1, piece2, piece3)):
            start = pl.multiple_of((ids[0] ^ place) * part, part)
            yield pltpu.make_async_copy(
                piece.at[pl.ds(which * part, part), :],
                weights.at[which, pl.ds(start, part), :],
                arrived.at[which, place],
            )

    @pl.when(first)
    def _():
        for which in range(3):
            for copy in copies(which):
                copy.start()
        for copy in copies(0):
            copy.wait()

    values = normed[0]
    gate = dot_nn(values, weights[0])

    @pl.when(first)
    def _():
        for which in (1, 2):
            for copy in copies(which):
                copy.wait()

    up = dot_nn(values, weights[1])
    grad_hidden = dot_nn(cotangent[0], weights[2])
    sigmoid = jax.nn.sigmoid(gate)
    silu = gate * sigmoid
    hidden_now = (silu * up).astype(BF16)
    hidden[0] = hidden_now
    gate_now = (grad_hidden * up * sigmoid * (1.0 + gate * (1.0 - sigmoid))).astype(BF16)
    up_now = (grad_hidden * silu).astype(BF16)
    grad_gate[0] = gate_now
    grad_up[0] = up_now
    grad_normed[0] = (dot_nt(gate_now, weights[0]) + dot_nt(up_now, weights[1])).astype(BF16)
    down[0] = dot_nt(hidden_now, weights[2]).astype(BF16)


def feedforward(ids, normed, cotangent, pieces, first, blocks, earlier):
    seqs, width, model = normed.shape
    units = pieces[0].shape[1]
    size = width // 2

    def seq(b, i, ids):
        return (ids[3 + first + b], i, 0)

    def own(b, i, ids):
        return (b, i, 0)

    wide = jax.ShapeDtypeStruct((seqs, width, units), BF16)
    return pl.pallas_call(
        feedforward_kernel,
        grid_spec=pltpu.PrefetchScalarGridSpec(
            num_scalar_prefetch=1,
            grid=(blocks, 2),
            in_specs=[
                pl.BlockSpec((1, size, model), seq),
                pl.BlockSpec((1, size, model), seq),
            ]
            + [pl.BlockSpec(memory_space=pl.ANY)] * (4 + len(earlier)),
            out_specs=[
                pl.BlockSpec((1, size, model), own),
                pl.BlockSpec((1, size, model), own),
                pl.BlockSpec((1, size, units), seq),
                pl.BlockSpec((1, size, units), seq),
                pl.BlockSpec((1, size, units), seq),
            ],
            scratch_shapes=[
                pltpu.VMEM((3, model, units), BF16),
                pltpu.SemaphoreType.DMA((3, 4)),
            ],
        ),
        out_shape=[
            jax.ShapeDtypeStruct((blocks, width, model), BF16),
            jax.ShapeDtypeStruct((blocks, width, model), BF16),
            wide,
            wide,
            wide,
        ],
        input_output_aliases={7: 2, 8: 3, 9: 4} if earlier else {},
        compiler_params=pltpu.CompilerParams(vmem_limit_bytes=36 * MIB),
        cost_estimate=pl.CostEstimate(flops=0, bytes_accessed=0, transcendentals=0),
        name="feedforward",
    )(ids, normed, cotangent, *pieces, *earlier)


def mixer_backward_kernel(
    ids, part0, part1, part2, part3, own, cotangent, gain, rows, weights, taps,
    grad_middle, grad_mixed, gain_grad, grad_convolved, grad_out_gate, in_gate, conv_input, tap_grads,
):
    @pl.when(pl.program_id(0) == 0)
    def _():
        incoming = sum(part[...].astype(F32) for part in (part0, part1, part2, part3))
        plain, inverse = norm_forward(own[...])
        gain_grad[...] = jnp.sum(incoming * plain, axis=0, keepdims=True)
        total = cotangent[0].astype(F32) + norm_backward(
            incoming, plain, inverse, gain[...].astype(F32)
        )
        grad_middle[...] = total
        grad_mixed[...] = total.astype(BF16)

    tap = taps[0].astype(F32)
    values = rows[0]
    first = dot_nn(values, weights[0, 0])
    third = dot_nn(values, weights[0, 2])
    out_gate = dot_nn(values[LEAD:], weights[0, 1])
    product = (first * third).astype(BF16).astype(F32)
    recent, previous, earlier = (
        product[LEAD:], pltpu.roll(product, 1, 0)[LEAD:], pltpu.roll(product, 2, 0)[LEAD:],
    )
    convolved = tap[0:1] * recent + tap[1:2] * previous + tap[2:3] * earlier
    in_gate[...] = first[LEAD:]
    conv_input[...] = third[LEAD:]
    grad_gated = dot_nn(grad_mixed[...], weights[0, 3])
    grad_out_gate[...] = (grad_gated * convolved).astype(BF16)
    low = (grad_gated * out_gate).astype(BF16)
    grad_convolved[...] = low
    low = low.astype(F32)
    tap_grads[0] = jnp.concatenate(
        [
            jnp.sum(low * recent, axis=0, keepdims=True),
            jnp.sum(low * previous, axis=0, keepdims=True),
            jnp.sum(low * earlier, axis=0, keepdims=True),
            jnp.zeros((5, low.shape[1]), F32),
        ]
    )


def mixer_backward(ids, parts, own, cotangent, gain, rows, weights, taps):
    width, model = own.shape
    long = rows.shape[1]
    count, _, _, part = weights.shape
    whole = pl.BlockSpec((width, model), lambda j, ids: (0, 0))
    line = pl.BlockSpec((1, model), lambda j, ids: (0, 0))
    column = pl.BlockSpec((width, part), lambda j, ids: (0, j))
    return pl.pallas_call(
        mixer_backward_kernel,
        grid_spec=pltpu.PrefetchScalarGridSpec(
            num_scalar_prefetch=1,
            grid=(count,),
            in_specs=[
                whole, whole, whole, whole, whole,
                pl.BlockSpec((1, width, model), lambda j, ids: (ids[1], 0, 0)),
                line,
                pl.BlockSpec((1, long, model), lambda j, ids: (ids[1], 0, 0)),
                pl.BlockSpec((1, 4, model, part), lambda j, ids: (j, 0, 0, 0)),
                pl.BlockSpec((1, LEAD, part), lambda j, ids: (j, 0, 0)),
            ],
            out_specs=[
                whole, whole, line, column, column, column, column,
                pl.BlockSpec((1, 8, part), lambda j, ids: (j, 0, 0)),
            ],
        ),
        out_shape=[
            jax.ShapeDtypeStruct((width, model), F32),
            jax.ShapeDtypeStruct((width, model), BF16),
            jax.ShapeDtypeStruct((1, model), F32),
            jax.ShapeDtypeStruct((width, model), BF16),
            jax.ShapeDtypeStruct((width, model), BF16),
            jax.ShapeDtypeStruct((width, model), F32),
            jax.ShapeDtypeStruct((width, model), F32),
            jax.ShapeDtypeStruct((count, 8, part), F32),
        ],
        compiler_params=pltpu.CompilerParams(vmem_limit_bytes=44 * MIB),
        cost_estimate=pl.CostEstimate(flops=0, bytes_accessed=0, transcendentals=0),
        name="mixer_backward",
    )(ids, *parts, own, cotangent, gain, rows, weights, taps)


def input_backward_kernel(
    ids, grad_convolved, edge, in_gate, conv_input, grad_out_gate, taps, weights, grad_middle, tokens, gain,
    grad_first, grad_third, grad_tokens, gain_grad, total,
):
    block = pl.program_id(0)
    width = grad_convolved.shape[0]
    tap = taps[0].astype(F32)
    longer = jnp.concatenate([grad_convolved[...], edge[...]]).astype(F32)
    count = longer.shape[0]
    grad_product = (
        tap[0:1] * longer
        + tap[1:2] * pltpu.roll(longer, count - 1, 0)
        + tap[2:3] * pltpu.roll(longer, count - 2, 0)
    )[:width]
    first = (grad_product * conv_input[...]).astype(BF16)
    third = (grad_product * in_gate[...]).astype(BF16)
    grad_first[...] = first
    grad_third[...] = third
    here = (
        dot_nt(first, weights[0, 0])
        + dot_nt(grad_out_gate[...], weights[0, 1])
        + dot_nt(third, weights[0, 2])
    )

    @pl.when(block == 0)
    def _():
        total[...] = here

    @pl.when(block > 0)
    def _():
        total[...] += here

    @pl.when(block == pl.num_programs(0) - 1)
    def _():
        incoming = total[...]
        plain, inverse = norm_forward(tokens[0].astype(F32))
        gain_grad[...] = jnp.sum(incoming * plain, axis=0, keepdims=True)
        grad_tokens[...] = (
            grad_middle[...] + norm_backward(incoming, plain, inverse, gain[...].astype(F32))
        ).astype(BF16)


def input_backward(
    ids, grad_convolved, edge, in_gate, conv_input, grad_out_gate, taps, weights, grad_middle, tokens, gain
):
    width, model = grad_middle.shape
    count, _, _, part = weights.shape
    whole = pl.BlockSpec((width, model), lambda j, ids: (0, 0))
    line = pl.BlockSpec((1, model), lambda j, ids: (0, 0))
    column = pl.BlockSpec((width, part), lambda j, ids: (0, j))
    return pl.pallas_call(
        input_backward_kernel,
        grid_spec=pltpu.PrefetchScalarGridSpec(
            num_scalar_prefetch=1,
            grid=(count,),
            in_specs=[
                column,
                pl.BlockSpec((edge.shape[0], part), lambda j, ids: (0, j)),
                column, column, column,
                pl.BlockSpec((1, LEAD, part), lambda j, ids: (j, 0, 0)),
                pl.BlockSpec((1, 4, model, part), lambda j, ids: (j, 0, 0, 0)),
                whole,
                pl.BlockSpec((1, width, model), lambda j, ids: (ids[1], 0, 0)),
                line,
            ],
            out_specs=[column, column, whole, line],
            scratch_shapes=[pltpu.VMEM((width, model), F32)],
        ),
        out_shape=[
            jax.ShapeDtypeStruct((width, model), BF16),
            jax.ShapeDtypeStruct((width, model), BF16),
            jax.ShapeDtypeStruct((width, model), BF16),
            jax.ShapeDtypeStruct((1, model), F32),
        ],
        compiler_params=pltpu.CompilerParams(vmem_limit_bytes=44 * MIB),
        cost_estimate=pl.CostEstimate(flops=0, bytes_accessed=0, transcendentals=0),
        name="input_backward",
    )(ids, grad_convolved, edge, in_gate, conv_input, grad_out_gate, taps, weights, grad_middle, tokens, gain)


def split_rows(ids, g):
    return ids[7 + g]


def feedforward_gradient_kernel(ids, left, right, send, keep):
    result = dot_tn(left[...], right[...]).astype(BF16)

    @pl.when(pl.program_id(0) < 2)
    def _():
        send[0] = result

    @pl.when(pl.program_id(0) >= 2)
    def _():
        keep[0] = result


def feedforward_gradient(ids, left, right):
    tokens, model = left.shape
    units = right.shape[1]
    part = model // 4
    shape = jax.ShapeDtypeStruct((2, part, units), BF16)
    return pl.pallas_call(
        feedforward_gradient_kernel,
        grid_spec=pltpu.PrefetchScalarGridSpec(
            num_scalar_prefetch=1,
            grid=(4,),
            in_specs=[
                pl.BlockSpec((tokens, part), lambda g, ids: (0, split_rows(ids, g))),
                pl.BlockSpec((tokens, units), lambda g, ids: (0, 0), pipeline_mode=pl.Buffered(1)),
            ],
            out_specs=[
                pl.BlockSpec((1, part, units), lambda g, ids: (jnp.minimum(g, 1), 0, 0)),
                pl.BlockSpec((1, part, units), lambda g, ids: (jnp.maximum(g - 2, 0), 0, 0)),
            ],
        ),
        out_shape=[shape, shape],
        compiler_params=pltpu.CompilerParams(vmem_limit_bytes=32 * MIB),
        cost_estimate=pl.CostEstimate(flops=0, bytes_accessed=0, transcendentals=0),
        name="feedforward_gradient",
    )(ids, left, right)


def mixer_gradient_kernel(ids, rows, mixed, first, second, third, gated, send, keep):
    part = mixed.shape[1]
    here = []
    for left, right in (
        (rows[0, LEAD:], first[...]),
        (rows[0, LEAD:], second[...]),
        (rows[0, LEAD:], third[...]),
        (mixed[...], gated[0]),
    ):
        here.append(dot_tn(left, right).astype(BF16))

    def store(out):
        for matrix, value in enumerate(here):
            for block in range(4):
                for upper in range(2):
                    out[0, ids[2] ^ upper, ids[11 + block], matrix] = value[
                        upper * part // 2 : (upper + 1) * part // 2, block * part : (block + 1) * part
                    ]

    @pl.when(pl.program_id(0) < 2)
    def _():
        store(send)

    @pl.when(pl.program_id(0) >= 2)
    def _():
        store(keep)


def mixer_gradient(ids, rows, mixed, first, second, third, gated):
    width, model = mixed.shape
    long = rows.shape[1]
    part = model // 4
    shape = jax.ShapeDtypeStruct((2, 2, 4, 4, part // 2, part), BF16)
    block = (1, 2, 4, 4, part // 2, part)
    whole = pl.BlockSpec((width, model), lambda g, ids: (0, 0))
    return pl.pallas_call(
        mixer_gradient_kernel,
        grid_spec=pltpu.PrefetchScalarGridSpec(
            num_scalar_prefetch=1,
            grid=(4,),
            in_specs=[
                pl.BlockSpec((1, long, part), lambda g, ids: (ids[1], 0, split_rows(ids, g))),
                pl.BlockSpec((width, part), lambda g, ids: (0, split_rows(ids, g))),
                whole, whole, whole,
                pl.BlockSpec((1, width, model), lambda g, ids: (ids[1], 0, 0)),
            ],
            out_specs=[
                pl.BlockSpec(block, lambda g, ids: (jnp.minimum(g, 1), 0, 0, 0, 0, 0)),
                pl.BlockSpec(block, lambda g, ids: (jnp.maximum(g - 2, 0), 0, 0, 0, 0, 0)),
            ],
        ),
        out_shape=[shape, shape],
        compiler_params=pltpu.CompilerParams(vmem_limit_bytes=40 * MIB),
        cost_estimate=pl.CostEstimate(flops=0, bytes_accessed=0, transcendentals=0),
        name="mixer_gradient",
    )(ids, rows, mixed, first, second, third, gated)


def local_by_links(
    tokens, norm_gain, w_in, conv_weight, convolution_out_weight, ffn_gain, w_gate, w_up, w_down, cotangent
):
    seqs, width, model = tokens.shape
    part = w_in.shape[1]
    units = w_gate.shape[1]
    shard, side, level = (lax.axis_index(name) for name in ("shard", "context", "tensor"))
    end = jnp.logical_or(level == 0, level == 3)
    order = [
        jnp.where(level < 2, 3, 0), jnp.where(level < 2, 2, 1), level ^ 1, level,
    ]
    place = [sum(jnp.where((level + block) % 4 == order[k], k, 0) for k in range(4)) for block in range(4)]
    ids = jnp.stack(
        [shard, level, side] + order + [shard ^ 1, shard ^ 3, shard, shard ^ 2] + place
    ).astype(jnp.int32)
    gain_one = norm_gain.reshape(1, model)
    gain_two = ffn_gain.reshape(1, model)
    def from_others(in_one, in_two, in_three):
        (inside, over, out_one), (over_end, out_two), out_three = in_one, in_two, in_three
        return (
            jnp.where(end, out_one, inside),
            jnp.where(end, out_two, over_end),
            jnp.where(end, out_three, over),
        )

    def placed(own, others, dtype):
        out = jnp.zeros((seqs, width, model), dtype)
        for bits, block in enumerate((own,) + others):
            out = lax.dynamic_update_slice(out, block.astype(dtype)[None], (level ^ bits, 0, 0))
        return out

    taps_near = jnp.concatenate([conv_weight, jnp.zeros((LEAD - 3, part), BF16)])
    near = jnp.concatenate(
        [w_in[0], w_in[1], taps_near, w_in[2], convolution_out_weight.T, taps_near]
    )
    half = near.shape[0] // 2

    def sides(value):
        return [lax.dynamic_slice_in_dim(value, (side ^ bit) * half, half, 0) for bit in range(2)]

    near, near_side, near_else = together(near, *sides(near))
    far = to_y(near)
    near_right, near_left = shifted(near_side, -1), shifted(near_side, 1)
    edge = lax.ppermute(tokens[:, width - 2 :, :], "context", [(0, 1)])
    feed = jnp.concatenate([w_gate, w_up, w_down.T])
    far, near_right, near_left, edge, feed, near_side, near_else = together(
        far, near_right, near_left, edge, feed, near_side, near_else
    )

    far_side, far_else = together(*sides(far))
    far_right, far_left = shifted(far_side, -1), shifted(far_side, 1)
    near_over = to_x(jnp.concatenate([near_right, near_left]))
    feed_far = to_y(feed)
    mine = together(jnp.concatenate([near_side, near_else, far_side, far_else]))[0]
    other = to_core(mine)
    rows = jnp.concatenate([jnp.zeros((seqs, LEAD - 2, model), BF16), edge, tokens], axis=1).astype(F32)
    rows = (norm_forward(rows)[0] * gain_one.astype(F32)).astype(BF16)
    state = mixer_forward(ids, rows, (mine, other), 0, ())
    far_right, far_left, near_over, near_right, near_left, rows, feed, cotangent, *state = together(
        far_right, far_left, near_over, near_right, near_left, rows, feed, cotangent, *state
    )

    near_far, far_far = shifted(near_right, -1), shifted(far_left, 1)
    far_over = to_x(jnp.concatenate([far_right, far_left]))
    feed_core = to_core(feed)
    near_far, far_far, far_over, feed_core, *state = together(
        near_far, far_far, far_over, feed_core, *state
    )

    last_over = to_x(jnp.concatenate([near_far, far_far]))
    for block, rows_of, (a, b) in (
        (1, slice(None, half), (near_right, far_right)),
        (3, slice(half, None), (near_left, far_left)),
    ):
        mine = together(jnp.concatenate([a, near_over[rows_of], b, far_over[rows_of]]))[0]
        state = mixer_forward(ids, rows, (mine, to_core(mine)), block, state)
    last_over, feed_far, *state = together(last_over, feed_far, *state)

    mine = together(jnp.concatenate([near_far, last_over[:half], far_far, last_over[half:]]))[0]
    state = mixer_forward(ids, rows, (mine, to_core(mine)), 2, state)
    gated, weights = state
    feed_far_core = to_core(feed_far)
    pieces = (feed, feed_core, feed_far, feed_far_core)
    taps = jnp.stack([near_side[2 * part :], near_right[2 * part :], near_far[2 * part :], near_left[2 * part :]])
    normed, middle_own = middle(ids, gated, weights, tokens, gain_two)
    normed_flat = normed.reshape(seqs * width, model)

    down0, grad0, *wide = feedforward(ids, normed, cotangent, pieces, 0, 1, ())
    down0, grad0, *wide = together(down0[0], grad0[0], *wide)

    grad_in0 = inward(grad0)
    down12, grad12, *wide = feedforward(ids, normed, cotangent, pieces, 1, 2, tuple(wide))
    grad1, grad2, down1, down2 = grad12[0], grad12[1], down12[0], down12[1]
    grad_in0, grad1, grad2, down1, down2, normed_flat, *wide = together(
        grad_in0, grad1, grad2, down1, down2, normed_flat, *wide
    )

    grad_in1 = inward(grad1)
    grad_over0 = across(added(grad0, grad_in0))
    down3, grad3, *wide = feedforward(ids, normed, cotangent, pieces, 3, 1, tuple(wide))
    hidden, grad_gate, grad_up = (v.reshape(seqs * width, units) for v in wide)
    send_down, keep_down = feedforward_gradient(ids, cotangent.reshape(seqs * width, model), hidden)
    grad_in1, grad_over0, grad_gate, grad_up, send_down, keep_down, grad2 = together(
        grad_in1, grad_over0, grad_gate, grad_up, send_down, keep_down, grad2
    )

    grad_in2 = inward(grad2)
    grad_over1 = across(added(grad1, grad_in1))
    grad_out = outward(added(grad2, grad_over0))
    core_down = to_core(send_down)
    send_gate, keep_gate = feedforward_gradient(ids, normed_flat, grad_gate)
    send_up, keep_up = feedforward_gradient(ids, normed_flat, grad_up)
    grad_in2, grad_over1, grad_out, core_down, send_gate, keep_gate, send_up, keep_up, down0 = together(
        grad_in2, grad_over1, grad_out, core_down, send_gate, keep_gate, send_up, keep_up, down0
    )

    down_in0 = inward(down0)
    y_down = to_y(added(keep_down[1], core_down[1]))
    core_gate, core_up = to_core(send_gate), to_core(send_up)
    (
        grad_middle, grad_mixed, gain_two_grad, grad_convolved, grad_out_gate, in_gate, conv_input, tap_grads,
    ) = mixer_backward(
        ids, (grad3[0], grad_in2, grad_over1, grad_out), middle_own, cotangent, gain_two, rows, weights, taps
    )
    behind = lax.ppermute(grad_convolved[:LEAD], "context", [(1, 0)])
    grad_first, grad_third, tokens_own, gain_one_grad = input_backward(
        ids, grad_convolved, behind, in_gate, conv_input, grad_out_gate, taps, weights, grad_middle,
        tokens, gain_one,
    )
    (
        down_in0, y_down, core_gate, core_up, tokens_own, grad_first, grad_third, grad_mixed, gain_one_grad,
    ) = together(
        down_in0, y_down, core_gate, core_up, tokens_own, grad_first, grad_third, grad_mixed, gain_one_grad,
    )

    tokens_in = inward(tokens_own)
    tokens_over = across(tokens_own)
    tokens_out1 = outward(tokens_own)
    mine_down = rounded(added(keep_down[0], core_down[0], y_down))
    x_down = to_x(mine_down)
    y_both = to_y(
        jnp.concatenate([added(keep_gate[1], core_gate[1]), added(keep_up[1], core_up[1])])
    )
    send_mixer, keep_mixer = mixer_gradient(
        ids, rows, grad_mixed, grad_first, grad_out_gate, grad_third, gated
    )
    tokens_in, tokens_over, tokens_out1, x_down, y_both, send_mixer, keep_mixer, down1, down2 = together(
        tokens_in, tokens_over, tokens_out1, x_down, y_both, send_mixer, keep_mixer, down1, down2
    )

    down_in1 = inward(down1)
    tokens_over_end = across(tokens_in)
    tokens_out2 = outward(tokens_over)
    mine_both = rounded(
        added(
            jnp.concatenate([keep_gate[0], keep_up[0]]),
            jnp.concatenate([core_gate[0], core_up[0]]),
            y_both,
        )
    )
    x_both = to_x(mine_both)
    core_mixer = to_core(send_mixer)
    total_down = (mine_down.astype(F32) + x_down.astype(F32)).T
    tap_rows = tap_grads[:, :3].transpose(1, 0, 2)
    tap_rows = jnp.roll(tap_rows, level, axis=1).reshape(3, model)
    small = jnp.concatenate([gain_one_grad, gain_two_grad, tap_rows, jnp.zeros((3, model), F32)])
    down_in1, tokens_over_end, tokens_out2, x_both, core_mixer, down0, down2, small, total_down = together(
        down_in1, tokens_over_end, tokens_out2, x_both, core_mixer, down0, down2, small, total_down
    )

    down_in2 = inward(down2)
    down_over0 = across(added(down0, down_in0))
    tokens_out3 = outward(tokens_over_end)
    y_mixer1 = to_y(added(keep_mixer[1, 1], core_mixer[1, 1]))
    small = small + to_core(small)
    total_both = mine_both.astype(F32) + x_both.astype(F32)
    total_gate, total_up = total_both[:part], total_both[part:]
    down_in2, down_over0, tokens_out3, y_mixer1, small, total_gate, total_up, keep_mixer = together(
        down_in2, down_over0, tokens_out3, y_mixer1, small, total_gate, total_up, keep_mixer
    )

    down_over1 = across(added(down1, down_in1))
    down_out = outward(added(down2, down_over0))
    x_mixer = to_x(added(keep_mixer[0, 1], core_mixer[0, 1], y_mixer1))
    y_mixer0 = to_y(added(keep_mixer[1, 0], core_mixer[1, 0]))
    grad_tokens = placed(
        tokens_own,
        from_others((tokens_in, tokens_over, tokens_out1), (tokens_over_end, tokens_out2), tokens_out3),
        F32,
    )
    down_over1, down_out, x_mixer, y_mixer0, grad_tokens = together(
        down_over1, down_out, x_mixer, y_mixer0, grad_tokens
    )

    out_own = rounded(
        middle_own
        + sum(value.astype(F32) for value in (down3[0], down_in2, down_over1, down_out))
    )
    out_in = inward(out_own)
    out_over = across(out_own)
    out_out1 = outward(out_own)
    mixer = added(keep_mixer[0, 0], core_mixer[0, 0], y_mixer0, x_mixer)
    small = small + to_y(small)
    out_in, out_over, out_out1, small, mixer = together(out_in, out_over, out_out1, small, mixer)

    out_over_end = across(out_in)
    out_out2 = outward(out_over)
    mixer_in = inward(mixer[:3])
    small = small + to_x(small)
    out_over_end, out_out2, mixer_in, small = together(out_over_end, out_out2, mixer_in, small)

    out_out3 = outward(out_over_end)
    mixer_over = across(added(mixer[:2], mixer_in[:2]))
    mixer_out = outward(added(mixer[2], mixer_over[0]))
    mine = rounded(
        sum(value.astype(F32) for value in (mixer[3], mixer_in[2], mixer_over[1], mixer_out))
    )
    other = to_x(mine)
    total = jnp.concatenate(
        [jnp.where(side == 0, mine, other), jnp.where(side == 0, other, mine)], axis=1
    ).astype(F32)
    small = small + swapped(small, "tensor", 1)
    small = small + swapped(small, "tensor", 2)
    total_taps = lax.dynamic_slice(small, (2, level * part), (3, part))
    block_out = placed(
        out_own, from_others((out_in, out_over, out_out1), (out_over_end, out_out2), out_out3), BF16
    )
    return (
        block_out, grad_tokens, small[0], total[:3], total_taps, total[3].T, small[1],
        total_gate, total_up, total_down,
    )


def from_behind(value, axis, steps):
    count = lax.axis_size(axis)
    initial, last = (max(0, -steps), min(count, count - steps))
    return lax.ppermute(value, axis, [(source, source + steps) for source in range(initial, last)])


def norm_backward_and_gain(grad_normed, plain, inverse, gain):
    grad_plain = grad_normed * gain
    grad_values = inverse * (
        grad_plain - plain * jnp.mean(grad_plain * plain, axis=-1, keepdims=True)
    )
    leading = tuple(range(grad_normed.ndim - 1))
    return (grad_values, jnp.sum(grad_normed * plain, axis=leading))


def local(
    tokens,
    norm_gain,
    w_in,
    conv_weight,
    convolution_out_weight,
    ffn_gain,
    w_gate,
    w_up,
    w_down,
    cotangent,
):
    input_rows = tokens.astype(jnp.float32)
    gain_one = norm_gain.astype(jnp.float32)
    gain_two = ffn_gain.astype(jnp.float32)
    taps = conv_weight.astype(jnp.float32)
    seqs, width, model = tokens.shape
    (
        complete_input_weight,
        complete_output_weight,
        feedforward_gate_weight,
        feedforward_up_weight,
        feedforward_down_weight,
    ) = (
        lax.all_gather(w_in, "shard", axis=1, tiled=True),
        lax.all_gather(convolution_out_weight, "shard", axis=1, tiled=True),
        lax.all_gather(w_gate, "shard", axis=0, tiled=True),
        lax.all_gather(w_up, "shard", axis=0, tiled=True),
        lax.all_gather(w_down, "shard", axis=1, tiled=True),
    )
    plain_one, inverse_one = norm_forward(input_rows)
    first_normalized = (plain_one * gain_one).astype(jnp.bfloat16)
    projection = jnp.einsum(
        "uiq,tqz->tuiz", first_normalized, complete_input_weight, preferred_element_type=jnp.float32
    )
    in_gate = projection[0]
    out_gate = projection[1]
    conv_input = projection[2]
    product = (in_gate * conv_input).astype(jnp.bfloat16)
    edge = from_behind(product[:, width - 2 :, :], "context", 1)
    extended = jnp.concatenate([edge, product], axis=1).astype(jnp.float32)
    recent = extended[:, 2:, :]
    previous = extended[:, 1 : width + 1, :]
    earlier = extended[:, :width, :]
    convolved = taps[0] * recent + taps[1] * previous + taps[2] * earlier
    gated_product = (out_gate * convolved).astype(jnp.bfloat16)
    partial_mixer_output = jnp.einsum(
        "zaw,wk->zak", gated_product, complete_output_weight, preferred_element_type=jnp.float32
    )
    residual_middle = input_rows + lax.psum(partial_mixer_output, "tensor")
    plain_two, inverse_two = norm_forward(residual_middle)
    second_normalized = (plain_two * gain_two).astype(jnp.bfloat16)
    gate_branch = jnp.einsum(
        "mut,tz->muz",
        second_normalized,
        feedforward_gate_weight,
        preferred_element_type=jnp.float32,
    )
    up_projection_branch = jnp.einsum(
        "mut,tz->muz", second_normalized, feedforward_up_weight, preferred_element_type=jnp.float32
    )
    sigmoid_gate = jax.nn.sigmoid(gate_branch)
    silu_gate = gate_branch * sigmoid_gate
    hidden_state = (silu_gate * up_projection_branch).astype(jnp.bfloat16)
    partial_feedforward = jnp.einsum(
        "eny,yv->env", hidden_state, feedforward_down_weight, preferred_element_type=jnp.float32
    )
    block_out = (
        residual_middle
        + lax.psum(partial_feedforward.astype(jnp.bfloat16), "tensor").astype(jnp.float32)
    ).astype(jnp.bfloat16)
    grad_out = cotangent.astype(jnp.float32)
    hidden_gradient = jnp.einsum(
        "qmn,pn->qmp", cotangent, feedforward_down_weight, preferred_element_type=jnp.float32
    )
    down_gradient = jnp.einsum(
        "eiu,eix->ux", hidden_state, cotangent, preferred_element_type=jnp.float32
    )
    gate_gradient = (
        hidden_gradient
        * up_projection_branch
        * sigmoid_gate
        * (1.0 + gate_branch * (1.0 - sigmoid_gate))
    ).astype(jnp.bfloat16)
    up_gradient = (hidden_gradient * silu_gate).astype(jnp.bfloat16)
    grad_w_gate = jnp.einsum(
        "rnj,rnt->jt", second_normalized, gate_gradient, preferred_element_type=jnp.float32
    )
    up_weight_gradient = jnp.einsum(
        "rnj,rnt->jt", second_normalized, up_gradient, preferred_element_type=jnp.float32
    )
    partial_normed_two = jnp.einsum(
        "wxo,qo->wxq", gate_gradient, feedforward_gate_weight, preferred_element_type=jnp.float32
    )
    partial_normed_two = partial_normed_two + jnp.einsum(
        "wxo,qo->wxq", up_gradient, feedforward_up_weight, preferred_element_type=jnp.float32
    )
    grad_normed_two = lax.psum(partial_normed_two, "tensor")
    grad_rows_two, gain_grad_two = norm_backward_and_gain(grad_normed_two, plain_two, inverse_two, gain_two)
    grad_middle = grad_out + grad_rows_two
    mixer_output_gradient = grad_middle.astype(jnp.bfloat16)
    grad_gated = jnp.einsum(
        "ymo,bo->ymb",
        mixer_output_gradient,
        complete_output_weight,
        preferred_element_type=jnp.float32,
    )
    out_weight_gradient = jnp.einsum(
        "miy,miq->yq", gated_product, mixer_output_gradient, preferred_element_type=jnp.float32
    )
    grad_convolved = (grad_gated * out_gate).astype(jnp.bfloat16)
    grad_out_gate = grad_gated * convolved
    grad_edge = from_behind(grad_convolved[:, :2, :], "context", -1)
    grad_extended = jnp.concatenate([grad_convolved, grad_edge], axis=1).astype(jnp.float32)
    grad_product = (
        taps[0] * grad_extended[:, :width, :]
        + taps[1] * grad_extended[:, 1 : width + 1, :]
        + taps[2] * grad_extended[:, 2:, :]
    )
    grad_local = grad_extended[:, :width, :]
    tap_grads = jnp.stack(
        [
            jnp.sum(grad_local * recent, axis=(0, 1)),
            jnp.sum(grad_local * previous, axis=(0, 1)),
            jnp.sum(grad_local * earlier, axis=(0, 1)),
        ]
    )
    projection_gradient = jnp.stack(
        [
            (grad_product * conv_input).astype(jnp.bfloat16),
            grad_out_gate.astype(jnp.bfloat16),
            (grad_product * in_gate).astype(jnp.bfloat16),
        ]
    )
    grad_w_in = jnp.einsum(
        "pxw,gpxt->gwt", first_normalized, projection_gradient, preferred_element_type=jnp.float32
    )
    partial_normed_one = jnp.einsum(
        "ireo,ivo->rev",
        projection_gradient,
        complete_input_weight,
        preferred_element_type=jnp.float32,
    )
    shard_in, shard_out, shard_gate, shard_up, shard_down = (
        lax.psum_scatter(
            grad_w_in.astype(jnp.bfloat16), "shard", scatter_dimension=1, tiled=True
        ).astype(jnp.float32),
        lax.psum_scatter(
            out_weight_gradient.astype(jnp.bfloat16), "shard", scatter_dimension=1, tiled=True
        ).astype(jnp.float32),
        lax.psum_scatter(
            grad_w_gate.astype(jnp.bfloat16), "shard", scatter_dimension=0, tiled=True
        ).astype(jnp.float32),
        lax.psum_scatter(
            up_weight_gradient.astype(jnp.bfloat16), "shard", scatter_dimension=0, tiled=True
        ).astype(jnp.float32),
        lax.psum_scatter(
            down_gradient.astype(jnp.bfloat16), "shard", scatter_dimension=1, tiled=True
        ).astype(jnp.float32),
    )
    total_in, total_out, total_gate, total_up, total_down = (
        lax.psum(shard_in.astype(jnp.bfloat16), "context").astype(jnp.float32),
        lax.psum(shard_out.astype(jnp.bfloat16), "context").astype(jnp.float32),
        lax.psum(shard_gate.astype(jnp.bfloat16), "context").astype(jnp.float32),
        lax.psum(shard_up.astype(jnp.bfloat16), "context").astype(jnp.float32),
        lax.psum(shard_down.astype(jnp.bfloat16), "context").astype(jnp.float32),
    )
    grad_normed_one = lax.psum(partial_normed_one.astype(jnp.bfloat16), "tensor").astype(
        jnp.float32
    )
    grad_rows_one, gain_grad_one = norm_backward_and_gain(grad_normed_one, plain_one, inverse_one, gain_one)
    grad_tokens = grad_middle + grad_rows_one
    total_gain_one, total_taps, total_gain_two = lax.psum(
        (gain_grad_one, tap_grads, gain_grad_two), ("shard", "context")
    )
    return (
        block_out,
        grad_tokens,
        total_gain_one,
        total_in,
        total_taps,
        total_out,
        total_gain_two,
        total_gate,
        total_up,
        total_down,
    )


def solution(mesh):
    in_specs = (
        P("shard", "context", None),
        P(),
        P(None, "shard", "tensor"),
        P(None, "tensor"),
        P("tensor", "shard"),
        P(),
        P("shard", "tensor"),
        P("shard", "tensor"),
        P("tensor", "shard"),
        P("shard", "context", None),
    )
    out_specs = (
        P("shard", "context", None),
        P("shard", "context", None),
        P(),
        P(None, "shard", "tensor"),
        P(None, "tensor"),
        P("tensor", "shard"),
        P(),
        P("shard", "tensor"),
        P("shard", "tensor"),
        P("tensor", "shard"),
    )
    sizes = mesh.shape
    by_links = (sizes["shard"], sizes["context"], sizes["tensor"]) == (4, 2, 4)
    body = local_by_links if by_links else local
    return jax.shard_map(body, mesh=mesh, in_specs=in_specs, out_specs=out_specs, check_vma=False)
```

```python
import functools

import jax
import jax.numpy as jnp
from jax import lax
from jax.experimental import pallas as pl
from jax.experimental.pallas import tpu as pltpu
from jax.sharding import PartitionSpec as P

EPSILON = 1e-05
F32 = jnp.float32
BF16 = jnp.bfloat16
MIB = 1024 * 1024
LEAD = 16


def norm_forward(values):
    inverse = lax.rsqrt(jnp.mean(values * values, axis=-1, keepdims=True) + EPSILON)
    return (values * inverse, inverse)


def norm_backward(grad_normed, plain, inverse, gain):
    grad_plain = grad_normed * gain
    return inverse * (
        grad_plain - plain * jnp.mean(grad_plain * plain, axis=-1, keepdims=True)
    )


def dot_nn(a, b):
    return lax.dot_general(a, b, (((1,), (0,)), ((), ())), preferred_element_type=F32)


def dot_nt(a, b):
    return lax.dot_general(a, b, (((1,), (1,)), ((), ())), preferred_element_type=F32)


def dot_tn(a, b):
    return lax.dot_general(a, b, (((0,), (0,)), ((), ())), preferred_element_type=F32)


def rounded(value):
    return lax.optimization_barrier(value.astype(BF16))


def shifted(value, steps):
    count = lax.axis_size("tensor")
    return lax.ppermute(value, "tensor", [(i, (i + steps) % count) for i in range(count)])


def swapped(value, axis, bit):
    count = lax.axis_size(axis)
    return lax.ppermute(value, axis, [(i, i ^ bit) for i in range(count)])


def to_core(value):
    return swapped(value, "shard", 1)


def to_y(value):
    return swapped(value, "shard", 2)


def to_x(value):
    return swapped(value, "context", 1)


def pair(value):
    return swapped(value, "tensor", 1)


def across(value):
    return lax.ppermute(value, "tensor", [(1, 2), (2, 1)])


def together(*values):
    return lax.optimization_barrier(values)


def added(*values):
    return sum(value.astype(F32) for value in values).astype(BF16)


def mixer_forward_kernel(ids, rows, mine, other, *rest):
    gated, weights, own = rest[-3:]
    part = mine.shape[1]
    half = 2 * part + LEAD

    @pl.when(pl.program_id(0) == 0)
    def _():
        for bit, piece in enumerate((mine, other)):
            for far in range(2):
                start = pl.multiple_of((ids[0] ^ (bit + 2 * far)) * part, part)
                for side in range(2):
                    first = 2 * (ids[2] ^ side)
                    base = (2 * far + side) * half
                    for which in range(2):
                        weights[0, first + which, pl.ds(start, part), :] = piece[
                            base + which * part : base + (which + 1) * part, :
                        ]

    taps = mine[2 * part : half, :].astype(F32)
    values = rows[0]
    in_gate = dot_nn(values, weights[0, 0])
    conv_input = dot_nn(values, weights[0, 2])
    out_gate = dot_nn(values, weights[0, 1])
    product = (in_gate * conv_input).astype(BF16).astype(F32)
    convolved = (
        taps[0:1] * product
        + taps[1:2] * pltpu.roll(product, 1, 0)
        + taps[2:3] * pltpu.roll(product, 2, 0)
    )[LEAD:]
    gated[0] = (out_gate[LEAD:] * convolved).astype(BF16)

    @pl.when(pl.program_id(0) == ids[1])
    def _():
        own[0] = in_gate.astype(BF16)
        own[1] = out_gate.astype(BF16)
        own[2] = conv_input.astype(BF16)


def mixer_forward(ids, rows, pieces, block, earlier):
    seqs, long, model = rows.shape
    width = long - LEAD
    part = pieces[0].shape[1]
    count = model // part
    specs = [pl.BlockSpec((1, long, model), lambda q, ids: (q, 0, 0))]
    specs += [pl.BlockSpec(piece.shape, lambda q, ids: (0, 0)) for piece in pieces]
    specs += [pl.BlockSpec(memory_space=pl.ANY)] * len(earlier)
    return pl.pallas_call(
        mixer_forward_kernel,
        grid_spec=pltpu.PrefetchScalarGridSpec(
            num_scalar_prefetch=1,
            grid=(seqs,),
            in_specs=specs,
            out_specs=[
                pl.BlockSpec((1, width, part), lambda q, ids: (q, 0, block)),
                pl.BlockSpec((1, 4, model, part), lambda q, ids: (block, 0, 0, 0)),
                pl.BlockSpec((3, long, part), lambda q, ids: (0, 0, block)),
            ],
        ),
        out_shape=[
            jax.ShapeDtypeStruct((seqs, width, model), BF16),
            jax.ShapeDtypeStruct((count, 4, model, part), BF16),
            jax.ShapeDtypeStruct((3, long, model), BF16),
        ],
        input_output_aliases={4: 0, 5: 1, 6: 2} if earlier else {},
        compiler_params=pltpu.CompilerParams(vmem_limit_bytes=24 * MIB),
        cost_estimate=pl.CostEstimate(flops=0, bytes_accessed=0, transcendentals=0),
        name="mixer_forward",
    )(ids, rows, *pieces, *earlier)


def feedforward_kernel(own, ids, gated, mixer, tokens, gain, cotangent, *rest):
    places, rest = rest[:12], rest[12:]
    outputs = rest[-8 - own : -2]
    weights, arrived = rest[-2:]
    normed, down, grad_normed, hidden, grad_gate, grad_up = outputs[:6]
    part = places[0].shape[0]
    count = mixer.shape[0]
    channels = mixer.shape[3]
    first = pl.program_id(0) == 0

    def copies(which):
        for place in range(4):
            start = pl.multiple_of((ids[0] ^ place) * part, part)
            yield pltpu.make_async_copy(
                places[4 * which + place],
                weights.at[which, pl.ds(start, part), :],
                arrived.at[which, place],
            )

    @pl.when(first)
    def _():
        for which in range(3):
            for copy in copies(which):
                copy.start()

    middle = tokens[0].astype(F32)
    for block in range(count):
        middle += dot_nt(gated[0, :, block * channels : (block + 1) * channels], mixer[block, 0])
    if own:
        rest[-3][...] = middle
    values = (norm_forward(middle)[0] * gain[...].astype(F32)).astype(BF16)
    normed[0] = values

    @pl.when(first)
    def _():
        for which in range(3):
            for copy in copies(which):
                copy.wait()

    gate = dot_nn(values, weights[0])
    up = dot_nn(values, weights[1])
    grad_hidden = dot_nn(cotangent[0], weights[2])
    sigmoid = jax.nn.sigmoid(gate)
    silu = gate * sigmoid
    hidden_now = (silu * up).astype(BF16)
    hidden[0] = hidden_now
    gate_now = (grad_hidden * up * sigmoid * (1.0 + gate * (1.0 - sigmoid))).astype(BF16)
    up_now = (grad_hidden * silu).astype(BF16)
    grad_gate[0] = gate_now
    grad_up[0] = up_now
    grad_normed[...] = (dot_nt(gate_now, weights[0]) + dot_nt(up_now, weights[1])).astype(BF16)
    down[...] = dot_nt(hidden_now, weights[2]).astype(BF16)


def feedforward(ids, gated, mixer, tokens, gain, cotangent, places, which, earlier):
    seqs, width, model = tokens.shape
    units = places[0].shape[1]
    count, _, _, channels = mixer.shape
    size = width // 2
    own = int(which == 3)

    def seq(i, ids):
        return (ids[3 + which], i, 0)

    def row(i, ids):
        return (i, 0)

    wide = jax.ShapeDtypeStruct((seqs, width, units), BF16)
    here = jax.ShapeDtypeStruct((width, model), BF16)
    first = 6 + len(places)
    return pl.pallas_call(
        functools.partial(feedforward_kernel, own),
        grid_spec=pltpu.PrefetchScalarGridSpec(
            num_scalar_prefetch=1,
            grid=(2,),
            in_specs=[
                pl.BlockSpec((1, size, model), seq),
                pl.BlockSpec((count, 1, model, channels), lambda i, ids: (0, 3, 0, 0), pipeline_mode=pl.Buffered(1)),
                pl.BlockSpec((1, size, model), seq),
                pl.BlockSpec((1, model), lambda i, ids: (0, 0)),
                pl.BlockSpec((1, size, model), seq),
            ]
            + [pl.BlockSpec(memory_space=pl.ANY)] * (len(places) + len(earlier)),
            out_specs=[
                pl.BlockSpec((1, size, model), seq),
                pl.BlockSpec((size, model), row),
                pl.BlockSpec((size, model), row),
                pl.BlockSpec((1, size, units), seq),
                pl.BlockSpec((1, size, units), seq),
                pl.BlockSpec((1, size, units), seq),
            ]
            + [pl.BlockSpec((size, model), row)] * own,
            scratch_shapes=[
                pltpu.VMEM((3, model, units), BF16),
                pltpu.SemaphoreType.DMA((3, 4)),
            ],
        ),
        out_shape=[
            jax.ShapeDtypeStruct(tokens.shape, BF16),
            here,
            here,
            wide,
            wide,
            wide,
        ]
        + [jax.ShapeDtypeStruct((width, model), F32)] * own,
        input_output_aliases={first: 0, first + 1: 3, first + 2: 4, first + 3: 5} if earlier else {},
        compiler_params=pltpu.CompilerParams(vmem_limit_bytes=40 * MIB),
        cost_estimate=pl.CostEstimate(flops=0, bytes_accessed=0, transcendentals=0),
        name="feedforward",
    )(ids, gated, mixer, tokens, gain, cotangent, *places, *earlier)


def mixer_backward_kernel(
    ids, part0, part1, part2, own, cotangent, gain, gates, weights, taps,
    grad_middle, grad_mixed, gain_grad, grad_convolved, grad_out_gate, tap_grads,
):
    @pl.when(pl.program_id(0) == 0)
    def _():
        incoming = sum(part[...].astype(F32) for part in (part0, part1, part2))
        plain, inverse = norm_forward(own[...])
        gain_grad[...] = jnp.sum(incoming * plain, axis=0, keepdims=True)
        total = cotangent[0].astype(F32) + norm_backward(
            incoming, plain, inverse, gain[...].astype(F32)
        )
        grad_middle[...] = total
        grad_mixed[...] = total.astype(BF16)

    tap = taps[0].astype(F32)
    out_gate = gates[1, LEAD:, :].astype(F32)
    product = (gates[0].astype(F32) * gates[2].astype(F32)).astype(BF16).astype(F32)
    recent, previous, earlier = (
        product[LEAD:], pltpu.roll(product, 1, 0)[LEAD:], pltpu.roll(product, 2, 0)[LEAD:],
    )
    convolved = tap[0:1] * recent + tap[1:2] * previous + tap[2:3] * earlier
    grad_gated = dot_nn(grad_mixed[...], weights[0, 0])
    grad_out_gate[...] = (grad_gated * convolved).astype(BF16)
    low = (grad_gated * out_gate).astype(BF16)
    grad_convolved[...] = low
    low = low.astype(F32)
    tap_grads[0] = jnp.concatenate(
        [
            jnp.sum(low * recent, axis=0, keepdims=True),
            jnp.sum(low * previous, axis=0, keepdims=True),
            jnp.sum(low * earlier, axis=0, keepdims=True),
            jnp.zeros((5, low.shape[1]), F32),
        ]
    )


def mixer_backward(ids, parts, own, cotangent, gain, gates, weights, taps):
    width, model = own.shape
    long = gates.shape[1]
    count, _, _, part = weights.shape
    whole = pl.BlockSpec((width, model), lambda j, ids: (0, 0))
    once = pl.BlockSpec((width, model), lambda j, ids: (0, 0), pipeline_mode=pl.Buffered(1))
    line = pl.BlockSpec((1, model), lambda j, ids: (0, 0))
    column = pl.BlockSpec((width, part), lambda j, ids: (0, j))
    return pl.pallas_call(
        mixer_backward_kernel,
        grid_spec=pltpu.PrefetchScalarGridSpec(
            num_scalar_prefetch=1,
            grid=(count,),
            in_specs=[
                once, once, once, once,
                pl.BlockSpec((1, width, model), lambda j, ids: (ids[1], 0, 0)),
                line,
                pl.BlockSpec((3, long, part), lambda j, ids: (0, 0, j)),
                pl.BlockSpec((1, 1, model, part), lambda j, ids: (j, 3, 0, 0)),
                pl.BlockSpec((1, LEAD, part), lambda j, ids: (j, 0, 0)),
            ],
            out_specs=[
                whole, whole, line, column, column,
                pl.BlockSpec((1, 8, part), lambda j, ids: (j, 0, 0)),
            ],
        ),
        out_shape=[
            jax.ShapeDtypeStruct((width, model), F32),
            jax.ShapeDtypeStruct((width, model), BF16),
            jax.ShapeDtypeStruct((1, model), F32),
            jax.ShapeDtypeStruct((width, model), BF16),
            jax.ShapeDtypeStruct((width, model), BF16),
            jax.ShapeDtypeStruct((count, 8, part), F32),
        ],
        compiler_params=pltpu.CompilerParams(vmem_limit_bytes=36 * MIB),
        cost_estimate=pl.CostEstimate(flops=0, bytes_accessed=0, transcendentals=0),
        name="mixer_backward",
    )(ids, *parts, own, cotangent, gain, gates, weights, taps)


def input_backward_kernel(
    ids, grad_convolved, edge, gates, grad_out_gate, taps, weights, grad_middle, tokens, gain,
    grad_first, grad_third, grad_tokens, gain_grad, total,
):
    block = pl.program_id(0)
    width = grad_convolved.shape[0]
    tap = taps[0].astype(F32)
    longer = jnp.concatenate([grad_convolved[...], edge[...]]).astype(F32)
    count = longer.shape[0]
    grad_product = (
        tap[0:1] * longer
        + tap[1:2] * pltpu.roll(longer, count - 1, 0)
        + tap[2:3] * pltpu.roll(longer, count - 2, 0)
    )[:width]
    first = (grad_product * gates[2, LEAD:, :].astype(F32)).astype(BF16)
    third = (grad_product * gates[0, LEAD:, :].astype(F32)).astype(BF16)
    grad_first[...] = first
    grad_third[...] = third
    here = (
        dot_nt(first, weights[0, 0])
        + dot_nt(grad_out_gate[...], weights[0, 1])
        + dot_nt(third, weights[0, 2])
    )

    @pl.when(block == 0)
    def _():
        total[...] = here

    @pl.when(block > 0)
    def _():
        total[...] += here

    @pl.when(block == pl.num_programs(0) - 1)
    def _():
        incoming = total[...]
        plain, inverse = norm_forward(tokens[0].astype(F32))
        gain_grad[...] = jnp.sum(incoming * plain, axis=0, keepdims=True)
        grad_tokens[...] = (
            grad_middle[...] + norm_backward(incoming, plain, inverse, gain[...].astype(F32))
        ).astype(BF16)


def input_backward(
    ids, grad_convolved, edge, gates, grad_out_gate, taps, weights, grad_middle, tokens, gain
):
    width, model = grad_middle.shape
    long = gates.shape[1]
    count, _, _, part = weights.shape
    whole = pl.BlockSpec((width, model), lambda j, ids: (0, 0))
    line = pl.BlockSpec((1, model), lambda j, ids: (0, 0))
    column = pl.BlockSpec((width, part), lambda j, ids: (0, j))
    return pl.pallas_call(
        input_backward_kernel,
        grid_spec=pltpu.PrefetchScalarGridSpec(
            num_scalar_prefetch=1,
            grid=(count,),
            in_specs=[
                column,
                pl.BlockSpec((edge.shape[0], part), lambda j, ids: (0, j)),
                pl.BlockSpec((3, long, part), lambda j, ids: (0, 0, j)),
                column,
                pl.BlockSpec((1, LEAD, part), lambda j, ids: (j, 0, 0)),
                pl.BlockSpec((1, 3, model, part), lambda j, ids: (j, 0, 0, 0)),
                whole,
                pl.BlockSpec((1, width, model), lambda j, ids: (ids[1], 0, 0)),
                line,
            ],
            out_specs=[column, column, whole, line],
            scratch_shapes=[pltpu.VMEM((width, model), F32)],
        ),
        out_shape=[
            jax.ShapeDtypeStruct((width, model), BF16),
            jax.ShapeDtypeStruct((width, model), BF16),
            jax.ShapeDtypeStruct((width, model), BF16),
            jax.ShapeDtypeStruct((1, model), F32),
        ],
        compiler_params=pltpu.CompilerParams(vmem_limit_bytes=44 * MIB),
        cost_estimate=pl.CostEstimate(flops=0, bytes_accessed=0, transcendentals=0),
        name="input_backward",
    )(ids, grad_convolved, edge, gates, grad_out_gate, taps, weights, grad_middle, tokens, gain)


def split_rows(ids, g):
    return ids[7 + g]


def feedforward_gradient_kernel(ids, left, right, send, keep):
    result = dot_tn(left[...], right[...]).astype(BF16)

    @pl.when(pl.program_id(0) < 2)
    def _():
        send[0] = result

    @pl.when(pl.program_id(0) >= 2)
    def _():
        keep[0] = result


def feedforward_gradient(ids, left, right):
    tokens, model = left.shape
    units = right.shape[1]
    part = model // 4
    shape = jax.ShapeDtypeStruct((2, part, units), BF16)
    return pl.pallas_call(
        feedforward_gradient_kernel,
        grid_spec=pltpu.PrefetchScalarGridSpec(
            num_scalar_prefetch=1,
            grid=(4,),
            in_specs=[
                pl.BlockSpec((tokens, part), lambda g, ids: (0, split_rows(ids, g))),
                pl.BlockSpec((tokens, units), lambda g, ids: (0, 0), pipeline_mode=pl.Buffered(1)),
            ],
            out_specs=[
                pl.BlockSpec((1, part, units), lambda g, ids: (jnp.minimum(g, 1), 0, 0)),
                pl.BlockSpec((1, part, units), lambda g, ids: (jnp.maximum(g - 2, 0), 0, 0)),
            ],
        ),
        out_shape=[shape, shape],
        compiler_params=pltpu.CompilerParams(vmem_limit_bytes=32 * MIB),
        cost_estimate=pl.CostEstimate(flops=0, bytes_accessed=0, transcendentals=0),
        name="feedforward_gradient",
    )(ids, left, right)


def mixer_gradient_kernel(ids, rows, mixed, first, second, third, gated, send, keep):
    part = mixed.shape[1]
    here = []
    for left, right in (
        (rows[0, LEAD:], first[...]),
        (rows[0, LEAD:], second[...]),
        (rows[0, LEAD:], third[...]),
        (mixed[...], gated[0]),
    ):
        here.append(dot_tn(left, right).astype(BF16))

    def store(out):
        for matrix, value in enumerate(here):
            for block in range(4):
                for upper in range(2):
                    out[0, ids[2] ^ upper, ids[11 + block], matrix] = value[
                        upper * part // 2 : (upper + 1) * part // 2, block * part : (block + 1) * part
                    ]

    @pl.when(pl.program_id(0) < 2)
    def _():
        store(send)

    @pl.when(pl.program_id(0) >= 2)
    def _():
        store(keep)


def mixer_gradient(ids, rows, mixed, first, second, third, gated):
    width, model = mixed.shape
    long = rows.shape[1]
    part = model // 4
    shape = jax.ShapeDtypeStruct((2, 2, 4, 4, part // 2, part), BF16)
    block = (1, 2, 4, 4, part // 2, part)
    whole = pl.BlockSpec((width, model), lambda g, ids: (0, 0))
    return pl.pallas_call(
        mixer_gradient_kernel,
        grid_spec=pltpu.PrefetchScalarGridSpec(
            num_scalar_prefetch=1,
            grid=(4,),
            in_specs=[
                pl.BlockSpec((1, long, part), lambda g, ids: (ids[1], 0, split_rows(ids, g))),
                pl.BlockSpec((width, part), lambda g, ids: (0, split_rows(ids, g))),
                whole, whole, whole,
                pl.BlockSpec((1, width, model), lambda g, ids: (ids[1], 0, 0)),
            ],
            out_specs=[
                pl.BlockSpec(block, lambda g, ids: (jnp.minimum(g, 1), 0, 0, 0, 0, 0)),
                pl.BlockSpec(block, lambda g, ids: (jnp.maximum(g - 2, 0), 0, 0, 0, 0, 0)),
            ],
        ),
        out_shape=[shape, shape],
        compiler_params=pltpu.CompilerParams(vmem_limit_bytes=40 * MIB),
        cost_estimate=pl.CostEstimate(flops=0, bytes_accessed=0, transcendentals=0),
        name="mixer_gradient",
    )(ids, rows, mixed, first, second, third, gated)


def local_by_links(
    tokens, norm_gain, w_in, conv_weight, convolution_out_weight, ffn_gain, w_gate, w_up, w_down, cotangent
):
    seqs, width, model = tokens.shape
    part = w_in.shape[1]
    units = w_gate.shape[1]
    shard, side, level = (lax.axis_index(name) for name in ("shard", "context", "tensor"))
    end = jnp.logical_or(level == 0, level == 3)
    order = [
        jnp.where(level < 2, 3, 0), jnp.where(level < 2, 2, 1), level ^ 1, level,
    ]
    place = [sum(jnp.where((level + block) % 4 == order[k], k, 0) for k in range(4)) for block in range(4)]
    ids = jnp.stack(
        [shard, level, side] + order + [shard ^ 1, shard ^ 3, shard, shard ^ 2] + place
    ).astype(jnp.int32)
    gain_one = norm_gain.reshape(1, model)
    gain_two = ffn_gain.reshape(1, model)
    def placed(own, others, dtype):
        out = jnp.zeros((seqs, width, model), dtype)
        for bits, block in enumerate((own,) + others):
            out = lax.dynamic_update_slice(out, block.astype(dtype)[None], (level ^ bits, 0, 0))
        return out

    taps_near = jnp.concatenate([conv_weight, jnp.zeros((LEAD - 3, part), BF16)])
    near = jnp.concatenate(
        [w_in[0], w_in[1], taps_near, w_in[2], convolution_out_weight.T, taps_near]
    )
    half = near.shape[0] // 2

    def sides(value):
        return [lax.dynamic_slice_in_dim(value, (side ^ bit) * half, half, 0) for bit in range(2)]

    near, near_side, near_else = together(near, *sides(near))
    far = to_y(near)
    near_right, near_left = shifted(near_side, -1), shifted(near_side, 1)
    edge = lax.ppermute(tokens[:, width - 2 :, :], "context", [(0, 1)])
    w_down = w_down.T
    feed = jnp.concatenate([w_gate, w_up, w_down])
    far, near_right, near_left, edge, feed, near_side, near_else, w_gate, w_up, w_down = together(
        far, near_right, near_left, edge, feed, near_side, near_else, w_gate, w_up, w_down
    )

    far_side, far_else = sides(far)
    far_right, far_left = shifted(far_side, -1), shifted(far_side, 1)
    near_over = to_x(jnp.concatenate([near_right, near_left]))
    far_gate = to_y(w_gate)
    mine = together(jnp.concatenate([near_side, near_else, far_side, far_else]))[0]
    other = to_core(mine)
    rows = jnp.concatenate([jnp.zeros((seqs, LEAD - 2, model), BF16), edge, tokens], axis=1).astype(F32)
    rows = (norm_forward(rows)[0] * gain_one.astype(F32)).astype(BF16)
    state = mixer_forward(ids, rows, (mine, other), 0, ())
    far_right, far_left, near_over, near_right, near_left, rows, feed, w_up, w_down, far_gate, *state = together(
        far_right, far_left, near_over, near_right, near_left, rows, feed, w_up, w_down, far_gate, *state
    )

    near_far, far_far = shifted(near_right, -1), shifted(far_left, 1)
    far_over = to_x(jnp.concatenate([far_right, far_left]))
    far_up = to_y(w_up)
    feed_core = to_core(feed)
    near_far, far_far, far_over, feed_core, far_up, w_down, *state = together(
        near_far, far_far, far_over, feed_core, far_up, w_down, *state
    )

    last_over = to_x(jnp.concatenate([near_far, far_far]))
    far_down = to_y(w_down)
    for block, rows_of, (a, b) in (
        (1, slice(None, half), (near_right, far_right)),
        (3, slice(half, None), (near_left, far_left)),
    ):
        mine = together(jnp.concatenate([a, near_over[rows_of], b, far_over[rows_of]]))[0]
        state = mixer_forward(ids, rows, (mine, to_core(mine)), block, state)
    last_over, far_down, far_gate, far_up, *state = together(
        last_over, far_down, far_gate, far_up, *state
    )

    mine = together(jnp.concatenate([near_far, last_over[:half], far_far, last_over[half:]]))[0]
    state = mixer_forward(ids, rows, (mine, to_core(mine)), 2, state)
    gated, weights, gates = state
    far_all = (far_gate, far_up, far_down)
    core_all = [to_core(value) for value in far_all]
    gated, weights, gates, *core_all = together(gated, weights, gates, *core_all)
    places = []
    for which in range(3):
        rows_of = slice(which * part, (which + 1) * part)
        places += [feed[rows_of], feed_core[rows_of], far_all[which], core_all[which]]
    taps = jnp.stack([near_side[2 * part :], near_right[2 * part :], near_far[2 * part :], near_left[2 * part :]])

    def forward(which, earlier):
        normed, down, grad, *wide = feedforward(
            ids, gated, weights, tokens, gain_two, cotangent, places, which, earlier
        )
        return down, grad, (normed, *wide[:3]), wide[3:]

    down0, grad0, done, _ = forward(0, ())
    down0, grad0, *done = together(down0, grad0, *done)

    grad_pair0 = pair(grad0)
    down1, grad1, done, _ = forward(1, tuple(done))
    grad_pair0, down1, grad1, *done = together(grad_pair0, down1, grad1, *done)

    grad_pair1 = pair(grad1)
    grad_over0 = across(added(grad0, grad_pair0))
    down2, grad2, done, _ = forward(2, tuple(done))
    grad_pair1, grad_over0, down2, grad2, *done = together(grad_pair1, grad_over0, down2, grad2, *done)

    grad_pair2 = pair(added(grad2, grad_over0))
    grad_over1 = across(added(grad1, grad_pair1))
    down3, grad3, done, (middle_own,) = forward(3, tuple(done))
    normed, hidden, grad_gate, grad_up = (v.reshape(seqs * width, v.shape[2]) for v in done)
    send_down, keep_down = feedforward_gradient(ids, cotangent.reshape(seqs * width, model), hidden)
    grad_pair2, grad_over1, grad3, normed, grad_gate, grad_up, send_down, keep_down, down0 = together(
        grad_pair2, grad_over1, grad3, normed, grad_gate, grad_up, send_down, keep_down, down0
    )

    down_pair0 = pair(down0)
    core_down = to_core(send_down)
    grad_middle, grad_mixed, gain_two_grad, grad_convolved, grad_out_gate, tap_grads = mixer_backward(
        ids, (grad3, grad_pair2, grad_over1), middle_own, cotangent, gain_two, gates, weights, taps
    )
    behind = lax.ppermute(grad_convolved[:LEAD], "context", [(1, 0)])
    grad_first, grad_third, tokens_own, gain_one_grad = input_backward(
        ids, grad_convolved, behind, gates, grad_out_gate, taps, weights, grad_middle, tokens, gain_one
    )
    (
        down_pair0, core_down, tokens_own, grad_first, grad_third, grad_mixed, gain_one_grad,
        normed, grad_gate, grad_up,
    ) = together(
        down_pair0, core_down, tokens_own, grad_first, grad_third, grad_mixed, gain_one_grad,
        normed, grad_gate, grad_up,
    )

    tokens_pair = pair(tokens_own)
    tokens_over = across(tokens_own)
    y_down = to_y(added(keep_down[1], core_down[1]))
    send_mixer, keep_mixer = mixer_gradient(
        ids, rows, grad_mixed, grad_first, grad_out_gate, grad_third, gated
    )
    send_gate, keep_gate = feedforward_gradient(ids, normed, grad_gate)
    tokens_pair, tokens_over, y_down, send_mixer, keep_mixer, send_gate, keep_gate, grad_up = together(
        tokens_pair, tokens_over, y_down, send_mixer, keep_mixer, send_gate, keep_gate, grad_up
    )

    mixed_pair1 = pair(jnp.where(end, down1, tokens_over))
    tokens_over_end = across(tokens_pair)
    core_mixer = to_core(send_mixer)
    core_gate = to_core(send_gate)
    mine_down = rounded(added(keep_down[0], core_down[0], y_down))
    x_down = to_x(mine_down)
    send_up, keep_up = feedforward_gradient(ids, normed, grad_up)
    tap_rows = tap_grads[:, :3].transpose(1, 0, 2)
    tap_rows = jnp.roll(tap_rows, level, axis=1).reshape(3, model)
    small = jnp.concatenate([gain_one_grad, gain_two_grad, tap_rows, jnp.zeros((3, model), F32)])
    mixed_pair1, tokens_over_end, core_mixer, core_gate, x_down, send_up, keep_up, small, down0 = together(
        mixed_pair1, tokens_over_end, core_mixer, core_gate, x_down, send_up, keep_up, small, down0
    )

    mixed_pair2 = pair(jnp.where(end, down2, tokens_over_end))
    down_over0 = across(added(down0, down_pair0))
    y_mixer1 = to_y(added(keep_mixer[1, 1], core_mixer[1, 1]))
    core_up = to_core(send_up)
    small = small + to_core(small)
    total_down = (mine_down.astype(F32) + x_down.astype(F32)).T
    mixed_pair2, down_over0, y_mixer1, core_up, small, total_down, keep_mixer = together(
        mixed_pair2, down_over0, y_mixer1, core_up, small, total_down, keep_mixer
    )

    down_pair3 = pair(added(down2, down_over0))
    down_over1 = across(added(down1, mixed_pair1))
    x_mixer = to_x(added(keep_mixer[0, 1], core_mixer[0, 1], y_mixer1))
    y_mixer0 = to_y(added(keep_mixer[1, 0], core_mixer[1, 0]))
    grad_tokens = placed(
        tokens_own,
        (
            tokens_pair,
            jnp.where(end, mixed_pair1, tokens_over_end),
            jnp.where(end, mixed_pair2, tokens_over),
        ),
        F32,
    )
    down_pair3, down_over1, x_mixer, y_mixer0, grad_tokens, keep_gate, keep_up = together(
        down_pair3, down_over1, x_mixer, y_mixer0, grad_tokens, keep_gate, keep_up
    )

    out_own = rounded(
        middle_own
        + down3.astype(F32)
        + jnp.where(end, down_pair3, mixed_pair2).astype(F32)
        + down_over1.astype(F32)
    )
    out_pair = pair(out_own)
    out_over = across(out_own)
    y_both = to_y(
        jnp.concatenate([added(keep_gate[1], core_gate[1]), added(keep_up[1], core_up[1])])
    )
    mixer = added(keep_mixer[0, 0], core_mixer[0, 0], y_mixer0, x_mixer)
    mixer_three = jnp.concatenate([mixer[:3].reshape(-1, model), jnp.zeros((width // 4, model), BF16)])
    small = small + to_x(small)
    out_pair, out_over, y_both, small, mixer, mixer_three = together(
        out_pair, out_over, y_both, small, mixer, mixer_three
    )

    out_over_end = across(out_pair)
    mixed_pair3 = pair(jnp.where(end, mixer_three, out_over))
    mine_both = rounded(
        added(
            jnp.concatenate([keep_gate[0], keep_up[0]]),
            jnp.concatenate([core_gate[0], core_up[0]]),
            y_both,
        )
    )
    x_both = to_x(mine_both)
    small = small + swapped(small, "tensor", 1)
    out_over_end, mixed_pair3, x_both, small = together(out_over_end, mixed_pair3, x_both, small)

    out_pair2 = pair(out_over_end)
    mixer_in = mixed_pair3[: 3 * width // 4].reshape(mixer[:3].shape)
    mixer_over = across(added(mixer[:2], mixer_in[:2]))
    total_both = mine_both.astype(F32) + x_both.astype(F32)
    total_gate, total_up = total_both[:part], total_both[part:]
    small = small + to_y(small)
    mixer_out = pair(added(mixer[2], mixer_over[0]))
    mine = rounded(
        mixer[3].astype(F32)
        + jnp.where(end, mixer_out, mixer_in[2]).astype(F32)
        + mixer_over[1].astype(F32)
    )
    other = to_x(mine)
    total = jnp.concatenate(
        [jnp.where(side == 0, mine, other), jnp.where(side == 0, other, mine)], axis=1
    ).astype(F32)
    small = small + swapped(small, "tensor", 2)
    total_taps = lax.dynamic_slice(small, (2, level * part), (3, part))
    block_out = placed(
        out_own,
        (out_pair, jnp.where(end, mixed_pair3, out_over_end), jnp.where(end, out_pair2, out_over)),
        BF16,
    )
    return (
        block_out, grad_tokens, small[0], total[:3], total_taps, total[3].T, small[1],
        total_gate, total_up, total_down,
    )


def from_behind(value, axis, steps):
    count = lax.axis_size(axis)
    initial, last = (max(0, -steps), min(count, count - steps))
    return lax.ppermute(value, axis, [(source, source + steps) for source in range(initial, last)])


def norm_backward_and_gain(grad_normed, plain, inverse, gain):
    grad_plain = grad_normed * gain
    grad_values = inverse * (
        grad_plain - plain * jnp.mean(grad_plain * plain, axis=-1, keepdims=True)
    )
    leading = tuple(range(grad_normed.ndim - 1))
    return (grad_values, jnp.sum(grad_normed * plain, axis=leading))


def local(
    tokens,
    norm_gain,
    w_in,
    conv_weight,
    convolution_out_weight,
    ffn_gain,
    w_gate,
    w_up,
    w_down,
    cotangent,
):
    input_rows = tokens.astype(jnp.float32)
    gain_one = norm_gain.astype(jnp.float32)
    gain_two = ffn_gain.astype(jnp.float32)
    taps = conv_weight.astype(jnp.float32)
    seqs, width, model = tokens.shape
    (
        complete_input_weight,
        complete_output_weight,
        feedforward_gate_weight,
        feedforward_up_weight,
        feedforward_down_weight,
    ) = (
        lax.all_gather(w_in, "shard", axis=1, tiled=True),
        lax.all_gather(convolution_out_weight, "shard", axis=1, tiled=True),
        lax.all_gather(w_gate, "shard", axis=0, tiled=True),
        lax.all_gather(w_up, "shard", axis=0, tiled=True),
        lax.all_gather(w_down, "shard", axis=1, tiled=True),
    )
    plain_one, inverse_one = norm_forward(input_rows)
    first_normalized = (plain_one * gain_one).astype(jnp.bfloat16)
    projection = jnp.einsum(
        "uiq,tqz->tuiz", first_normalized, complete_input_weight, preferred_element_type=jnp.float32
    )
    in_gate = projection[0]
    out_gate = projection[1]
    conv_input = projection[2]
    product = (in_gate * conv_input).astype(jnp.bfloat16)
    edge = from_behind(product[:, width - 2 :, :], "context", 1)
    extended = jnp.concatenate([edge, product], axis=1).astype(jnp.float32)
    recent = extended[:, 2:, :]
    previous = extended[:, 1 : width + 1, :]
    earlier = extended[:, :width, :]
    convolved = taps[0] * recent + taps[1] * previous + taps[2] * earlier
    gated_product = (out_gate * convolved).astype(jnp.bfloat16)
    partial_mixer_output = jnp.einsum(
        "zaw,wk->zak", gated_product, complete_output_weight, preferred_element_type=jnp.float32
    )
    residual_middle = input_rows + lax.psum(partial_mixer_output, "tensor")
    plain_two, inverse_two = norm_forward(residual_middle)
    second_normalized = (plain_two * gain_two).astype(jnp.bfloat16)
    gate_branch = jnp.einsum(
        "mut,tz->muz",
        second_normalized,
        feedforward_gate_weight,
        preferred_element_type=jnp.float32,
    )
    up_projection_branch = jnp.einsum(
        "mut,tz->muz", second_normalized, feedforward_up_weight, preferred_element_type=jnp.float32
    )
    sigmoid_gate = jax.nn.sigmoid(gate_branch)
    silu_gate = gate_branch * sigmoid_gate
    hidden_state = (silu_gate * up_projection_branch).astype(jnp.bfloat16)
    partial_feedforward = jnp.einsum(
        "eny,yv->env", hidden_state, feedforward_down_weight, preferred_element_type=jnp.float32
    )
    block_out = (
        residual_middle
        + lax.psum(partial_feedforward.astype(jnp.bfloat16), "tensor").astype(jnp.float32)
    ).astype(jnp.bfloat16)
    grad_out = cotangent.astype(jnp.float32)
    hidden_gradient = jnp.einsum(
        "qmn,pn->qmp", cotangent, feedforward_down_weight, preferred_element_type=jnp.float32
    )
    down_gradient = jnp.einsum(
        "eiu,eix->ux", hidden_state, cotangent, preferred_element_type=jnp.float32
    )
    gate_gradient = (
        hidden_gradient
        * up_projection_branch
        * sigmoid_gate
        * (1.0 + gate_branch * (1.0 - sigmoid_gate))
    ).astype(jnp.bfloat16)
    up_gradient = (hidden_gradient * silu_gate).astype(jnp.bfloat16)
    grad_w_gate = jnp.einsum(
        "rnj,rnt->jt", second_normalized, gate_gradient, preferred_element_type=jnp.float32
    )
    up_weight_gradient = jnp.einsum(
        "rnj,rnt->jt", second_normalized, up_gradient, preferred_element_type=jnp.float32
    )
    partial_normed_two = jnp.einsum(
        "wxo,qo->wxq", gate_gradient, feedforward_gate_weight, preferred_element_type=jnp.float32
    )
    partial_normed_two = partial_normed_two + jnp.einsum(
        "wxo,qo->wxq", up_gradient, feedforward_up_weight, preferred_element_type=jnp.float32
    )
    grad_normed_two = lax.psum(partial_normed_two, "tensor")
    grad_rows_two, gain_grad_two = norm_backward_and_gain(grad_normed_two, plain_two, inverse_two, gain_two)
    grad_middle = grad_out + grad_rows_two
    mixer_output_gradient = grad_middle.astype(jnp.bfloat16)
    grad_gated = jnp.einsum(
        "ymo,bo->ymb",
        mixer_output_gradient,
        complete_output_weight,
        preferred_element_type=jnp.float32,
    )
    out_weight_gradient = jnp.einsum(
        "miy,miq->yq", gated_product, mixer_output_gradient, preferred_element_type=jnp.float32
    )
    grad_convolved = (grad_gated * out_gate).astype(jnp.bfloat16)
    grad_out_gate = grad_gated * convolved
    grad_edge = from_behind(grad_convolved[:, :2, :], "context", -1)
    grad_extended = jnp.concatenate([grad_convolved, grad_edge], axis=1).astype(jnp.float32)
    grad_product = (
        taps[0] * grad_extended[:, :width, :]
        + taps[1] * grad_extended[:, 1 : width + 1, :]
        + taps[2] * grad_extended[:, 2:, :]
    )
    grad_local = grad_extended[:, :width, :]
    tap_grads = jnp.stack(
        [
            jnp.sum(grad_local * recent, axis=(0, 1)),
            jnp.sum(grad_local * previous, axis=(0, 1)),
            jnp.sum(grad_local * earlier, axis=(0, 1)),
        ]
    )
    projection_gradient = jnp.stack(
        [
            (grad_product * conv_input).astype(jnp.bfloat16),
            grad_out_gate.astype(jnp.bfloat16),
            (grad_product * in_gate).astype(jnp.bfloat16),
        ]
    )
    grad_w_in = jnp.einsum(
        "pxw,gpxt->gwt", first_normalized, projection_gradient, preferred_element_type=jnp.float32
    )
    partial_normed_one = jnp.einsum(
        "ireo,ivo->rev",
        projection_gradient,
        complete_input_weight,
        preferred_element_type=jnp.float32,
    )
    shard_in, shard_out, shard_gate, shard_up, shard_down = (
        lax.psum_scatter(
            grad_w_in.astype(jnp.bfloat16), "shard", scatter_dimension=1, tiled=True
        ).astype(jnp.float32),
        lax.psum_scatter(
            out_weight_gradient.astype(jnp.bfloat16), "shard", scatter_dimension=1, tiled=True
        ).astype(jnp.float32),
        lax.psum_scatter(
            grad_w_gate.astype(jnp.bfloat16), "shard", scatter_dimension=0, tiled=True
        ).astype(jnp.float32),
        lax.psum_scatter(
            up_weight_gradient.astype(jnp.bfloat16), "shard", scatter_dimension=0, tiled=True
        ).astype(jnp.float32),
        lax.psum_scatter(
            down_gradient.astype(jnp.bfloat16), "shard", scatter_dimension=1, tiled=True
        ).astype(jnp.float32),
    )
    total_in, total_out, total_gate, total_up, total_down = (
        lax.psum(shard_in.astype(jnp.bfloat16), "context").astype(jnp.float32),
        lax.psum(shard_out.astype(jnp.bfloat16), "context").astype(jnp.float32),
        lax.psum(shard_gate.astype(jnp.bfloat16), "context").astype(jnp.float32),
        lax.psum(shard_up.astype(jnp.bfloat16), "context").astype(jnp.float32),
        lax.psum(shard_down.astype(jnp.bfloat16), "context").astype(jnp.float32),
    )
    grad_normed_one = lax.psum(partial_normed_one.astype(jnp.bfloat16), "tensor").astype(
        jnp.float32
    )
    grad_rows_one, gain_grad_one = norm_backward_and_gain(grad_normed_one, plain_one, inverse_one, gain_one)
    grad_tokens = grad_middle + grad_rows_one
    total_gain_one, total_taps, total_gain_two = lax.psum(
        (gain_grad_one, tap_grads, gain_grad_two), ("shard", "context")
    )
    return (
        block_out,
        grad_tokens,
        total_gain_one,
        total_in,
        total_taps,
        total_out,
        total_gain_two,
        total_gate,
        total_up,
        total_down,
    )


def solution(mesh):
    in_specs = (
        P("shard", "context", None),
        P(),
        P(None, "shard", "tensor"),
        P(None, "tensor"),
        P("tensor", "shard"),
        P(),
        P("shard", "tensor"),
        P("shard", "tensor"),
        P("tensor", "shard"),
        P("shard", "context", None),
    )
    out_specs = (
        P("shard", "context", None),
        P("shard", "context", None),
        P(),
        P(None, "shard", "tensor"),
        P(None, "tensor"),
        P("tensor", "shard"),
        P(),
        P("shard", "tensor"),
        P("shard", "tensor"),
        P("tensor", "shard"),
    )
    sizes = mesh.shape
    by_links = (sizes["shard"], sizes["context"], sizes["tensor"]) == (4, 2, 4)
    body = local_by_links if by_links else local
    return jax.shard_map(body, mesh=mesh, in_specs=in_specs, out_specs=out_specs, check_vma=False)
```

```python
import functools

import jax
import jax.numpy as jnp
from jax import lax
from jax.experimental import pallas as pl
from jax.experimental.pallas import tpu as pltpu
from jax.sharding import PartitionSpec as P

EPSILON = 1e-05
F32 = jnp.float32
BF16 = jnp.bfloat16
MIB = 1024 * 1024
LEAD = 16


def norm_forward(values):
    inverse = lax.rsqrt(jnp.mean(values * values, axis=-1, keepdims=True) + EPSILON)
    return (values * inverse, inverse)


def norm_backward(grad_normed, plain, inverse, gain):
    grad_plain = grad_normed * gain
    return inverse * (
        grad_plain - plain * jnp.mean(grad_plain * plain, axis=-1, keepdims=True)
    )


def dot_nn(a, b):
    return lax.dot_general(a, b, (((1,), (0,)), ((), ())), preferred_element_type=F32)


def dot_nt(a, b):
    return lax.dot_general(a, b, (((1,), (1,)), ((), ())), preferred_element_type=F32)


def dot_tn(a, b):
    return lax.dot_general(a, b, (((0,), (0,)), ((), ())), preferred_element_type=F32)


def rounded(value):
    return lax.optimization_barrier(value.astype(BF16))


def shifted(value, steps):
    count = lax.axis_size("tensor")
    return lax.ppermute(value, "tensor", [(i, (i + steps) % count) for i in range(count)])


def swapped(value, axis, bit):
    count = lax.axis_size(axis)
    return lax.ppermute(value, axis, [(i, i ^ bit) for i in range(count)])


def to_core(value):
    return swapped(value, "shard", 1)


def to_y(value):
    return swapped(value, "shard", 2)


def to_x(value):
    return swapped(value, "context", 1)


def pair(value):
    return swapped(value, "tensor", 1)


def across(value):
    return lax.ppermute(value, "tensor", [(1, 2), (2, 1)])


def together(*values):
    return lax.optimization_barrier(values)


def added(*values):
    return sum(value.astype(F32) for value in values).astype(BF16)


def mixer_forward_kernel(ids, rows, mine, other, *rest):
    gated, weights, own = rest[-3:]
    part = mine.shape[1]
    half = 2 * part + LEAD

    @pl.when(pl.program_id(0) == 0)
    def _():
        for bit, piece in enumerate((mine, other)):
            for far in range(2):
                start = pl.multiple_of((ids[0] ^ (bit + 2 * far)) * part, part)
                for side in range(2):
                    first = 2 * (ids[2] ^ side)
                    base = (2 * far + side) * half
                    for which in range(2):
                        weights[0, first + which, pl.ds(start, part), :] = piece[
                            base + which * part : base + (which + 1) * part, :
                        ]

    taps = mine[2 * part : half, :].astype(F32)
    values = rows[0]
    in_gate = dot_nn(values, weights[0, 0])
    conv_input = dot_nn(values, weights[0, 2])
    out_gate = dot_nn(values, weights[0, 1])
    product = (in_gate * conv_input).astype(BF16).astype(F32)
    convolved = (
        taps[0:1] * product
        + taps[1:2] * pltpu.roll(product, 1, 0)
        + taps[2:3] * pltpu.roll(product, 2, 0)
    )[LEAD:]
    gated[0] = (out_gate[LEAD:] * convolved).astype(BF16)

    @pl.when(pl.program_id(0) == ids[1])
    def _():
        own[0] = in_gate.astype(BF16)
        own[1] = out_gate.astype(BF16)
        own[2] = conv_input.astype(BF16)


def mixer_forward(ids, rows, pieces, block, earlier):
    seqs, long, model = rows.shape
    width = long - LEAD
    part = pieces[0].shape[1]
    count = model // part
    specs = [pl.BlockSpec((1, long, model), lambda q, ids: (q, 0, 0))]
    specs += [pl.BlockSpec(piece.shape, lambda q, ids: (0, 0)) for piece in pieces]
    specs += [pl.BlockSpec(memory_space=pl.ANY)] * len(earlier)
    return pl.pallas_call(
        mixer_forward_kernel,
        grid_spec=pltpu.PrefetchScalarGridSpec(
            num_scalar_prefetch=1,
            grid=(seqs,),
            in_specs=specs,
            out_specs=[
                pl.BlockSpec((1, width, part), lambda q, ids: (q, 0, block)),
                pl.BlockSpec((1, 4, model, part), lambda q, ids: (block, 0, 0, 0)),
                pl.BlockSpec((3, long, part), lambda q, ids: (0, 0, block)),
            ],
        ),
        out_shape=[
            jax.ShapeDtypeStruct((seqs, width, model), BF16),
            jax.ShapeDtypeStruct((count, 4, model, part), BF16),
            jax.ShapeDtypeStruct((3, long, model), BF16),
        ],
        input_output_aliases={4: 0, 5: 1, 6: 2} if earlier else {},
        compiler_params=pltpu.CompilerParams(vmem_limit_bytes=24 * MIB),
        cost_estimate=pl.CostEstimate(flops=0, bytes_accessed=0, transcendentals=0),
        name="mixer_forward",
    )(ids, rows, *pieces, *earlier)


def feedforward_kernel(own, ids, gated, mixer, tokens, gain, cotangent, *rest):
    near, near_core, *rest = rest
    far, rest = rest[:6], rest[6:]
    outputs = rest[-8 - own : -2]
    weights, arrived = rest[-2:]
    normed, down, grad_normed, hidden, grad_gate, grad_up = outputs[:6]
    part = far[0].shape[0]
    count = mixer.shape[0]
    channels = mixer.shape[3]
    first = pl.program_id(0) == 0

    def copies(which):
        rows = pl.ds(which * part, part)
        sources = (near.at[rows, :], near_core.at[rows, :], far[which], far[3 + which])
        for place, source in enumerate(sources):
            start = pl.multiple_of((ids[0] ^ place) * part, part)
            yield pltpu.make_async_copy(
                source,
                weights.at[which, pl.ds(start, part), :],
                arrived.at[which, place],
            )

    @pl.when(first)
    def _():
        for which in range(3):
            for copy in copies(which):
                copy.start()

    middle = tokens[0].astype(F32)
    for block in range(count):
        middle += dot_nt(gated[0, :, block * channels : (block + 1) * channels], mixer[block, 0])
    if own:
        rest[-3][...] = middle
    values = (norm_forward(middle)[0] * gain[...].astype(F32)).astype(BF16)
    normed[0] = values

    @pl.when(first)
    def _():
        for which in range(3):
            for copy in copies(which):
                copy.wait()

    gate = dot_nn(values, weights[0])
    up = dot_nn(values, weights[1])
    grad_hidden = dot_nn(cotangent[0], weights[2])
    sigmoid = jax.nn.sigmoid(gate)
    silu = gate * sigmoid
    hidden_now = (silu * up).astype(BF16)
    hidden[0] = hidden_now
    gate_now = (grad_hidden * up * sigmoid * (1.0 + gate * (1.0 - sigmoid))).astype(BF16)
    up_now = (grad_hidden * silu).astype(BF16)
    grad_gate[0] = gate_now
    grad_up[0] = up_now
    grad_normed[...] = (dot_nt(gate_now, weights[0]) + dot_nt(up_now, weights[1])).astype(BF16)
    down[...] = dot_nt(hidden_now, weights[2]).astype(BF16)


def feedforward(ids, gated, mixer, tokens, gain, cotangent, places, which, earlier):
    seqs, width, model = tokens.shape
    units = places[0].shape[1]
    count, _, _, channels = mixer.shape
    size = width // 2
    own = int(which == 3)

    def seq(i, ids):
        return (ids[3 + which], i, 0)

    def row(i, ids):
        return (i, 0)

    wide = jax.ShapeDtypeStruct((seqs, width, units), BF16)
    here = jax.ShapeDtypeStruct((width, model), BF16)
    first = 6 + len(places)
    return pl.pallas_call(
        functools.partial(feedforward_kernel, own),
        grid_spec=pltpu.PrefetchScalarGridSpec(
            num_scalar_prefetch=1,
            grid=(2,),
            in_specs=[
                pl.BlockSpec((1, size, model), seq),
                pl.BlockSpec((count, 1, model, channels), lambda i, ids: (0, 3, 0, 0), pipeline_mode=pl.Buffered(1)),
                pl.BlockSpec((1, size, model), seq),
                pl.BlockSpec((1, model), lambda i, ids: (0, 0)),
                pl.BlockSpec((1, size, model), seq),
            ]
            + [pl.BlockSpec(memory_space=pltpu.HBM)] * len(places)
            + [pl.BlockSpec(memory_space=pl.ANY)] * len(earlier),
            out_specs=[
                pl.BlockSpec((1, size, model), seq),
                pl.BlockSpec((size, model), row),
                pl.BlockSpec((size, model), row),
                pl.BlockSpec((1, size, units), seq),
                pl.BlockSpec((1, size, units), seq),
                pl.BlockSpec((1, size, units), seq),
            ]
            + [pl.BlockSpec((size, model), row)] * own,
            scratch_shapes=[
                pltpu.VMEM((3, model, units), BF16),
                pltpu.SemaphoreType.DMA((3, 4)),
            ],
        ),
        out_shape=[
            jax.ShapeDtypeStruct(tokens.shape, BF16),
            here,
            here,
            wide,
            wide,
            wide,
        ]
        + [jax.ShapeDtypeStruct((width, model), F32)] * own,
        input_output_aliases={first: 0, first + 1: 3, first + 2: 4, first + 3: 5} if earlier else {},
        compiler_params=pltpu.CompilerParams(vmem_limit_bytes=40 * MIB),
        cost_estimate=pl.CostEstimate(flops=0, bytes_accessed=0, transcendentals=0),
        name="feedforward",
    )(ids, gated, mixer, tokens, gain, cotangent, *places, *earlier)


def mixer_backward_kernel(
    ids, part0, part1, part2, own, cotangent, gain, gates, weights, taps,
    grad_middle, grad_mixed, gain_grad, grad_convolved, grad_out_gate, tap_grads,
):
    @pl.when(pl.program_id(0) == 0)
    def _():
        incoming = sum(part[...].astype(F32) for part in (part0, part1, part2))
        plain, inverse = norm_forward(own[...])
        gain_grad[...] = jnp.sum(incoming * plain, axis=0, keepdims=True)
        total = cotangent[0].astype(F32) + norm_backward(
            incoming, plain, inverse, gain[...].astype(F32)
        )
        grad_middle[...] = total
        grad_mixed[...] = total.astype(BF16)

    tap = taps[0].astype(F32)
    out_gate = gates[1, LEAD:, :].astype(F32)
    product = (gates[0].astype(F32) * gates[2].astype(F32)).astype(BF16).astype(F32)
    recent, previous, earlier = (
        product[LEAD:], pltpu.roll(product, 1, 0)[LEAD:], pltpu.roll(product, 2, 0)[LEAD:],
    )
    convolved = tap[0:1] * recent + tap[1:2] * previous + tap[2:3] * earlier
    grad_gated = dot_nn(grad_mixed[...], weights[0, 0])
    grad_out_gate[...] = (grad_gated * convolved).astype(BF16)
    low = (grad_gated * out_gate).astype(BF16)
    grad_convolved[...] = low
    low = low.astype(F32)
    tap_grads[0] = jnp.concatenate(
        [
            jnp.sum(low * recent, axis=0, keepdims=True),
            jnp.sum(low * previous, axis=0, keepdims=True),
            jnp.sum(low * earlier, axis=0, keepdims=True),
            jnp.zeros((5, low.shape[1]), F32),
        ]
    )


def mixer_backward(ids, parts, own, cotangent, gain, gates, weights, taps):
    width, model = own.shape
    long = gates.shape[1]
    count, _, _, part = weights.shape
    whole = pl.BlockSpec((width, model), lambda j, ids: (0, 0))
    once = pl.BlockSpec((width, model), lambda j, ids: (0, 0), pipeline_mode=pl.Buffered(1))
    line = pl.BlockSpec((1, model), lambda j, ids: (0, 0))
    column = pl.BlockSpec((width, part), lambda j, ids: (0, j))
    return pl.pallas_call(
        mixer_backward_kernel,
        grid_spec=pltpu.PrefetchScalarGridSpec(
            num_scalar_prefetch=1,
            grid=(count,),
            in_specs=[
                once, once, once, once,
                pl.BlockSpec((1, width, model), lambda j, ids: (ids[1], 0, 0)),
                line,
                pl.BlockSpec((3, long, part), lambda j, ids: (0, 0, j)),
                pl.BlockSpec((1, 1, model, part), lambda j, ids: (j, 3, 0, 0)),
                pl.BlockSpec((1, LEAD, part), lambda j, ids: (j, 0, 0)),
            ],
            out_specs=[
                whole, whole, line, column, column,
                pl.BlockSpec((1, 8, part), lambda j, ids: (j, 0, 0)),
            ],
        ),
        out_shape=[
            jax.ShapeDtypeStruct((width, model), F32),
            jax.ShapeDtypeStruct((width, model), BF16),
            jax.ShapeDtypeStruct((1, model), F32),
            jax.ShapeDtypeStruct((width, model), BF16),
            jax.ShapeDtypeStruct((width, model), BF16),
            jax.ShapeDtypeStruct((count, 8, part), F32),
        ],
        compiler_params=pltpu.CompilerParams(vmem_limit_bytes=36 * MIB),
        cost_estimate=pl.CostEstimate(flops=0, bytes_accessed=0, transcendentals=0),
        name="mixer_backward",
    )(ids, *parts, own, cotangent, gain, gates, weights, taps)


def input_backward_kernel(
    ids, grad_convolved, edge, gates, grad_out_gate, taps, weights, grad_middle, tokens, gain,
    grad_first, grad_third, grad_tokens, gain_grad, total,
):
    block = pl.program_id(0)
    width = grad_convolved.shape[0]
    tap = taps[0].astype(F32)
    longer = jnp.concatenate([grad_convolved[...], edge[...]]).astype(F32)
    count = longer.shape[0]
    grad_product = (
        tap[0:1] * longer
        + tap[1:2] * pltpu.roll(longer, count - 1, 0)
        + tap[2:3] * pltpu.roll(longer, count - 2, 0)
    )[:width]
    first = (grad_product * gates[2, LEAD:, :].astype(F32)).astype(BF16)
    third = (grad_product * gates[0, LEAD:, :].astype(F32)).astype(BF16)
    grad_first[...] = first
    grad_third[...] = third
    here = (
        dot_nt(first, weights[0, 0])
        + dot_nt(grad_out_gate[...], weights[0, 1])
        + dot_nt(third, weights[0, 2])
    )

    @pl.when(block == 0)
    def _():
        total[...] = here

    @pl.when(block > 0)
    def _():
        total[...] += here

    @pl.when(block == pl.num_programs(0) - 1)
    def _():
        incoming = total[...]
        plain, inverse = norm_forward(tokens[0].astype(F32))
        gain_grad[...] = jnp.sum(incoming * plain, axis=0, keepdims=True)
        grad_tokens[...] = (
            grad_middle[...] + norm_backward(incoming, plain, inverse, gain[...].astype(F32))
        ).astype(BF16)


def input_backward(
    ids, grad_convolved, edge, gates, grad_out_gate, taps, weights, grad_middle, tokens, gain
):
    width, model = grad_middle.shape
    long = gates.shape[1]
    count, _, _, part = weights.shape
    whole = pl.BlockSpec((width, model), lambda j, ids: (0, 0))
    line = pl.BlockSpec((1, model), lambda j, ids: (0, 0))
    column = pl.BlockSpec((width, part), lambda j, ids: (0, j))
    return pl.pallas_call(
        input_backward_kernel,
        grid_spec=pltpu.PrefetchScalarGridSpec(
            num_scalar_prefetch=1,
            grid=(count,),
            in_specs=[
                column,
                pl.BlockSpec((edge.shape[0], part), lambda j, ids: (0, j)),
                pl.BlockSpec((3, long, part), lambda j, ids: (0, 0, j)),
                column,
                pl.BlockSpec((1, LEAD, part), lambda j, ids: (j, 0, 0)),
                pl.BlockSpec((1, 3, model, part), lambda j, ids: (j, 0, 0, 0)),
                whole,
                pl.BlockSpec((1, width, model), lambda j, ids: (ids[1], 0, 0)),
                line,
            ],
            out_specs=[column, column, whole, line],
            scratch_shapes=[pltpu.VMEM((width, model), F32)],
        ),
        out_shape=[
            jax.ShapeDtypeStruct((width, model), BF16),
            jax.ShapeDtypeStruct((width, model), BF16),
            jax.ShapeDtypeStruct((width, model), BF16),
            jax.ShapeDtypeStruct((1, model), F32),
        ],
        compiler_params=pltpu.CompilerParams(vmem_limit_bytes=44 * MIB),
        cost_estimate=pl.CostEstimate(flops=0, bytes_accessed=0, transcendentals=0),
        name="input_backward",
    )(ids, grad_convolved, edge, gates, grad_out_gate, taps, weights, grad_middle, tokens, gain)


def split_rows(ids, g):
    return ids[7 + g]


def feedforward_gradient_kernel(ids, left, right, send, keep):
    result = dot_tn(left[...], right[...]).astype(BF16)

    @pl.when(pl.program_id(0) < 2)
    def _():
        send[0] = result

    @pl.when(pl.program_id(0) >= 2)
    def _():
        keep[0] = result


def feedforward_gradient(ids, left, right):
    tokens, model = left.shape
    units = right.shape[1]
    part = model // 4
    shape = jax.ShapeDtypeStruct((2, part, units), BF16)
    return pl.pallas_call(
        feedforward_gradient_kernel,
        grid_spec=pltpu.PrefetchScalarGridSpec(
            num_scalar_prefetch=1,
            grid=(4,),
            in_specs=[
                pl.BlockSpec((tokens, part), lambda g, ids: (0, split_rows(ids, g))),
                pl.BlockSpec((tokens, units), lambda g, ids: (0, 0), pipeline_mode=pl.Buffered(1)),
            ],
            out_specs=[
                pl.BlockSpec((1, part, units), lambda g, ids: (jnp.minimum(g, 1), 0, 0)),
                pl.BlockSpec((1, part, units), lambda g, ids: (jnp.maximum(g - 2, 0), 0, 0)),
            ],
        ),
        out_shape=[shape, shape],
        compiler_params=pltpu.CompilerParams(vmem_limit_bytes=32 * MIB),
        cost_estimate=pl.CostEstimate(flops=0, bytes_accessed=0, transcendentals=0),
        name="feedforward_gradient",
    )(ids, left, right)


def mixer_gradient_kernel(ids, rows, mixed, first, second, third, gated, send, keep):
    part = mixed.shape[1]
    here = []
    for left, right in (
        (rows[0, LEAD:], first[...]),
        (rows[0, LEAD:], second[...]),
        (rows[0, LEAD:], third[...]),
        (mixed[...], gated[0]),
    ):
        here.append(dot_tn(left, right).astype(BF16))

    def store(out):
        for matrix, value in enumerate(here):
            for block in range(4):
                for upper in range(2):
                    out[0, ids[2] ^ upper, ids[11 + block], matrix] = value[
                        upper * part // 2 : (upper + 1) * part // 2, block * part : (block + 1) * part
                    ]

    @pl.when(pl.program_id(0) < 2)
    def _():
        store(send)

    @pl.when(pl.program_id(0) >= 2)
    def _():
        store(keep)


def mixer_gradient(ids, rows, mixed, first, second, third, gated):
    width, model = mixed.shape
    long = rows.shape[1]
    part = model // 4
    shape = jax.ShapeDtypeStruct((2, 2, 4, 4, part // 2, part), BF16)
    block = (1, 2, 4, 4, part // 2, part)
    whole = pl.BlockSpec((width, model), lambda g, ids: (0, 0))
    return pl.pallas_call(
        mixer_gradient_kernel,
        grid_spec=pltpu.PrefetchScalarGridSpec(
            num_scalar_prefetch=1,
            grid=(4,),
            in_specs=[
                pl.BlockSpec((1, long, part), lambda g, ids: (ids[1], 0, split_rows(ids, g))),
                pl.BlockSpec((width, part), lambda g, ids: (0, split_rows(ids, g))),
                whole, whole, whole,
                pl.BlockSpec((1, width, model), lambda g, ids: (ids[1], 0, 0)),
            ],
            out_specs=[
                pl.BlockSpec(block, lambda g, ids: (jnp.minimum(g, 1), 0, 0, 0, 0, 0)),
                pl.BlockSpec(block, lambda g, ids: (jnp.maximum(g - 2, 0), 0, 0, 0, 0, 0)),
            ],
        ),
        out_shape=[shape, shape],
        compiler_params=pltpu.CompilerParams(vmem_limit_bytes=40 * MIB),
        cost_estimate=pl.CostEstimate(flops=0, bytes_accessed=0, transcendentals=0),
        name="mixer_gradient",
    )(ids, rows, mixed, first, second, third, gated)


def local_by_links(
    tokens, norm_gain, w_in, conv_weight, convolution_out_weight, ffn_gain, w_gate, w_up, w_down, cotangent
):
    seqs, width, model = tokens.shape
    part = w_in.shape[1]
    units = w_gate.shape[1]
    shard, side, level = (lax.axis_index(name) for name in ("shard", "context", "tensor"))
    end = jnp.logical_or(level == 0, level == 3)
    order = [
        jnp.where(level < 2, 3, 0), jnp.where(level < 2, 2, 1), level ^ 1, level,
    ]
    place = [sum(jnp.where((level + block) % 4 == order[k], k, 0) for k in range(4)) for block in range(4)]
    ids = jnp.stack(
        [shard, level, side] + order + [shard ^ 1, shard ^ 3, shard, shard ^ 2] + place
    ).astype(jnp.int32)
    gain_one = norm_gain.reshape(1, model)
    gain_two = ffn_gain.reshape(1, model)
    def placed(own, others, dtype):
        out = jnp.zeros((seqs, width, model), dtype)
        for bits, block in enumerate((own,) + others):
            out = lax.dynamic_update_slice(out, block.astype(dtype)[None], (level ^ bits, 0, 0))
        return out

    taps_near = jnp.concatenate([conv_weight, jnp.zeros((LEAD - 3, part), BF16)])
    near = jnp.concatenate(
        [w_in[0], w_in[1], taps_near, w_in[2], convolution_out_weight.T, taps_near]
    )
    half = near.shape[0] // 2

    def sides(value):
        return [lax.dynamic_slice_in_dim(value, (side ^ bit) * half, half, 0) for bit in range(2)]

    near, near_side, near_else = together(near, *sides(near))
    far = to_y(near)
    near_right, near_left = shifted(near_side, -1), shifted(near_side, 1)
    edge = lax.ppermute(tokens[:, width - 2 :, :], "context", [(0, 1)])
    w_down = w_down.T
    feed = jnp.concatenate([w_gate, w_up, w_down])
    far, near_right, near_left, edge, feed, near_side, near_else, w_gate, w_up, w_down = together(
        far, near_right, near_left, edge, feed, near_side, near_else, w_gate, w_up, w_down
    )

    far_side, far_else = sides(far)
    far_right, far_left = shifted(far_side, -1), shifted(far_side, 1)
    near_over = to_x(jnp.concatenate([near_right, near_left]))
    far_gate = to_y(w_gate)
    mine = together(jnp.concatenate([near_side, near_else, far_side, far_else]))[0]
    other = to_core(mine)
    rows = jnp.concatenate([jnp.zeros((seqs, LEAD - 2, model), BF16), edge, tokens], axis=1).astype(F32)
    rows = (norm_forward(rows)[0] * gain_one.astype(F32)).astype(BF16)
    state = mixer_forward(ids, rows, (mine, other), 0, ())
    far_right, far_left, near_over, near_right, near_left, rows, feed, w_up, w_down, far_gate, *state = together(
        far_right, far_left, near_over, near_right, near_left, rows, feed, w_up, w_down, far_gate, *state
    )

    near_far, far_far = shifted(near_right, -1), shifted(far_left, 1)
    far_over = to_x(jnp.concatenate([far_right, far_left]))
    far_up = to_y(w_up)
    feed_core = to_core(feed)
    near_far, far_far, far_over, feed_core, far_up, w_down, *state = together(
        near_far, far_far, far_over, feed_core, far_up, w_down, *state
    )

    last_over = to_x(jnp.concatenate([near_far, far_far]))
    far_down = to_y(w_down)
    for block, rows_of, (a, b) in (
        (1, slice(None, half), (near_right, far_right)),
        (3, slice(half, None), (near_left, far_left)),
    ):
        mine = together(jnp.concatenate([a, near_over[rows_of], b, far_over[rows_of]]))[0]
        state = mixer_forward(ids, rows, (mine, to_core(mine)), block, state)
    last_over, far_down, far_gate, far_up, *state = together(
        last_over, far_down, far_gate, far_up, *state
    )

    mine = together(jnp.concatenate([near_far, last_over[:half], far_far, last_over[half:]]))[0]
    state = mixer_forward(ids, rows, (mine, to_core(mine)), 2, state)
    gated, weights, gates = state
    far_all = (far_gate, far_up, far_down)
    core_all = [to_core(value) for value in far_all]
    gated, weights, gates, *core_all = together(gated, weights, gates, *core_all)
    places = (feed, feed_core, *far_all, *core_all)
    taps = jnp.stack([near_side[2 * part :], near_right[2 * part :], near_far[2 * part :], near_left[2 * part :]])

    def forward(which, earlier):
        normed, down, grad, *wide = feedforward(
            ids, gated, weights, tokens, gain_two, cotangent, places, which, earlier
        )
        return down, grad, (normed, *wide[:3]), wide[3:]

    down0, grad0, done, _ = forward(0, ())
    down0, grad0, *done = together(down0, grad0, *done)

    grad_pair0 = pair(grad0)
    down1, grad1, done, _ = forward(1, tuple(done))
    grad_pair0, down1, grad1, *done = together(grad_pair0, down1, grad1, *done)

    grad_pair1 = pair(grad1)
    grad_over0 = across(added(grad0, grad_pair0))
    down2, grad2, done, _ = forward(2, tuple(done))
    grad_pair1, grad_over0, down2, grad2, *done = together(grad_pair1, grad_over0, down2, grad2, *done)

    grad_pair2 = pair(added(grad2, grad_over0))
    grad_over1 = across(added(grad1, grad_pair1))
    down3, grad3, done, (middle_own,) = forward(3, tuple(done))
    normed, hidden, grad_gate, grad_up = (v.reshape(seqs * width, v.shape[2]) for v in done)
    grad_pair2, grad_over1, grad3, normed, hidden, grad_gate, grad_up, down0 = together(
        grad_pair2, grad_over1, grad3, normed, hidden, grad_gate, grad_up, down0
    )

    down_pair0 = pair(down0)
    grad_middle, grad_mixed, gain_two_grad, grad_convolved, grad_out_gate, tap_grads = mixer_backward(
        ids, (grad3, grad_pair2, grad_over1), middle_own, cotangent, gain_two, gates, weights, taps
    )
    behind = lax.ppermute(grad_convolved[:LEAD], "context", [(1, 0)])
    grad_first, grad_third, tokens_own, gain_one_grad = input_backward(
        ids, grad_convolved, behind, gates, grad_out_gate, taps, weights, grad_middle, tokens, gain_one
    )
    (
        down_pair0, tokens_own, grad_first, grad_third, grad_mixed, gain_one_grad, normed, hidden, grad_gate, grad_up,
    ) = together(
        down_pair0, tokens_own, grad_first, grad_third, grad_mixed, gain_one_grad, normed, hidden, grad_gate, grad_up,
    )

    tokens_pair = pair(tokens_own)
    tokens_over = across(tokens_own)
    send_mixer, keep_mixer = mixer_gradient(
        ids, rows, grad_mixed, grad_first, grad_out_gate, grad_third, gated
    )
    send_down, keep_down = feedforward_gradient(ids, cotangent.reshape(seqs * width, model), hidden)
    down_sum0 = added(down0, down_pair0)
    tokens_pair, tokens_over, send_mixer, keep_mixer, send_down, keep_down, grad_gate, grad_up, down_sum0 = together(
        tokens_pair, tokens_over, send_mixer, keep_mixer, send_down, keep_down, grad_gate, grad_up, down_sum0
    )

    mixed_pair1 = pair(jnp.where(end, down1, tokens_over))
    tokens_over_end = across(tokens_pair)
    core_mixer = to_core(send_mixer)
    core_down = to_core(send_down)
    send_gate, keep_gate = feedforward_gradient(ids, normed, grad_gate)
    send_up, keep_up = feedforward_gradient(ids, normed, grad_up)
    tap_rows = tap_grads[:, :3].transpose(1, 0, 2)
    tap_rows = jnp.roll(tap_rows, level, axis=1).reshape(3, model)
    small = jnp.concatenate([gain_one_grad, gain_two_grad, tap_rows, jnp.zeros((3, model), F32)])
    small = small + to_core(small)
    mixed_pair1, tokens_over_end, core_mixer, core_down, send_gate, keep_gate, send_up, keep_up, small, down_sum0 = together(
        mixed_pair1, tokens_over_end, core_mixer, core_down, send_gate, keep_gate, send_up, keep_up, small, down_sum0
    )

    mixed_pair2 = pair(jnp.where(end, down2, tokens_over_end))
    down_over0 = across(down_sum0)
    y_mixer1 = to_y(added(keep_mixer[1, 1], core_mixer[1, 1]))
    core_gate, core_up = to_core(send_gate), to_core(send_up)
    small = small + to_x(small)
    down_sum1 = added(down1, mixed_pair1)
    mixed_pair2, down_over0, y_mixer1, core_gate, core_up, small, keep_mixer, down_sum1 = together(
        mixed_pair2, down_over0, y_mixer1, core_gate, core_up, small, keep_mixer, down_sum1
    )

    down_pair3 = pair(added(down2, down_over0))
    down_over1 = across(down_sum1)
    x_mixer = to_x(added(keep_mixer[0, 1], core_mixer[0, 1], y_mixer1))
    y_mixer0 = to_y(added(keep_mixer[1, 0], core_mixer[1, 0]))
    grad_tokens = placed(
        tokens_own,
        (
            tokens_pair,
            jnp.where(end, mixed_pair1, tokens_over_end),
            jnp.where(end, mixed_pair2, tokens_over),
        ),
        F32,
    )
    small = small + swapped(small, "tensor", 1)
    down_pair3, down_over1, x_mixer, y_mixer0, grad_tokens, keep_gate, keep_up, small = together(
        down_pair3, down_over1, x_mixer, y_mixer0, grad_tokens, keep_gate, keep_up, small
    )

    out_own = rounded(
        middle_own
        + down3.astype(F32)
        + jnp.where(end, down_pair3, mixed_pair2).astype(F32)
        + down_over1.astype(F32)
    )
    out_pair = pair(out_own)
    out_over = across(out_own)
    y_both = to_y(
        jnp.concatenate([added(keep_gate[1], core_gate[1]), added(keep_up[1], core_up[1])])
    )
    mixer = added(keep_mixer[0, 0], core_mixer[0, 0], y_mixer0, x_mixer)
    mixer_three = jnp.concatenate([mixer[:3].reshape(-1, model), jnp.zeros((width // 4, model), BF16)])
    small = small + swapped(small, "tensor", 2)
    out_pair, out_over, y_both, small, mixer, mixer_three = together(
        out_pair, out_over, y_both, small, mixer, mixer_three
    )

    out_over_end = across(out_pair)
    mixed_pair3 = pair(jnp.where(end, mixer_three, out_over))
    mine_both = rounded(
        added(
            jnp.concatenate([keep_gate[0], keep_up[0]]),
            jnp.concatenate([core_gate[0], core_up[0]]),
            y_both,
        )
    )
    x_both = to_x(mine_both)
    y_down = to_y(added(keep_down[1], core_down[1]))
    small = small + to_y(small)
    out_over_end, mixed_pair3, x_both, y_down, small = together(out_over_end, mixed_pair3, x_both, y_down, small)

    out_pair2 = pair(out_over_end)
    mixer_in = mixed_pair3[: 3 * width // 4].reshape(mixer[:3].shape)
    mixer_over = across(added(mixer[:2], mixer_in[:2]))
    mine_down = rounded(added(keep_down[0], core_down[0], y_down))
    total_down = (mine_down.astype(F32) + to_x(mine_down).astype(F32)).T
    total_both = mine_both.astype(F32) + x_both.astype(F32)
    total_gate, total_up = total_both[:part], total_both[part:]
    mixer_out = pair(added(mixer[2], mixer_over[0]))
    mine = rounded(
        mixer[3].astype(F32)
        + jnp.where(end, mixer_out, mixer_in[2]).astype(F32)
        + mixer_over[1].astype(F32)
    )
    other = to_x(mine)
    total = jnp.concatenate(
        [jnp.where(side == 0, mine, other), jnp.where(side == 0, other, mine)], axis=1
    ).astype(F32)
    total_taps = lax.dynamic_slice(small, (2, level * part), (3, part))
    block_out = placed(
        out_own,
        (out_pair, jnp.where(end, mixed_pair3, out_over_end), jnp.where(end, out_pair2, out_over)),
        BF16,
    )
    return (
        block_out, grad_tokens, small[0], total[:3], total_taps, total[3].T, small[1],
        total_gate, total_up, total_down,
    )


def from_behind(value, axis, steps):
    count = lax.axis_size(axis)
    initial, last = (max(0, -steps), min(count, count - steps))
    return lax.ppermute(value, axis, [(source, source + steps) for source in range(initial, last)])


def norm_backward_and_gain(grad_normed, plain, inverse, gain):
    grad_plain = grad_normed * gain
    grad_values = inverse * (
        grad_plain - plain * jnp.mean(grad_plain * plain, axis=-1, keepdims=True)
    )
    leading = tuple(range(grad_normed.ndim - 1))
    return (grad_values, jnp.sum(grad_normed * plain, axis=leading))


def local(
    tokens,
    norm_gain,
    w_in,
    conv_weight,
    convolution_out_weight,
    ffn_gain,
    w_gate,
    w_up,
    w_down,
    cotangent,
):
    input_rows = tokens.astype(jnp.float32)
    gain_one = norm_gain.astype(jnp.float32)
    gain_two = ffn_gain.astype(jnp.float32)
    taps = conv_weight.astype(jnp.float32)
    seqs, width, model = tokens.shape
    (
        complete_input_weight,
        complete_output_weight,
        feedforward_gate_weight,
        feedforward_up_weight,
        feedforward_down_weight,
    ) = (
        lax.all_gather(w_in, "shard", axis=1, tiled=True),
        lax.all_gather(convolution_out_weight, "shard", axis=1, tiled=True),
        lax.all_gather(w_gate, "shard", axis=0, tiled=True),
        lax.all_gather(w_up, "shard", axis=0, tiled=True),
        lax.all_gather(w_down, "shard", axis=1, tiled=True),
    )
    plain_one, inverse_one = norm_forward(input_rows)
    first_normalized = (plain_one * gain_one).astype(jnp.bfloat16)
    projection = jnp.einsum(
        "uiq,tqz->tuiz", first_normalized, complete_input_weight, preferred_element_type=jnp.float32
    )
    in_gate = projection[0]
    out_gate = projection[1]
    conv_input = projection[2]
    product = (in_gate * conv_input).astype(jnp.bfloat16)
    edge = from_behind(product[:, width - 2 :, :], "context", 1)
    extended = jnp.concatenate([edge, product], axis=1).astype(jnp.float32)
    recent = extended[:, 2:, :]
    previous = extended[:, 1 : width + 1, :]
    earlier = extended[:, :width, :]
    convolved = taps[0] * recent + taps[1] * previous + taps[2] * earlier
    gated_product = (out_gate * convolved).astype(jnp.bfloat16)
    partial_mixer_output = jnp.einsum(
        "zaw,wk->zak", gated_product, complete_output_weight, preferred_element_type=jnp.float32
    )
    residual_middle = input_rows + lax.psum(partial_mixer_output, "tensor")
    plain_two, inverse_two = norm_forward(residual_middle)
    second_normalized = (plain_two * gain_two).astype(jnp.bfloat16)
    gate_branch = jnp.einsum(
        "mut,tz->muz",
        second_normalized,
        feedforward_gate_weight,
        preferred_element_type=jnp.float32,
    )
    up_projection_branch = jnp.einsum(
        "mut,tz->muz", second_normalized, feedforward_up_weight, preferred_element_type=jnp.float32
    )
    sigmoid_gate = jax.nn.sigmoid(gate_branch)
    silu_gate = gate_branch * sigmoid_gate
    hidden_state = (silu_gate * up_projection_branch).astype(jnp.bfloat16)
    partial_feedforward = jnp.einsum(
        "eny,yv->env", hidden_state, feedforward_down_weight, preferred_element_type=jnp.float32
    )
    block_out = (
        residual_middle
        + lax.psum(partial_feedforward.astype(jnp.bfloat16), "tensor").astype(jnp.float32)
    ).astype(jnp.bfloat16)
    grad_out = cotangent.astype(jnp.float32)
    hidden_gradient = jnp.einsum(
        "qmn,pn->qmp", cotangent, feedforward_down_weight, preferred_element_type=jnp.float32
    )
    down_gradient = jnp.einsum(
        "eiu,eix->ux", hidden_state, cotangent, preferred_element_type=jnp.float32
    )
    gate_gradient = (
        hidden_gradient
        * up_projection_branch
        * sigmoid_gate
        * (1.0 + gate_branch * (1.0 - sigmoid_gate))
    ).astype(jnp.bfloat16)
    up_gradient = (hidden_gradient * silu_gate).astype(jnp.bfloat16)
    grad_w_gate = jnp.einsum(
        "rnj,rnt->jt", second_normalized, gate_gradient, preferred_element_type=jnp.float32
    )
    up_weight_gradient = jnp.einsum(
        "rnj,rnt->jt", second_normalized, up_gradient, preferred_element_type=jnp.float32
    )
    partial_normed_two = jnp.einsum(
        "wxo,qo->wxq", gate_gradient, feedforward_gate_weight, preferred_element_type=jnp.float32
    )
    partial_normed_two = partial_normed_two + jnp.einsum(
        "wxo,qo->wxq", up_gradient, feedforward_up_weight, preferred_element_type=jnp.float32
    )
    grad_normed_two = lax.psum(partial_normed_two, "tensor")
    grad_rows_two, gain_grad_two = norm_backward_and_gain(grad_normed_two, plain_two, inverse_two, gain_two)
    grad_middle = grad_out + grad_rows_two
    mixer_output_gradient = grad_middle.astype(jnp.bfloat16)
    grad_gated = jnp.einsum(
        "ymo,bo->ymb",
        mixer_output_gradient,
        complete_output_weight,
        preferred_element_type=jnp.float32,
    )
    out_weight_gradient = jnp.einsum(
        "miy,miq->yq", gated_product, mixer_output_gradient, preferred_element_type=jnp.float32
    )
    grad_convolved = (grad_gated * out_gate).astype(jnp.bfloat16)
    grad_out_gate = grad_gated * convolved
    grad_edge = from_behind(grad_convolved[:, :2, :], "context", -1)
    grad_extended = jnp.concatenate([grad_convolved, grad_edge], axis=1).astype(jnp.float32)
    grad_product = (
        taps[0] * grad_extended[:, :width, :]
        + taps[1] * grad_extended[:, 1 : width + 1, :]
        + taps[2] * grad_extended[:, 2:, :]
    )
    grad_local = grad_extended[:, :width, :]
    tap_grads = jnp.stack(
        [
            jnp.sum(grad_local * recent, axis=(0, 1)),
            jnp.sum(grad_local * previous, axis=(0, 1)),
            jnp.sum(grad_local * earlier, axis=(0, 1)),
        ]
    )
    projection_gradient = jnp.stack(
        [
            (grad_product * conv_input).astype(jnp.bfloat16),
            grad_out_gate.astype(jnp.bfloat16),
            (grad_product * in_gate).astype(jnp.bfloat16),
        ]
    )
    grad_w_in = jnp.einsum(
        "pxw,gpxt->gwt", first_normalized, projection_gradient, preferred_element_type=jnp.float32
    )
    partial_normed_one = jnp.einsum(
        "ireo,ivo->rev",
        projection_gradient,
        complete_input_weight,
        preferred_element_type=jnp.float32,
    )
    shard_in, shard_out, shard_gate, shard_up, shard_down = (
        lax.psum_scatter(
            grad_w_in.astype(jnp.bfloat16), "shard", scatter_dimension=1, tiled=True
        ).astype(jnp.float32),
        lax.psum_scatter(
            out_weight_gradient.astype(jnp.bfloat16), "shard", scatter_dimension=1, tiled=True
        ).astype(jnp.float32),
        lax.psum_scatter(
            grad_w_gate.astype(jnp.bfloat16), "shard", scatter_dimension=0, tiled=True
        ).astype(jnp.float32),
        lax.psum_scatter(
            up_weight_gradient.astype(jnp.bfloat16), "shard", scatter_dimension=0, tiled=True
        ).astype(jnp.float32),
        lax.psum_scatter(
            down_gradient.astype(jnp.bfloat16), "shard", scatter_dimension=1, tiled=True
        ).astype(jnp.float32),
    )
    total_in, total_out, total_gate, total_up, total_down = (
        lax.psum(shard_in.astype(jnp.bfloat16), "context").astype(jnp.float32),
        lax.psum(shard_out.astype(jnp.bfloat16), "context").astype(jnp.float32),
        lax.psum(shard_gate.astype(jnp.bfloat16), "context").astype(jnp.float32),
        lax.psum(shard_up.astype(jnp.bfloat16), "context").astype(jnp.float32),
        lax.psum(shard_down.astype(jnp.bfloat16), "context").astype(jnp.float32),
    )
    grad_normed_one = lax.psum(partial_normed_one.astype(jnp.bfloat16), "tensor").astype(
        jnp.float32
    )
    grad_rows_one, gain_grad_one = norm_backward_and_gain(grad_normed_one, plain_one, inverse_one, gain_one)
    grad_tokens = grad_middle + grad_rows_one
    total_gain_one, total_taps, total_gain_two = lax.psum(
        (gain_grad_one, tap_grads, gain_grad_two), ("shard", "context")
    )
    return (
        block_out,
        grad_tokens,
        total_gain_one,
        total_in,
        total_taps,
        total_out,
        total_gain_two,
        total_gate,
        total_up,
        total_down,
    )


def solution(mesh):
    in_specs = (
        P("shard", "context", None),
        P(),
        P(None, "shard", "tensor"),
        P(None, "tensor"),
        P("tensor", "shard"),
        P(),
        P("shard", "tensor"),
        P("shard", "tensor"),
        P("tensor", "shard"),
        P("shard", "context", None),
    )
    out_specs = (
        P("shard", "context", None),
        P("shard", "context", None),
        P(),
        P(None, "shard", "tensor"),
        P(None, "tensor"),
        P("tensor", "shard"),
        P(),
        P("shard", "tensor"),
        P("shard", "tensor"),
        P("tensor", "shard"),
    )
    sizes = mesh.shape
    by_links = (sizes["shard"], sizes["context"], sizes["tensor"]) == (4, 2, 4)
    body = local_by_links if by_links else local
    return jax.shard_map(body, mesh=mesh, in_specs=in_specs, out_specs=out_specs, check_vma=False)
```

```python
import functools

import jax
import jax.numpy as jnp
from jax import lax
from jax.experimental import pallas as pl
from jax.experimental.pallas import tpu as pltpu
from jax.sharding import PartitionSpec as P

EPSILON = 1e-05
F32 = jnp.float32
BF16 = jnp.bfloat16
MIB = 1024 * 1024
LEAD = 16


def norm_forward(values):
    inverse = lax.rsqrt(jnp.mean(values * values, axis=-1, keepdims=True) + EPSILON)
    return (values * inverse, inverse)


def norm_backward(grad_normed, plain, inverse, gain):
    grad_plain = grad_normed * gain
    return inverse * (
        grad_plain - plain * jnp.mean(grad_plain * plain, axis=-1, keepdims=True)
    )


def dot_nn(a, b):
    return lax.dot_general(a, b, (((1,), (0,)), ((), ())), preferred_element_type=F32)


def dot_nt(a, b):
    return lax.dot_general(a, b, (((1,), (1,)), ((), ())), preferred_element_type=F32)


def dot_tn(a, b):
    return lax.dot_general(a, b, (((0,), (0,)), ((), ())), preferred_element_type=F32)


def rounded(value):
    return lax.optimization_barrier(value.astype(BF16))


def shifted(value, steps):
    count = lax.axis_size("tensor")
    return lax.ppermute(value, "tensor", [(i, (i + steps) % count) for i in range(count)])


def swapped(value, axis, bit):
    count = lax.axis_size(axis)
    return lax.ppermute(value, axis, [(i, i ^ bit) for i in range(count)])


def to_core(value):
    return swapped(value, "shard", 1)


def to_y(value):
    return swapped(value, "shard", 2)


def to_x(value):
    return swapped(value, "context", 1)


def pair(value):
    return swapped(value, "tensor", 1)


def inward(value):
    return lax.ppermute(value, "tensor", [(0, 1), (3, 2)])


def outward(value):
    return lax.ppermute(value, "tensor", [(1, 0), (2, 3)])


def across(value):
    return lax.ppermute(value, "tensor", [(1, 2), (2, 1)])


def together(*values):
    return lax.optimization_barrier(values)


def added(*values):
    return sum(value.astype(F32) for value in values).astype(BF16)


def mixer_forward_kernel(ids, rows, mine, other, *rest):
    gated, weights, out_weights, own = rest[-4:]
    part = mine.shape[1]
    half = 2 * part + LEAD

    @pl.when(pl.program_id(0) == 0)
    def _():
        for bit, piece in enumerate((mine, other)):
            for far in range(2):
                start = pl.multiple_of((ids[0] ^ (bit + 2 * far)) * part, part)
                for side in range(2):
                    first = 2 * (ids[2] ^ side)
                    base = (2 * far + side) * half
                    lower = piece[base : base + part, :]
                    upper = piece[base + part : base + 2 * part, :]
                    weights[0, first, pl.ds(start, part), :] = lower

                    @pl.when(first == 0)
                    def _(start=start, upper=upper):
                        weights[0, 1, pl.ds(start, part), :] = upper

                    @pl.when(first == 2)
                    def _(start=start, upper=upper):
                        out_weights[0, pl.ds(start, part), :] = upper

    taps = mine[2 * part : half, :].astype(F32)
    values = rows[0]
    in_gate = dot_nn(values, weights[0, 0])
    conv_input = dot_nn(values, weights[0, 2])
    out_gate = dot_nn(values, weights[0, 1])
    product = (in_gate * conv_input).astype(BF16).astype(F32)
    convolved = (
        taps[0:1] * product
        + taps[1:2] * pltpu.roll(product, 1, 0)
        + taps[2:3] * pltpu.roll(product, 2, 0)
    )[LEAD:]
    gated[0] = (out_gate[LEAD:] * convolved).astype(BF16)

    @pl.when(pl.program_id(0) == ids[1])
    def _():
        own[0] = in_gate.astype(BF16)
        own[1] = out_gate.astype(BF16)
        own[2] = conv_input.astype(BF16)


def mixer_forward(ids, rows, pieces, block, earlier):
    seqs, long, model = rows.shape
    width = long - LEAD
    part = pieces[0].shape[1]
    count = model // part
    specs = [pl.BlockSpec((1, long, model), lambda q, ids: (q, 0, 0))]
    specs += [pl.BlockSpec(piece.shape, lambda q, ids: (0, 0)) for piece in pieces]
    specs += [pl.BlockSpec(memory_space=pl.ANY)] * len(earlier)
    return pl.pallas_call(
        mixer_forward_kernel,
        grid_spec=pltpu.PrefetchScalarGridSpec(
            num_scalar_prefetch=1,
            grid=(seqs,),
            in_specs=specs,
            out_specs=[
                pl.BlockSpec((1, width, part), lambda q, ids: (q, 0, block)),
                pl.BlockSpec((1, 3, model, part), lambda q, ids: (block, 0, 0, 0)),
                pl.BlockSpec((1, model, part), lambda q, ids: (block, 0, 0)),
                pl.BlockSpec((3, long, part), lambda q, ids: (0, 0, block)),
            ],
        ),
        out_shape=[
            jax.ShapeDtypeStruct((seqs, width, model), BF16),
            jax.ShapeDtypeStruct((count, 3, model, part), BF16),
            jax.ShapeDtypeStruct((count, model, part), BF16),
            jax.ShapeDtypeStruct((3, long, model), BF16),
        ],
        input_output_aliases={4: 0, 5: 1, 6: 2, 7: 3} if earlier else {},
        compiler_params=pltpu.CompilerParams(vmem_limit_bytes=24 * MIB),
        cost_estimate=pl.CostEstimate(flops=0, bytes_accessed=0, transcendentals=0),
        name="mixer_forward",
    )(ids, rows, *pieces, *earlier)


def feedforward_kernel(own, ids, gated, mixer, tokens, gain, cotangent, *rest):
    near, near_core, *rest = rest
    far, rest = rest[:6], rest[6:]
    outputs = rest[-8 - own : -2]
    weights, arrived = rest[-2:]
    normed, down, grad_normed, hidden, grad_gate, grad_up = outputs[:6]
    part = far[0].shape[0]
    count = mixer.shape[0]
    channels = mixer.shape[2]
    first = pl.program_id(0) == 0

    def copies(which):
        rows = pl.ds(which * part, part)
        sources = (near.at[rows, :], near_core.at[rows, :], far[which], far[3 + which])
        for place, source in enumerate(sources):
            start = pl.multiple_of((ids[0] ^ place) * part, part)
            yield pltpu.make_async_copy(
                source,
                weights.at[which, pl.ds(start, part), :],
                arrived.at[which, place],
            )

    @pl.when(first)
    def _():
        for which in range(3):
            for copy in copies(which):
                copy.start()

    middle = tokens[0].astype(F32)
    for block in range(count):
        middle += dot_nt(gated[0, :, block * channels : (block + 1) * channels], mixer[block])
    if own:
        rest[-3][...] = middle
    values = (norm_forward(middle)[0] * gain[...].astype(F32)).astype(BF16)
    normed[0] = values

    @pl.when(first)
    def _():
        for which in range(3):
            for copy in copies(which):
                copy.wait()

    gate = dot_nn(values, weights[0])
    up = dot_nn(values, weights[1])
    grad_hidden = dot_nn(cotangent[0], weights[2])
    sigmoid = jax.nn.sigmoid(gate)
    silu = gate * sigmoid
    hidden_now = (silu * up).astype(BF16)
    hidden[0] = hidden_now
    gate_now = (grad_hidden * up * sigmoid * (1.0 + gate * (1.0 - sigmoid))).astype(BF16)
    up_now = (grad_hidden * silu).astype(BF16)
    grad_gate[0] = gate_now
    grad_up[0] = up_now
    grad_normed[...] = (dot_nt(gate_now, weights[0]) + dot_nt(up_now, weights[1])).astype(BF16)
    down[...] = dot_nt(hidden_now, weights[2]).astype(BF16)


def feedforward(ids, gated, mixer, tokens, gain, cotangent, places, which, earlier):
    seqs, width, model = tokens.shape
    units = places[0].shape[1]
    count, _, channels = mixer.shape
    size = width // 2
    own = int(which == 3)

    def seq(i, ids):
        return (ids[3 + which], i, 0)

    def row(i, ids):
        return (i, 0)

    wide = jax.ShapeDtypeStruct((seqs, width, units), BF16)
    here = jax.ShapeDtypeStruct((width, model), BF16)
    first = 6 + len(places)
    return pl.pallas_call(
        functools.partial(feedforward_kernel, own),
        grid_spec=pltpu.PrefetchScalarGridSpec(
            num_scalar_prefetch=1,
            grid=(2,),
            in_specs=[
                pl.BlockSpec((1, size, model), seq),
                pl.BlockSpec((count, model, channels), lambda i, ids: (0, 0, 0), pipeline_mode=pl.Buffered(1)),
                pl.BlockSpec((1, size, model), seq),
                pl.BlockSpec((1, model), lambda i, ids: (0, 0)),
                pl.BlockSpec((1, size, model), seq),
            ]
            + [pl.BlockSpec(memory_space=pltpu.HBM)] * len(places)
            + [pl.BlockSpec(memory_space=pl.ANY)] * len(earlier),
            out_specs=[
                pl.BlockSpec((1, size, model), seq),
                pl.BlockSpec((size, model), row),
                pl.BlockSpec((size, model), row),
                pl.BlockSpec((1, size, units), seq),
                pl.BlockSpec((1, size, units), seq),
                pl.BlockSpec((1, size, units), seq),
            ]
            + [pl.BlockSpec((size, model), row)] * own,
            scratch_shapes=[
                pltpu.VMEM((3, model, units), BF16),
                pltpu.SemaphoreType.DMA((3, 4)),
            ],
        ),
        out_shape=[
            jax.ShapeDtypeStruct(tokens.shape, BF16),
            here,
            here,
            wide,
            wide,
            wide,
        ]
        + [jax.ShapeDtypeStruct((width, model), F32)] * own,
        input_output_aliases={first: 0, first + 1: 3, first + 2: 4, first + 3: 5} if earlier else {},
        compiler_params=pltpu.CompilerParams(vmem_limit_bytes=40 * MIB),
        cost_estimate=pl.CostEstimate(flops=0, bytes_accessed=0, transcendentals=0),
        name="feedforward",
    )(ids, gated, mixer, tokens, gain, cotangent, *places, *earlier)


def middle_gradient(parts, own, cotangent, gain):
    incoming = sum(part[...].astype(F32) for part in parts)
    plain, inverse = norm_forward(own[...])
    total = cotangent[0].astype(F32) + norm_backward(incoming, plain, inverse, gain[...].astype(F32))
    return total, jnp.sum(incoming * plain, axis=0, keepdims=True)


def edge_kernel(ids, part0, part1, part2, own, cotangent, gain, gate, out_weights, edge):
    mixed = middle_gradient((part0, part1, part2), own, cotangent, gain)[0].astype(BF16)
    count, _, part = out_weights.shape
    for block in range(count):
        columns = slice(block * part, (block + 1) * part)
        grad_gated = dot_nn(mixed, out_weights[block])
        edge[:, columns] = (grad_gated * gate[0, :, columns].astype(F32)).astype(BF16)


def edge_gradient(ids, parts, own, cotangent, gain, gates, out_weights):
    width, model = own.shape
    rows = pl.BlockSpec((LEAD, model), lambda i, ids: (0, 0))
    return pl.pallas_call(
        edge_kernel,
        grid_spec=pltpu.PrefetchScalarGridSpec(
            num_scalar_prefetch=1,
            grid=(1,),
            in_specs=[
                rows, rows, rows, rows,
                pl.BlockSpec((1, LEAD, model), lambda i, ids: (ids[1], 0, 0)),
                pl.BlockSpec((1, model), lambda i, ids: (0, 0)),
                pl.BlockSpec((1, LEAD, model), lambda i, ids: (1, 1, 0)),
                pl.BlockSpec(out_weights.shape, lambda i, ids: (0, 0, 0)),
            ],
            out_specs=rows,
        ),
        out_shape=jax.ShapeDtypeStruct((LEAD, model), BF16),
        compiler_params=pltpu.CompilerParams(vmem_limit_bytes=60 * MIB),
        cost_estimate=pl.CostEstimate(flops=0, bytes_accessed=0, transcendentals=0),
        name="edge_gradient",
    )(ids, *parts, own, cotangent, gain, gates, out_weights)


def mixer_backward_kernel(
    ids, part0, part1, part2, own, cotangent, gain_two, gates, edge, weights, out_weights, taps, tokens, gain_one,
    grad_mixed, gain_two_grad, grad_first, grad_out_gate, grad_third, tap_grads, grad_tokens, gain_one_grad,
    grad_middle, total,
):
    block = pl.program_id(0)
    width = grad_mixed.shape[0]

    @pl.when(block == 0)
    def _():
        here, gain_grad = middle_gradient((part0, part1, part2), own, cotangent, gain_two)
        gain_two_grad[...] = gain_grad
        grad_middle[...] = here
        grad_mixed[...] = here.astype(BF16)
        total[...] = jnp.zeros_like(total)

    tap = taps[0].astype(F32)
    in_gate = gates[0].astype(F32)
    conv_input = gates[2].astype(F32)
    product = (in_gate * conv_input).astype(BF16).astype(F32)
    recent, previous, earlier = (
        product[LEAD:], pltpu.roll(product, 1, 0)[LEAD:], pltpu.roll(product, 2, 0)[LEAD:],
    )
    convolved = tap[0:1] * recent + tap[1:2] * previous + tap[2:3] * earlier
    grad_gated = dot_nn(grad_mixed[...], out_weights[0])
    second = (grad_gated * convolved).astype(BF16)
    grad_out_gate[...] = second
    low = (grad_gated * gates[1, LEAD:, :].astype(F32)).astype(BF16).astype(F32)
    tap_grads[0] = jnp.concatenate(
        [
            jnp.sum(low * recent, axis=0, keepdims=True),
            jnp.sum(low * previous, axis=0, keepdims=True),
            jnp.sum(low * earlier, axis=0, keepdims=True),
            jnp.zeros((5, low.shape[1]), F32),
        ]
    )
    longer = jnp.concatenate([low, edge[...].astype(F32)])
    count = longer.shape[0]
    grad_product = (
        tap[0:1] * longer
        + tap[1:2] * pltpu.roll(longer, count - 1, 0)
        + tap[2:3] * pltpu.roll(longer, count - 2, 0)
    )[:width]
    first = (grad_product * conv_input[LEAD:]).astype(BF16)
    third = (grad_product * in_gate[LEAD:]).astype(BF16)
    grad_first[...] = first
    grad_third[...] = third
    total[...] += (
        dot_nt(first, weights[0, 0]) + dot_nt(second, weights[0, 1]) + dot_nt(third, weights[0, 2])
    )

    @pl.when(block == pl.num_programs(0) - 1)
    def _():
        incoming = total[...]
        plain, inverse = norm_forward(tokens[0].astype(F32))
        gain_one_grad[...] = jnp.sum(incoming * plain, axis=0, keepdims=True)
        grad_tokens[...] = (
            grad_middle[...] + norm_backward(incoming, plain, inverse, gain_one[...].astype(F32))
        ).astype(BF16)


def mixer_backward(
    ids, parts, own, cotangent, gain_two, gates, edge, weights, out_weights, taps, tokens, gain_one
):
    width, model = own.shape
    long = gates.shape[1]
    count, _, _, part = weights.shape
    whole = pl.BlockSpec((width, model), lambda j, ids: (0, 0))
    once = pl.BlockSpec((width, model), lambda j, ids: (0, 0), pipeline_mode=pl.Buffered(1))
    mine = pl.BlockSpec((1, width, model), lambda j, ids: (ids[1], 0, 0), pipeline_mode=pl.Buffered(1))
    line = pl.BlockSpec((1, model), lambda j, ids: (0, 0))
    column = pl.BlockSpec((width, part), lambda j, ids: (0, j))
    lines = jax.ShapeDtypeStruct((1, model), F32)
    matrix = jax.ShapeDtypeStruct((width, model), BF16)
    return pl.pallas_call(
        mixer_backward_kernel,
        grid_spec=pltpu.PrefetchScalarGridSpec(
            num_scalar_prefetch=1,
            grid=(count,),
            in_specs=[
                once, once, once, once, mine, line,
                pl.BlockSpec((3, long, part), lambda j, ids: (0, 0, j)),
                pl.BlockSpec((LEAD, part), lambda j, ids: (0, j)),
                pl.BlockSpec((1, 3, model, part), lambda j, ids: (j, 0, 0, 0)),
                pl.BlockSpec((1, model, part), lambda j, ids: (j, 0, 0)),
                pl.BlockSpec((1, LEAD, part), lambda j, ids: (j, 0, 0)),
                mine, line,
            ],
            out_specs=[
                whole, line, column, column, column,
                pl.BlockSpec((1, 8, part), lambda j, ids: (j, 0, 0)),
                whole, line,
            ],
            scratch_shapes=[pltpu.VMEM((width, model), F32), pltpu.VMEM((width, model), F32)],
        ),
        out_shape=[
            matrix, lines, matrix, matrix, matrix,
            jax.ShapeDtypeStruct((count, 8, part), F32),
            matrix, lines,
        ],
        compiler_params=pltpu.CompilerParams(vmem_limit_bytes=60 * MIB),
        cost_estimate=pl.CostEstimate(flops=0, bytes_accessed=0, transcendentals=0),
        name="mixer_backward",
    )(ids, *parts, own, cotangent, gain_two, gates, edge, weights, out_weights, taps, tokens, gain_one)


def split_rows(ids, g):
    return ids[7 + g]


def feedforward_gradient_kernel(ids, left, right, send, keep):
    result = dot_tn(left[...], right[...]).astype(BF16)

    @pl.when(pl.program_id(0) < 2)
    def _():
        send[0] = result

    @pl.when(pl.program_id(0) >= 2)
    def _():
        keep[0] = result


def feedforward_gradient(ids, left, right):
    tokens, model = left.shape
    units = right.shape[1]
    part = model // 4
    shape = jax.ShapeDtypeStruct((2, part, units), BF16)
    return pl.pallas_call(
        feedforward_gradient_kernel,
        grid_spec=pltpu.PrefetchScalarGridSpec(
            num_scalar_prefetch=1,
            grid=(4,),
            in_specs=[
                pl.BlockSpec((tokens, part), lambda g, ids: (0, split_rows(ids, g))),
                pl.BlockSpec((tokens, units), lambda g, ids: (0, 0), pipeline_mode=pl.Buffered(1)),
            ],
            out_specs=[
                pl.BlockSpec((1, part, units), lambda g, ids: (jnp.minimum(g, 1), 0, 0)),
                pl.BlockSpec((1, part, units), lambda g, ids: (jnp.maximum(g - 2, 0), 0, 0)),
            ],
        ),
        out_shape=[shape, shape],
        compiler_params=pltpu.CompilerParams(vmem_limit_bytes=32 * MIB),
        cost_estimate=pl.CostEstimate(flops=0, bytes_accessed=0, transcendentals=0),
        name="feedforward_gradient",
    )(ids, left, right)


def mixer_gradient_kernel(ids, rows, mixed, first, second, third, gated, send, keep):
    part = mixed.shape[1]
    here = []
    for left, right in (
        (rows[0, LEAD:], first[...]),
        (rows[0, LEAD:], second[...]),
        (rows[0, LEAD:], third[...]),
        (mixed[...], gated[0]),
    ):
        here.append(dot_tn(left, right).astype(BF16))

    def store(out):
        for matrix, value in enumerate(here):
            for block in range(4):
                for upper in range(2):
                    out[0, ids[2] ^ upper, ids[11 + block], matrix] = value[
                        upper * part // 2 : (upper + 1) * part // 2, block * part : (block + 1) * part
                    ]

    @pl.when(pl.program_id(0) < 2)
    def _():
        store(send)

    @pl.when(pl.program_id(0) >= 2)
    def _():
        store(keep)


def mixer_gradient(ids, rows, mixed, first, second, third, gated):
    width, model = mixed.shape
    long = rows.shape[1]
    part = model // 4
    shape = jax.ShapeDtypeStruct((2, 2, 4, 4, part // 2, part), BF16)
    block = (1, 2, 4, 4, part // 2, part)
    whole = pl.BlockSpec((width, model), lambda g, ids: (0, 0))
    return pl.pallas_call(
        mixer_gradient_kernel,
        grid_spec=pltpu.PrefetchScalarGridSpec(
            num_scalar_prefetch=1,
            grid=(4,),
            in_specs=[
                pl.BlockSpec((1, long, part), lambda g, ids: (ids[1], 0, split_rows(ids, g))),
                pl.BlockSpec((width, part), lambda g, ids: (0, split_rows(ids, g))),
                whole, whole, whole,
                pl.BlockSpec((1, width, model), lambda g, ids: (ids[1], 0, 0)),
            ],
            out_specs=[
                pl.BlockSpec(block, lambda g, ids: (jnp.minimum(g, 1), 0, 0, 0, 0, 0)),
                pl.BlockSpec(block, lambda g, ids: (jnp.maximum(g - 2, 0), 0, 0, 0, 0, 0)),
            ],
        ),
        out_shape=[shape, shape],
        compiler_params=pltpu.CompilerParams(vmem_limit_bytes=40 * MIB),
        cost_estimate=pl.CostEstimate(flops=0, bytes_accessed=0, transcendentals=0),
        name="mixer_gradient",
    )(ids, rows, mixed, first, second, third, gated)


def local_by_links(
    tokens, norm_gain, w_in, conv_weight, convolution_out_weight, ffn_gain, w_gate, w_up, w_down, cotangent
):
    seqs, width, model = tokens.shape
    part = w_in.shape[1]
    units = w_gate.shape[1]
    shard, side, level = (lax.axis_index(name) for name in ("shard", "context", "tensor"))
    end = jnp.logical_or(level == 0, level == 3)
    order = [
        jnp.where(level < 2, 3, 0), jnp.where(level < 2, 2, 1), level ^ 1, level,
    ]
    place = [sum(jnp.where((level + block) % 4 == order[k], k, 0) for k in range(4)) for block in range(4)]
    ids = jnp.stack(
        [shard, level, side] + order + [shard ^ 1, shard ^ 3, shard, shard ^ 2] + place
    ).astype(jnp.int32)
    gain_one = norm_gain.reshape(1, model)
    gain_two = ffn_gain.reshape(1, model)
    def placed(own, others, dtype):
        out = jnp.zeros((seqs, width, model), dtype)
        for bits, block in enumerate((own,) + others):
            out = lax.dynamic_update_slice(out, block.astype(dtype)[None], (level ^ bits, 0, 0))
        return out

    taps_near = jnp.concatenate([conv_weight, jnp.zeros((LEAD - 3, part), BF16)])
    near = jnp.concatenate(
        [w_in[0], w_in[1], taps_near, w_in[2], convolution_out_weight.T, taps_near]
    )
    half = near.shape[0] // 2

    def sides(value):
        return [lax.dynamic_slice_in_dim(value, (side ^ bit) * half, half, 0) for bit in range(2)]

    near, near_side, near_else = together(near, *sides(near))
    far = to_y(near)
    near_right, near_left = shifted(near_side, -1), shifted(near_side, 1)
    edge = lax.ppermute(tokens[:, width - 2 :, :], "context", [(0, 1)])
    w_down = w_down.T
    feed = jnp.concatenate([w_gate, w_up, w_down])
    far, near_right, near_left, edge, feed, near_side, near_else, w_gate, w_up, w_down = together(
        far, near_right, near_left, edge, feed, near_side, near_else, w_gate, w_up, w_down
    )

    far_side, far_else = sides(far)
    far_right, far_left = shifted(far_side, -1), shifted(far_side, 1)
    near_over = to_x(jnp.concatenate([near_right, near_left]))
    far_gate = to_y(w_gate)
    mine = together(jnp.concatenate([near_side, near_else, far_side, far_else]))[0]
    other = to_core(mine)
    rows = jnp.concatenate([jnp.zeros((seqs, LEAD - 2, model), BF16), edge, tokens], axis=1).astype(F32)
    rows = (norm_forward(rows)[0] * gain_one.astype(F32)).astype(BF16)
    state = mixer_forward(ids, rows, (mine, other), 0, ())
    far_right, far_left, near_over, near_right, near_left, rows, feed, w_up, w_down, far_gate, *state = together(
        far_right, far_left, near_over, near_right, near_left, rows, feed, w_up, w_down, far_gate, *state
    )

    near_far, far_far = shifted(near_right, -1), shifted(far_left, 1)
    far_over = to_x(jnp.concatenate([far_right, far_left]))
    far_up = to_y(w_up)
    feed_core = to_core(feed)
    near_far, far_far, far_over, feed_core, far_up, w_down, *state = together(
        near_far, far_far, far_over, feed_core, far_up, w_down, *state
    )

    last_over = to_x(jnp.concatenate([near_far, far_far]))
    far_down = to_y(w_down)
    for block, rows_of, (a, b) in (
        (1, slice(None, half), (near_right, far_right)),
        (3, slice(half, None), (near_left, far_left)),
    ):
        mine = together(jnp.concatenate([a, near_over[rows_of], b, far_over[rows_of]]))[0]
        state = mixer_forward(ids, rows, (mine, to_core(mine)), block, state)
    last_over, far_down, far_gate, far_up, *state = together(
        last_over, far_down, far_gate, far_up, *state
    )

    mine = together(jnp.concatenate([near_far, last_over[:half], far_far, last_over[half:]]))[0]
    state = mixer_forward(ids, rows, (mine, to_core(mine)), 2, state)
    gated, weights, out_weights, gates = state
    far_all = (far_gate, far_up, far_down)
    core_all = [to_core(value) for value in far_all]
    gated, weights, out_weights, gates, *core_all = together(gated, weights, out_weights, gates, *core_all)
    places = (feed, feed_core, *far_all, *core_all)
    taps = jnp.stack([near_side[2 * part :], near_right[2 * part :], near_far[2 * part :], near_left[2 * part :]])

    def forward(which, earlier):
        normed, down, grad, *wide = feedforward(
            ids, gated, out_weights, tokens, gain_two, cotangent, places, which, earlier
        )
        return down, grad, (normed, *wide[:3]), wide[3:]

    down0, grad0, done, _ = forward(0, ())
    down0, grad0, *done = together(down0, grad0, *done)

    grad_pair0 = pair(grad0)
    down1, grad1, done, _ = forward(1, tuple(done))
    grad_pair0, down1, grad1, *done = together(grad_pair0, down1, grad1, *done)

    grad_pair1 = pair(grad1)
    grad_over0 = across(added(grad0, grad_pair0))
    down2, grad2, done, _ = forward(2, tuple(done))
    grad_pair1, grad_over0, down2, grad2, *done = together(grad_pair1, grad_over0, down2, grad2, *done)

    grad_pair2 = pair(added(grad2, grad_over0))
    grad_over1 = across(added(grad1, grad_pair1))
    down3, grad3, done, (middle_own,) = forward(3, tuple(done))
    normed, hidden, grad_gate, grad_up = (v.reshape(seqs * width, v.shape[2]) for v in done)
    grad_pair2, grad_over1, grad3, normed, hidden, grad_gate, grad_up, down0 = together(
        grad_pair2, grad_over1, grad3, normed, hidden, grad_gate, grad_up, down0
    )

    down_pair0 = pair(down0)
    grad_parts = (grad3, grad_pair2, grad_over1)
    edge = edge_gradient(ids, grad_parts, middle_own, cotangent, gain_two, gates, out_weights)
    edge = lax.ppermute(edge, "context", [(1, 0)])
    (
        grad_mixed, gain_two_grad, grad_first, grad_out_gate, grad_third, tap_grads, tokens_own, gain_one_grad,
    ) = mixer_backward(
        ids, grad_parts, middle_own, cotangent, gain_two, gates, edge, weights, out_weights, taps, tokens, gain_one
    )
    (
        down_pair0, tokens_own, grad_first, grad_third, grad_mixed, gain_one_grad, normed, hidden, grad_gate, grad_up,
    ) = together(
        down_pair0, tokens_own, grad_first, grad_third, grad_mixed, gain_one_grad, normed, hidden, grad_gate, grad_up,
    )

    tokens_pair = pair(tokens_own)
    tokens_over = across(tokens_own)
    send_mixer, keep_mixer = mixer_gradient(
        ids, rows, grad_mixed, grad_first, grad_out_gate, grad_third, gated
    )
    send_down, keep_down = feedforward_gradient(ids, cotangent.reshape(seqs * width, model), hidden)
    tap_rows = tap_grads[:, :3].transpose(1, 0, 2)
    tap_rows = jnp.roll(tap_rows, level, axis=1).reshape(3, model)
    small = jnp.concatenate([gain_one_grad, gain_two_grad, tap_rows, jnp.zeros((3, model), F32)])
    small = small + swapped(small, "tensor", 1)
    tokens_pair, tokens_over, send_mixer, keep_mixer, send_down, keep_down, grad_gate, grad_up, small, down0 = together(
        tokens_pair, tokens_over, send_mixer, keep_mixer, send_down, keep_down, grad_gate, grad_up, small, down0
    )

    mixed_pair1 = pair(jnp.where(end, down1, tokens_over))
    tokens_over_end = across(tokens_pair)
    core_mixer = to_core(send_mixer)
    core_down = to_core(send_down)
    send_gate, keep_gate = feedforward_gradient(ids, normed, grad_gate)
    send_up, keep_up = feedforward_gradient(ids, normed, grad_up)
    small = small + swapped(small, "tensor", 2)
    down_sum0 = added(down0, down_pair0)
    mixed_pair1, tokens_over_end, core_mixer, core_down, send_gate, keep_gate, send_up, keep_up, small, down_sum0 = together(
        mixed_pair1, tokens_over_end, core_mixer, core_down, send_gate, keep_gate, send_up, keep_up, small, down_sum0
    )

    mixed_pair2 = pair(jnp.where(end, down2, tokens_over_end))
    down_over0 = across(down_sum0)
    core_gate = to_core(send_gate)
    small = small + to_x(small)
    sum_down = added(keep_down, core_down)
    y_down = to_y(sum_down[1])
    sum_mixer = added(keep_mixer, core_mixer)
    low, high = slice(None, part // 4), slice(part // 4, None)
    here_low, send_low = sum_mixer[0, :, :, :, low], sum_mixer[1, :, :, :, low]
    here_high, send_high = sum_mixer[:, 0, :, :, high], sum_mixer[:, 1, :, :, high]
    down_sum1 = added(down1, mixed_pair1)
    (
        mixed_pair2, down_over0, core_gate, send_up, y_down, here_low, send_low, here_high, send_high, down_sum1,
        small, tokens_own,
    ) = together(
        mixed_pair2, down_over0, core_gate, send_up, y_down, here_low, send_low, here_high, send_high, down_sum1,
        small, tokens_own,
    )

    down_pair3 = pair(added(down2, down_over0))
    down_over1 = across(down_sum1)
    y_low, x_high = to_y(send_low), to_x(send_high)
    grad_tokens = placed(
        tokens_own,
        (
            tokens_pair,
            jnp.where(end, mixed_pair1, tokens_over_end),
            jnp.where(end, mixed_pair2, tokens_over),
        ),
        F32,
    )
    mine_down = rounded(added(sum_down[0], y_down))
    sum_gate = added(keep_gate, core_gate)
    core_up = to_core(send_up)
    down_pair3, down_over1, y_low, x_high, grad_tokens, mine_down, sum_gate, core_up, small = together(
        down_pair3, down_over1, y_low, x_high, grad_tokens, mine_down, sum_gate, core_up, small
    )

    out_own = rounded(
        middle_own
        + down3.astype(F32)
        + jnp.where(end, down_pair3, mixed_pair2).astype(F32)
        + down_over1.astype(F32)
    )
    out_pair = pair(out_own)
    out_over = across(out_own)
    half_low = added(here_low, y_low)
    half_high = added(here_high, x_high)
    x_low, y_high = to_x(half_low[1]), to_y(half_high[1])
    mixer = jnp.concatenate([added(half_low[0], x_low), added(half_high[0], y_high)], axis=2)
    sum_up = added(keep_up, core_up)
    send_both = jnp.concatenate([sum_gate[1], sum_up[1]])
    here_both = jnp.concatenate([sum_gate[0], sum_up[0]])
    small = small + to_core(small)
    out_pair, out_over, mixer, send_both, here_both, mine_down, small = together(
        out_pair, out_over, mixer, send_both, here_both, mine_down, small
    )

    out_over_end = across(out_pair)
    out_out2 = outward(out_over)
    mixer_in = inward(mixer[:3])
    y_both = to_y(send_both)
    x_down = to_x(mine_down)
    total_down = (mine_down.astype(F32) + x_down.astype(F32)).T
    out_over_end, out_out2, mixer_in, y_both, total_down, small = together(
        out_over_end, out_out2, mixer_in, y_both, total_down, small
    )

    out_out3 = outward(out_over_end)
    mixer_over = across(added(mixer[:2], mixer_in[:2]))
    small = small + to_y(small)
    mixer_out = outward(added(mixer[2], mixer_over[0]))
    mine_both = rounded(added(here_both, y_both))
    total_both = mine_both.astype(F32) + to_x(mine_both).astype(F32)
    total_gate, total_up = total_both[:part], total_both[part:]
    mine = rounded(
        sum(value.astype(F32) for value in (mixer[3], mixer_out, mixer_in[2], mixer_over[1]))
    )
    other = to_x(mine)
    total = jnp.concatenate(
        [jnp.where(side == 0, mine, other), jnp.where(side == 0, other, mine)], axis=1
    ).astype(F32)
    total_taps = lax.dynamic_slice(small, (2, level * part), (3, part))
    block_out = placed(
        out_own,
        (out_pair, jnp.where(end, out_out2, out_over_end), jnp.where(end, out_out3, out_over)),
        BF16,
    )
    return (
        block_out, grad_tokens, small[0], total[:3], total_taps, total[3].T, small[1],
        total_gate, total_up, total_down,
    )


def from_behind(value, axis, steps):
    count = lax.axis_size(axis)
    initial, last = (max(0, -steps), min(count, count - steps))
    return lax.ppermute(value, axis, [(source, source + steps) for source in range(initial, last)])


def norm_backward_and_gain(grad_normed, plain, inverse, gain):
    grad_plain = grad_normed * gain
    grad_values = inverse * (
        grad_plain - plain * jnp.mean(grad_plain * plain, axis=-1, keepdims=True)
    )
    leading = tuple(range(grad_normed.ndim - 1))
    return (grad_values, jnp.sum(grad_normed * plain, axis=leading))


def local(
    tokens,
    norm_gain,
    w_in,
    conv_weight,
    convolution_out_weight,
    ffn_gain,
    w_gate,
    w_up,
    w_down,
    cotangent,
):
    input_rows = tokens.astype(jnp.float32)
    gain_one = norm_gain.astype(jnp.float32)
    gain_two = ffn_gain.astype(jnp.float32)
    taps = conv_weight.astype(jnp.float32)
    seqs, width, model = tokens.shape
    (
        complete_input_weight,
        complete_output_weight,
        feedforward_gate_weight,
        feedforward_up_weight,
        feedforward_down_weight,
    ) = (
        lax.all_gather(w_in, "shard", axis=1, tiled=True),
        lax.all_gather(convolution_out_weight, "shard", axis=1, tiled=True),
        lax.all_gather(w_gate, "shard", axis=0, tiled=True),
        lax.all_gather(w_up, "shard", axis=0, tiled=True),
        lax.all_gather(w_down, "shard", axis=1, tiled=True),
    )
    plain_one, inverse_one = norm_forward(input_rows)
    first_normalized = (plain_one * gain_one).astype(jnp.bfloat16)
    projection = jnp.einsum(
        "uiq,tqz->tuiz", first_normalized, complete_input_weight, preferred_element_type=jnp.float32
    )
    in_gate = projection[0]
    out_gate = projection[1]
    conv_input = projection[2]
    product = (in_gate * conv_input).astype(jnp.bfloat16)
    edge = from_behind(product[:, width - 2 :, :], "context", 1)
    extended = jnp.concatenate([edge, product], axis=1).astype(jnp.float32)
    recent = extended[:, 2:, :]
    previous = extended[:, 1 : width + 1, :]
    earlier = extended[:, :width, :]
    convolved = taps[0] * recent + taps[1] * previous + taps[2] * earlier
    gated_product = (out_gate * convolved).astype(jnp.bfloat16)
    partial_mixer_output = jnp.einsum(
        "zaw,wk->zak", gated_product, complete_output_weight, preferred_element_type=jnp.float32
    )
    residual_middle = input_rows + lax.psum(partial_mixer_output, "tensor")
    plain_two, inverse_two = norm_forward(residual_middle)
    second_normalized = (plain_two * gain_two).astype(jnp.bfloat16)
    gate_branch = jnp.einsum(
        "mut,tz->muz",
        second_normalized,
        feedforward_gate_weight,
        preferred_element_type=jnp.float32,
    )
    up_projection_branch = jnp.einsum(
        "mut,tz->muz", second_normalized, feedforward_up_weight, preferred_element_type=jnp.float32
    )
    sigmoid_gate = jax.nn.sigmoid(gate_branch)
    silu_gate = gate_branch * sigmoid_gate
    hidden_state = (silu_gate * up_projection_branch).astype(jnp.bfloat16)
    partial_feedforward = jnp.einsum(
        "eny,yv->env", hidden_state, feedforward_down_weight, preferred_element_type=jnp.float32
    )
    block_out = (
        residual_middle
        + lax.psum(partial_feedforward.astype(jnp.bfloat16), "tensor").astype(jnp.float32)
    ).astype(jnp.bfloat16)
    grad_out = cotangent.astype(jnp.float32)
    hidden_gradient = jnp.einsum(
        "qmn,pn->qmp", cotangent, feedforward_down_weight, preferred_element_type=jnp.float32
    )
    down_gradient = jnp.einsum(
        "eiu,eix->ux", hidden_state, cotangent, preferred_element_type=jnp.float32
    )
    gate_gradient = (
        hidden_gradient
        * up_projection_branch
        * sigmoid_gate
        * (1.0 + gate_branch * (1.0 - sigmoid_gate))
    ).astype(jnp.bfloat16)
    up_gradient = (hidden_gradient * silu_gate).astype(jnp.bfloat16)
    grad_w_gate = jnp.einsum(
        "rnj,rnt->jt", second_normalized, gate_gradient, preferred_element_type=jnp.float32
    )
    up_weight_gradient = jnp.einsum(
        "rnj,rnt->jt", second_normalized, up_gradient, preferred_element_type=jnp.float32
    )
    partial_normed_two = jnp.einsum(
        "wxo,qo->wxq", gate_gradient, feedforward_gate_weight, preferred_element_type=jnp.float32
    )
    partial_normed_two = partial_normed_two + jnp.einsum(
        "wxo,qo->wxq", up_gradient, feedforward_up_weight, preferred_element_type=jnp.float32
    )
    grad_normed_two = lax.psum(partial_normed_two, "tensor")
    grad_rows_two, gain_grad_two = norm_backward_and_gain(grad_normed_two, plain_two, inverse_two, gain_two)
    grad_middle = grad_out + grad_rows_two
    mixer_output_gradient = grad_middle.astype(jnp.bfloat16)
    grad_gated = jnp.einsum(
        "ymo,bo->ymb",
        mixer_output_gradient,
        complete_output_weight,
        preferred_element_type=jnp.float32,
    )
    out_weight_gradient = jnp.einsum(
        "miy,miq->yq", gated_product, mixer_output_gradient, preferred_element_type=jnp.float32
    )
    grad_convolved = (grad_gated * out_gate).astype(jnp.bfloat16)
    grad_out_gate = grad_gated * convolved
    grad_edge = from_behind(grad_convolved[:, :2, :], "context", -1)
    grad_extended = jnp.concatenate([grad_convolved, grad_edge], axis=1).astype(jnp.float32)
    grad_product = (
        taps[0] * grad_extended[:, :width, :]
        + taps[1] * grad_extended[:, 1 : width + 1, :]
        + taps[2] * grad_extended[:, 2:, :]
    )
    grad_local = grad_extended[:, :width, :]
    tap_grads = jnp.stack(
        [
            jnp.sum(grad_local * recent, axis=(0, 1)),
            jnp.sum(grad_local * previous, axis=(0, 1)),
            jnp.sum(grad_local * earlier, axis=(0, 1)),
        ]
    )
    projection_gradient = jnp.stack(
        [
            (grad_product * conv_input).astype(jnp.bfloat16),
            grad_out_gate.astype(jnp.bfloat16),
            (grad_product * in_gate).astype(jnp.bfloat16),
        ]
    )
    grad_w_in = jnp.einsum(
        "pxw,gpxt->gwt", first_normalized, projection_gradient, preferred_element_type=jnp.float32
    )
    partial_normed_one = jnp.einsum(
        "ireo,ivo->rev",
        projection_gradient,
        complete_input_weight,
        preferred_element_type=jnp.float32,
    )
    shard_in, shard_out, shard_gate, shard_up, shard_down = (
        lax.psum_scatter(
            grad_w_in.astype(jnp.bfloat16), "shard", scatter_dimension=1, tiled=True
        ).astype(jnp.float32),
        lax.psum_scatter(
            out_weight_gradient.astype(jnp.bfloat16), "shard", scatter_dimension=1, tiled=True
        ).astype(jnp.float32),
        lax.psum_scatter(
            grad_w_gate.astype(jnp.bfloat16), "shard", scatter_dimension=0, tiled=True
        ).astype(jnp.float32),
        lax.psum_scatter(
            up_weight_gradient.astype(jnp.bfloat16), "shard", scatter_dimension=0, tiled=True
        ).astype(jnp.float32),
        lax.psum_scatter(
            down_gradient.astype(jnp.bfloat16), "shard", scatter_dimension=1, tiled=True
        ).astype(jnp.float32),
    )
    total_in, total_out, total_gate, total_up, total_down = (
        lax.psum(shard_in.astype(jnp.bfloat16), "context").astype(jnp.float32),
        lax.psum(shard_out.astype(jnp.bfloat16), "context").astype(jnp.float32),
        lax.psum(shard_gate.astype(jnp.bfloat16), "context").astype(jnp.float32),
        lax.psum(shard_up.astype(jnp.bfloat16), "context").astype(jnp.float32),
        lax.psum(shard_down.astype(jnp.bfloat16), "context").astype(jnp.float32),
    )
    grad_normed_one = lax.psum(partial_normed_one.astype(jnp.bfloat16), "tensor").astype(
        jnp.float32
    )
    grad_rows_one, gain_grad_one = norm_backward_and_gain(grad_normed_one, plain_one, inverse_one, gain_one)
    grad_tokens = grad_middle + grad_rows_one
    total_gain_one, total_taps, total_gain_two = lax.psum(
        (gain_grad_one, tap_grads, gain_grad_two), ("shard", "context")
    )
    return (
        block_out,
        grad_tokens,
        total_gain_one,
        total_in,
        total_taps,
        total_out,
        total_gain_two,
        total_gate,
        total_up,
        total_down,
    )


def solution(mesh):
    in_specs = (
        P("shard", "context", None),
        P(),
        P(None, "shard", "tensor"),
        P(None, "tensor"),
        P("tensor", "shard"),
        P(),
        P("shard", "tensor"),
        P("shard", "tensor"),
        P("tensor", "shard"),
        P("shard", "context", None),
    )
    out_specs = (
        P("shard", "context", None),
        P("shard", "context", None),
        P(),
        P(None, "shard", "tensor"),
        P(None, "tensor"),
        P("tensor", "shard"),
        P(),
        P("shard", "tensor"),
        P("shard", "tensor"),
        P("tensor", "shard"),
    )
    sizes = mesh.shape
    by_links = (sizes["shard"], sizes["context"], sizes["tensor"]) == (4, 2, 4)
    body = local_by_links if by_links else local
    return jax.shard_map(body, mesh=mesh, in_specs=in_specs, out_specs=out_specs, check_vma=False)
```

```python
import functools

import jax
import jax.numpy as jnp
from jax import lax
from jax.experimental import pallas as pl
from jax.experimental.pallas import tpu as pltpu
from jax.sharding import PartitionSpec as P

EPSILON = 1e-05
F32 = jnp.float32
BF16 = jnp.bfloat16
MIB = 1024 * 1024
LEAD = 16


def norm_forward(values):
    inverse = lax.rsqrt(jnp.mean(values * values, axis=-1, keepdims=True) + EPSILON)
    return (values * inverse, inverse)


def norm_backward(grad_normed, plain, inverse, gain):
    grad_plain = grad_normed * gain
    return inverse * (
        grad_plain - plain * jnp.mean(grad_plain * plain, axis=-1, keepdims=True)
    )


def dot_nn(a, b):
    return lax.dot_general(a, b, (((1,), (0,)), ((), ())), preferred_element_type=F32)


def dot_nt(a, b):
    return lax.dot_general(a, b, (((1,), (1,)), ((), ())), preferred_element_type=F32)


def dot_tn(a, b):
    return lax.dot_general(a, b, (((0,), (0,)), ((), ())), preferred_element_type=F32)


def rounded(value):
    return lax.optimization_barrier(value.astype(BF16))


def shifted(value, steps):
    count = lax.axis_size("tensor")
    return lax.ppermute(value, "tensor", [(i, (i + steps) % count) for i in range(count)])


def swapped(value, axis, bit):
    count = lax.axis_size(axis)
    return lax.ppermute(value, axis, [(i, i ^ bit) for i in range(count)])


def to_core(value):
    return swapped(value, "shard", 1)


def to_y(value):
    return swapped(value, "shard", 2)


def to_x(value):
    return swapped(value, "context", 1)


def pair(value):
    return swapped(value, "tensor", 1)


def inward(value):
    return lax.ppermute(value, "tensor", [(0, 1), (3, 2)])


def outward(value):
    return lax.ppermute(value, "tensor", [(1, 0), (2, 3)])


def across(value):
    return lax.ppermute(value, "tensor", [(1, 2), (2, 1)])


def together(*values):
    return lax.optimization_barrier(values)


def added(*values):
    return sum(value.astype(F32) for value in values).astype(BF16)


def mixer_forward_kernel(ids, rows, mine, other, *rest):
    gated, weights, out_weights, own = rest[-4:]
    part = mine.shape[1]
    half = 2 * part + LEAD

    @pl.when(pl.program_id(0) == 0)
    def _():
        for bit, piece in enumerate((mine, other)):
            for far in range(2):
                start = pl.multiple_of((ids[0] ^ (bit + 2 * far)) * part, part)
                for side in range(2):
                    first = 2 * (ids[2] ^ side)
                    base = (2 * far + side) * half
                    lower = piece[base : base + part, :]
                    upper = piece[base + part : base + 2 * part, :]

                    @pl.when(first == 0)
                    def _(start=start, lower=lower, upper=upper):
                        weights[0, pl.ds(start, part), :part] = lower
                        weights[0, pl.ds(start, part), part : 2 * part] = upper

                    @pl.when(first == 2)
                    def _(start=start, lower=lower, upper=upper):
                        weights[0, pl.ds(start, part), 2 * part :] = lower
                        out_weights[pl.ds(start, part), :] = upper

    taps = mine[2 * part : half, :].astype(F32)
    values = rows[0]
    in_gate = dot_nn(values, weights[0, :, :part])
    conv_input = dot_nn(values, weights[0, :, 2 * part :])
    out_gate = dot_nn(values, weights[0, :, part : 2 * part])
    product = (in_gate * conv_input).astype(BF16).astype(F32)
    convolved = (
        taps[0:1] * product
        + taps[1:2] * pltpu.roll(product, 1, 0)
        + taps[2:3] * pltpu.roll(product, 2, 0)
    )[LEAD:]
    gated[0] = (out_gate[LEAD:] * convolved).astype(BF16)

    @pl.when(pl.program_id(0) == ids[1])
    def _():
        own[0] = in_gate.astype(BF16)
        own[1] = out_gate.astype(BF16)
        own[2] = conv_input.astype(BF16)


def mixer_forward(ids, rows, pieces, block, earlier):
    seqs, long, model = rows.shape
    width = long - LEAD
    part = pieces[0].shape[1]
    count = model // part
    specs = [pl.BlockSpec((1, long, model), lambda q, ids: (q, 0, 0))]
    specs += [pl.BlockSpec(piece.shape, lambda q, ids: (0, 0)) for piece in pieces]
    specs += [pl.BlockSpec(memory_space=pl.ANY)] * len(earlier)
    return pl.pallas_call(
        mixer_forward_kernel,
        grid_spec=pltpu.PrefetchScalarGridSpec(
            num_scalar_prefetch=1,
            grid=(seqs,),
            in_specs=specs,
            out_specs=[
                pl.BlockSpec((1, width, part), lambda q, ids: (q, 0, block)),
                pl.BlockSpec((1, model, 3 * part), lambda q, ids: (block, 0, 0)),
                pl.BlockSpec((model, part), lambda q, ids: (0, block)),
                pl.BlockSpec((3, long, part), lambda q, ids: (0, 0, block)),
            ],
        ),
        out_shape=[
            jax.ShapeDtypeStruct((seqs, width, model), BF16),
            jax.ShapeDtypeStruct((count, model, 3 * part), BF16),
            jax.ShapeDtypeStruct((model, model), BF16),
            jax.ShapeDtypeStruct((3, long, model), BF16),
        ],
        input_output_aliases={4: 0, 5: 1, 6: 2, 7: 3} if earlier else {},
        compiler_params=pltpu.CompilerParams(vmem_limit_bytes=36 * MIB),
        cost_estimate=pl.CostEstimate(flops=0, bytes_accessed=0, transcendentals=0),
        name="mixer_forward",
    )(ids, rows, *pieces, *earlier)


def feedforward_kernel(own, ids, gated, mixer, tokens, gain, cotangent, *rest):
    near, near_core, *rest = rest
    far, rest = rest[:6], rest[6:]
    outputs = rest[-8 - own : -2]
    weights, arrived = rest[-2:]
    normed, down, grad_normed, hidden, grad_gate, grad_up = outputs[:6]
    part = far[0].shape[0]
    first = pl.program_id(0) == 0

    def copies(which):
        rows = pl.ds(which * part, part)
        sources = (near.at[rows, :], near_core.at[rows, :], far[which], far[3 + which])
        for place, source in enumerate(sources):
            start = pl.multiple_of((ids[0] ^ place) * part, part)
            yield pltpu.make_async_copy(
                source,
                weights.at[which, pl.ds(start, part), :],
                arrived.at[which, place],
            )

    @pl.when(first)
    def _():
        for which in range(3):
            for copy in copies(which):
                copy.start()

    middle = tokens[0].astype(F32) + dot_nt(gated[0], mixer[...])
    if own:
        rest[-3][...] = middle
    values = (norm_forward(middle)[0] * gain[...].astype(F32)).astype(BF16)
    normed[0] = values

    @pl.when(first)
    def _():
        for which in range(3):
            for copy in copies(which):
                copy.wait()

    gate = dot_nn(values, weights[0])
    up = dot_nn(values, weights[1])
    grad_hidden = dot_nn(cotangent[0], weights[2])
    sigmoid = jax.nn.sigmoid(gate)
    silu = gate * sigmoid
    hidden_now = (silu * up).astype(BF16)
    hidden[0] = hidden_now
    gate_now = (grad_hidden * up * sigmoid * (1.0 + gate * (1.0 - sigmoid))).astype(BF16)
    up_now = (grad_hidden * silu).astype(BF16)
    grad_gate[0] = gate_now
    grad_up[0] = up_now
    grad_normed[...] = (dot_nt(gate_now, weights[0]) + dot_nt(up_now, weights[1])).astype(BF16)
    down[...] = dot_nt(hidden_now, weights[2]).astype(BF16)


def feedforward(ids, gated, mixer, tokens, gain, cotangent, places, which, earlier):
    seqs, width, model = tokens.shape
    units = places[0].shape[1]
    size = width // 2
    own = int(which == 3)

    def seq(i, ids):
        return (ids[3 + which], i, 0)

    def row(i, ids):
        return (i, 0)

    wide = jax.ShapeDtypeStruct((seqs, width, units), BF16)
    here = jax.ShapeDtypeStruct((width, model), BF16)
    first = 6 + len(places)
    return pl.pallas_call(
        functools.partial(feedforward_kernel, own),
        grid_spec=pltpu.PrefetchScalarGridSpec(
            num_scalar_prefetch=1,
            grid=(2,),
            in_specs=[
                pl.BlockSpec((1, size, model), seq),
                pl.BlockSpec((model, model), lambda i, ids: (0, 0), pipeline_mode=pl.Buffered(1)),
                pl.BlockSpec((1, size, model), seq),
                pl.BlockSpec((1, model), lambda i, ids: (0, 0)),
                pl.BlockSpec((1, size, model), seq),
            ]
            + [pl.BlockSpec(memory_space=pltpu.HBM)] * len(places)
            + [pl.BlockSpec(memory_space=pl.ANY)] * len(earlier),
            out_specs=[
                pl.BlockSpec((1, size, model), seq),
                pl.BlockSpec((size, model), row),
                pl.BlockSpec((size, model), row),
                pl.BlockSpec((1, size, units), seq),
                pl.BlockSpec((1, size, units), seq),
                pl.BlockSpec((1, size, units), seq),
            ]
            + [pl.BlockSpec((size, model), row)] * own,
            scratch_shapes=[
                pltpu.VMEM((3, model, units), BF16),
                pltpu.SemaphoreType.DMA((3, 4)),
            ],
        ),
        out_shape=[
            jax.ShapeDtypeStruct(tokens.shape, BF16),
            here,
            here,
            wide,
            wide,
            wide,
        ]
        + [jax.ShapeDtypeStruct((width, model), F32)] * own,
        input_output_aliases={first: 0, first + 1: 3, first + 2: 4, first + 3: 5} if earlier else {},
        compiler_params=pltpu.CompilerParams(vmem_limit_bytes=40 * MIB),
        cost_estimate=pl.CostEstimate(flops=0, bytes_accessed=0, transcendentals=0),
        name="feedforward",
    )(ids, gated, mixer, tokens, gain, cotangent, *places, *earlier)


def middle_gradient(parts, own, cotangent, gain):
    incoming = sum(part[...].astype(F32) for part in parts)
    plain, inverse = norm_forward(own[...])
    total = cotangent[0].astype(F32) + norm_backward(incoming, plain, inverse, gain[...].astype(F32))
    return total, jnp.sum(incoming * plain, axis=0, keepdims=True)


def edge_kernel(ids, part0, part1, part2, own, cotangent, gain, gate, out_weights, edge):
    mixed = middle_gradient((part0, part1, part2), own, cotangent, gain)[0].astype(BF16)
    edge[...] = (dot_nn(mixed, out_weights[...]) * gate[0].astype(F32)).astype(BF16)


def edge_gradient(ids, parts, own, cotangent, gain, gates, out_weights):
    width, model = own.shape
    rows = pl.BlockSpec((LEAD, model), lambda i, ids: (0, 0))
    return pl.pallas_call(
        edge_kernel,
        grid_spec=pltpu.PrefetchScalarGridSpec(
            num_scalar_prefetch=1,
            grid=(1,),
            in_specs=[
                rows, rows, rows, rows,
                pl.BlockSpec((1, LEAD, model), lambda i, ids: (ids[1], 0, 0)),
                pl.BlockSpec((1, model), lambda i, ids: (0, 0)),
                pl.BlockSpec((1, LEAD, model), lambda i, ids: (1, 1, 0)),
                pl.BlockSpec(out_weights.shape, lambda i, ids: (0, 0)),
            ],
            out_specs=rows,
        ),
        out_shape=jax.ShapeDtypeStruct((LEAD, model), BF16),
        compiler_params=pltpu.CompilerParams(vmem_limit_bytes=60 * MIB),
        cost_estimate=pl.CostEstimate(flops=0, bytes_accessed=0, transcendentals=0),
        name="edge_gradient",
    )(ids, *parts, own, cotangent, gain, gates, out_weights)


def mixer_backward_kernel(
    ids, part0, part1, part2, own, cotangent, gain_two, gates, edge, weights, out_weights, taps, tokens, gain_one,
    grad_mixed, gain_two_grad, grad_first, grad_out_gate, grad_third, tap_grads, grad_tokens, gain_one_grad,
    grad_middle, total,
):
    block = pl.program_id(0)
    width = grad_mixed.shape[0]

    @pl.when(block == 0)
    def _():
        here, gain_grad = middle_gradient((part0, part1, part2), own, cotangent, gain_two)
        gain_two_grad[...] = gain_grad
        grad_middle[...] = here
        grad_mixed[...] = here.astype(BF16)
        total[...] = jnp.zeros_like(total)

    tap = taps[0].astype(F32)
    in_gate = gates[0].astype(F32)
    conv_input = gates[2].astype(F32)
    product = (in_gate * conv_input).astype(BF16).astype(F32)
    recent, previous, earlier = (
        product[LEAD:], pltpu.roll(product, 1, 0)[LEAD:], pltpu.roll(product, 2, 0)[LEAD:],
    )
    convolved = tap[0:1] * recent + tap[1:2] * previous + tap[2:3] * earlier
    grad_gated = dot_nn(grad_mixed[...], out_weights[...])
    second = (grad_gated * convolved).astype(BF16)
    grad_out_gate[...] = second
    low = (grad_gated * gates[1, LEAD:, :].astype(F32)).astype(BF16).astype(F32)
    tap_grads[0] = jnp.concatenate(
        [
            jnp.sum(low * recent, axis=0, keepdims=True),
            jnp.sum(low * previous, axis=0, keepdims=True),
            jnp.sum(low * earlier, axis=0, keepdims=True),
            jnp.zeros((5, low.shape[1]), F32),
        ]
    )
    longer = jnp.concatenate([low, edge[...].astype(F32)])
    count = longer.shape[0]
    grad_product = (
        tap[0:1] * longer
        + tap[1:2] * pltpu.roll(longer, count - 1, 0)
        + tap[2:3] * pltpu.roll(longer, count - 2, 0)
    )[:width]
    first = (grad_product * conv_input[LEAD:]).astype(BF16)
    third = (grad_product * in_gate[LEAD:]).astype(BF16)
    grad_first[...] = first
    grad_third[...] = third
    total[...] += dot_nt(jnp.concatenate([first, second, third], axis=1), weights[0])

    @pl.when(block == pl.num_programs(0) - 1)
    def _():
        incoming = total[...]
        plain, inverse = norm_forward(tokens[0].astype(F32))
        gain_one_grad[...] = jnp.sum(incoming * plain, axis=0, keepdims=True)
        grad_tokens[...] = (
            grad_middle[...] + norm_backward(incoming, plain, inverse, gain_one[...].astype(F32))
        ).astype(BF16)


def mixer_backward(
    ids, parts, own, cotangent, gain_two, gates, edge, weights, out_weights, taps, tokens, gain_one
):
    width, model = own.shape
    long = gates.shape[1]
    count = weights.shape[0]
    part = model // count
    whole = pl.BlockSpec((width, model), lambda j, ids: (0, 0))
    once = pl.BlockSpec((width, model), lambda j, ids: (0, 0), pipeline_mode=pl.Buffered(1))
    mine = pl.BlockSpec((1, width, model), lambda j, ids: (ids[1], 0, 0), pipeline_mode=pl.Buffered(1))
    line = pl.BlockSpec((1, model), lambda j, ids: (0, 0))
    column = pl.BlockSpec((width, part), lambda j, ids: (0, j))
    lines = jax.ShapeDtypeStruct((1, model), F32)
    matrix = jax.ShapeDtypeStruct((width, model), BF16)
    return pl.pallas_call(
        mixer_backward_kernel,
        grid_spec=pltpu.PrefetchScalarGridSpec(
            num_scalar_prefetch=1,
            grid=(count,),
            in_specs=[
                once, once, once, once, mine, line,
                pl.BlockSpec((3, long, part), lambda j, ids: (0, 0, j)),
                pl.BlockSpec((LEAD, part), lambda j, ids: (0, j)),
                pl.BlockSpec((1, model, 3 * part), lambda j, ids: (j, 0, 0)),
                pl.BlockSpec((model, part), lambda j, ids: (0, j)),
                pl.BlockSpec((1, LEAD, part), lambda j, ids: (j, 0, 0)),
                mine, line,
            ],
            out_specs=[
                whole, line, column, column, column,
                pl.BlockSpec((1, 8, part), lambda j, ids: (j, 0, 0)),
                whole, line,
            ],
            scratch_shapes=[pltpu.VMEM((width, model), F32), pltpu.VMEM((width, model), F32)],
        ),
        out_shape=[
            matrix, lines, matrix, matrix, matrix,
            jax.ShapeDtypeStruct((count, 8, part), F32),
            matrix, lines,
        ],
        compiler_params=pltpu.CompilerParams(vmem_limit_bytes=60 * MIB),
        cost_estimate=pl.CostEstimate(flops=0, bytes_accessed=0, transcendentals=0),
        name="mixer_backward",
    )(ids, *parts, own, cotangent, gain_two, gates, edge, weights, out_weights, taps, tokens, gain_one)


def split_rows(ids, g):
    return ids[7 + g]


def feedforward_gradient_kernel(ids, left, right, send, keep):
    result = dot_tn(left[...], right[...]).astype(BF16)

    @pl.when(pl.program_id(0) < 2)
    def _():
        send[0] = result

    @pl.when(pl.program_id(0) >= 2)
    def _():
        keep[0] = result


def feedforward_gradient(ids, left, right):
    tokens, model = left.shape
    units = right.shape[1]
    part = model // 4
    shape = jax.ShapeDtypeStruct((2, part, units), BF16)
    return pl.pallas_call(
        feedforward_gradient_kernel,
        grid_spec=pltpu.PrefetchScalarGridSpec(
            num_scalar_prefetch=1,
            grid=(4,),
            in_specs=[
                pl.BlockSpec((tokens, part), lambda g, ids: (0, split_rows(ids, g))),
                pl.BlockSpec((tokens, units), lambda g, ids: (0, 0), pipeline_mode=pl.Buffered(1)),
            ],
            out_specs=[
                pl.BlockSpec((1, part, units), lambda g, ids: (jnp.minimum(g, 1), 0, 0)),
                pl.BlockSpec((1, part, units), lambda g, ids: (jnp.maximum(g - 2, 0), 0, 0)),
            ],
        ),
        out_shape=[shape, shape],
        compiler_params=pltpu.CompilerParams(vmem_limit_bytes=32 * MIB),
        cost_estimate=pl.CostEstimate(flops=0, bytes_accessed=0, transcendentals=0),
        name="feedforward_gradient",
    )(ids, left, right)


def mixer_gradient_kernel(ids, rows, mixed, first, second, third, gated, send, keep):
    part = mixed.shape[1]
    here = []
    for left, right in (
        (rows[0, LEAD:], first[...]),
        (rows[0, LEAD:], second[...]),
        (rows[0, LEAD:], third[...]),
        (mixed[...], gated[0]),
    ):
        here.append(dot_tn(left, right).astype(BF16))

    def store(out):
        for matrix, value in enumerate(here):
            for block in range(4):
                for upper in range(2):
                    out[0, ids[2] ^ upper, ids[11 + block], matrix] = value[
                        upper * part // 2 : (upper + 1) * part // 2, block * part : (block + 1) * part
                    ]

    @pl.when(pl.program_id(0) < 2)
    def _():
        store(send)

    @pl.when(pl.program_id(0) >= 2)
    def _():
        store(keep)


def mixer_gradient(ids, rows, mixed, first, second, third, gated):
    width, model = mixed.shape
    long = rows.shape[1]
    part = model // 4
    shape = jax.ShapeDtypeStruct((2, 2, 4, 4, part // 2, part), BF16)
    block = (1, 2, 4, 4, part // 2, part)
    whole = pl.BlockSpec((width, model), lambda g, ids: (0, 0))
    return pl.pallas_call(
        mixer_gradient_kernel,
        grid_spec=pltpu.PrefetchScalarGridSpec(
            num_scalar_prefetch=1,
            grid=(4,),
            in_specs=[
                pl.BlockSpec((1, long, part), lambda g, ids: (ids[1], 0, split_rows(ids, g))),
                pl.BlockSpec((width, part), lambda g, ids: (0, split_rows(ids, g))),
                whole, whole, whole,
                pl.BlockSpec((1, width, model), lambda g, ids: (ids[1], 0, 0)),
            ],
            out_specs=[
                pl.BlockSpec(block, lambda g, ids: (jnp.minimum(g, 1), 0, 0, 0, 0, 0)),
                pl.BlockSpec(block, lambda g, ids: (jnp.maximum(g - 2, 0), 0, 0, 0, 0, 0)),
            ],
        ),
        out_shape=[shape, shape],
        compiler_params=pltpu.CompilerParams(vmem_limit_bytes=40 * MIB),
        cost_estimate=pl.CostEstimate(flops=0, bytes_accessed=0, transcendentals=0),
        name="mixer_gradient",
    )(ids, rows, mixed, first, second, third, gated)


def local_by_links(
    tokens, norm_gain, w_in, conv_weight, convolution_out_weight, ffn_gain, w_gate, w_up, w_down, cotangent
):
    seqs, width, model = tokens.shape
    part = w_in.shape[1]
    units = w_gate.shape[1]
    shard, side, level = (lax.axis_index(name) for name in ("shard", "context", "tensor"))
    end = jnp.logical_or(level == 0, level == 3)
    order = [
        jnp.where(level < 2, 3, 0), jnp.where(level < 2, 2, 1), level ^ 1, level,
    ]
    place = [sum(jnp.where((level + block) % 4 == order[k], k, 0) for k in range(4)) for block in range(4)]
    ids = jnp.stack(
        [shard, level, side] + order + [shard ^ 1, shard ^ 3, shard, shard ^ 2] + place
    ).astype(jnp.int32)
    gain_one = norm_gain.reshape(1, model)
    gain_two = ffn_gain.reshape(1, model)
    def placed(own, others, dtype):
        out = jnp.zeros((seqs, width, model), dtype)
        for bits, block in enumerate((own,) + others):
            out = lax.dynamic_update_slice(out, block.astype(dtype)[None], (level ^ bits, 0, 0))
        return out

    taps_near = jnp.concatenate([conv_weight, jnp.zeros((LEAD - 3, part), BF16)])
    near = jnp.concatenate(
        [w_in[0], w_in[1], taps_near, w_in[2], convolution_out_weight.T, taps_near]
    )
    half = near.shape[0] // 2

    def sides(value):
        return [lax.dynamic_slice_in_dim(value, (side ^ bit) * half, half, 0) for bit in range(2)]

    near, near_side, near_else = together(near, *sides(near))
    far = to_y(near)
    near_right, near_left = shifted(near_side, -1), shifted(near_side, 1)
    edge = lax.ppermute(tokens[:, width - 2 :, :], "context", [(0, 1)])
    w_down = w_down.T
    feed = jnp.concatenate([w_gate, w_up, w_down])
    far, near_right, near_left, edge, feed, near_side, near_else, w_gate, w_up, w_down = together(
        far, near_right, near_left, edge, feed, near_side, near_else, w_gate, w_up, w_down
    )

    far_side, far_else = sides(far)
    far_right, far_left = shifted(far_side, -1), shifted(far_side, 1)
    near_over = to_x(jnp.concatenate([near_right, near_left]))
    far_gate = to_y(w_gate)
    mine = together(jnp.concatenate([near_side, near_else, far_side, far_else]))[0]
    other = to_core(mine)
    rows = jnp.concatenate([jnp.zeros((seqs, LEAD - 2, model), BF16), edge, tokens], axis=1).astype(F32)
    rows = (norm_forward(rows)[0] * gain_one.astype(F32)).astype(BF16)
    state = mixer_forward(ids, rows, (mine, other), 0, ())
    far_right, far_left, near_over, near_right, near_left, rows, feed, w_up, w_down, far_gate, *state = together(
        far_right, far_left, near_over, near_right, near_left, rows, feed, w_up, w_down, far_gate, *state
    )

    near_far, far_far = shifted(near_right, -1), shifted(far_left, 1)
    far_over = to_x(jnp.concatenate([far_right, far_left]))
    far_up = to_y(w_up)
    feed_core = to_core(feed)
    near_far, far_far, far_over, feed_core, far_up, w_down, *state = together(
        near_far, far_far, far_over, feed_core, far_up, w_down, *state
    )

    last_over = to_x(jnp.concatenate([near_far, far_far]))
    far_down = to_y(w_down)
    for block, rows_of, (a, b) in (
        (1, slice(None, half), (near_right, far_right)),
        (3, slice(half, None), (near_left, far_left)),
    ):
        mine = together(jnp.concatenate([a, near_over[rows_of], b, far_over[rows_of]]))[0]
        state = mixer_forward(ids, rows, (mine, to_core(mine)), block, state)
    last_over, far_down, far_gate, far_up, *state = together(
        last_over, far_down, far_gate, far_up, *state
    )

    mine = together(jnp.concatenate([near_far, last_over[:half], far_far, last_over[half:]]))[0]
    state = mixer_forward(ids, rows, (mine, to_core(mine)), 2, state)
    gated, weights, out_weights, gates = state
    far_all = (far_gate, far_up, far_down)
    core_all = [to_core(value) for value in far_all]
    gated, weights, out_weights, gates, *core_all = together(gated, weights, out_weights, gates, *core_all)
    places = (feed, feed_core, *far_all, *core_all)
    taps = jnp.stack([near_side[2 * part :], near_right[2 * part :], near_far[2 * part :], near_left[2 * part :]])

    def forward(which, earlier):
        normed, down, grad, *wide = feedforward(
            ids, gated, out_weights, tokens, gain_two, cotangent, places, which, earlier
        )
        return down, grad, (normed, *wide[:3]), wide[3:]

    down0, grad0, done, _ = forward(0, ())
    down0, grad0, *done = together(down0, grad0, *done)

    grad_pair0 = pair(grad0)
    down1, grad1, done, _ = forward(1, tuple(done))
    grad_pair0, down1, grad1, *done = together(grad_pair0, down1, grad1, *done)

    grad_pair1 = pair(grad1)
    grad_over0 = across(added(grad0, grad_pair0))
    down2, grad2, done, _ = forward(2, tuple(done))
    grad_pair1, grad_over0, down2, grad2, *done = together(grad_pair1, grad_over0, down2, grad2, *done)

    grad_pair2 = pair(added(grad2, grad_over0))
    grad_over1 = across(added(grad1, grad_pair1))
    down3, grad3, done, (middle_own,) = forward(3, tuple(done))
    normed, hidden, grad_gate, grad_up = (v.reshape(seqs * width, v.shape[2]) for v in done)
    grad_pair2, grad_over1, grad3, normed, hidden, grad_gate, grad_up, down0 = together(
        grad_pair2, grad_over1, grad3, normed, hidden, grad_gate, grad_up, down0
    )

    down_pair0 = pair(down0)
    grad_parts = (grad3, grad_pair2, grad_over1)
    edge = edge_gradient(ids, grad_parts, middle_own, cotangent, gain_two, gates, out_weights)
    edge = lax.ppermute(edge, "context", [(1, 0)])
    (
        grad_mixed, gain_two_grad, grad_first, grad_out_gate, grad_third, tap_grads, tokens_own, gain_one_grad,
    ) = mixer_backward(
        ids, grad_parts, middle_own, cotangent, gain_two, gates, edge, weights, out_weights, taps, tokens, gain_one
    )
    (
        down_pair0, tokens_own, grad_first, grad_third, grad_mixed, gain_one_grad, normed, hidden, grad_gate, grad_up,
    ) = together(
        down_pair0, tokens_own, grad_first, grad_third, grad_mixed, gain_one_grad, normed, hidden, grad_gate, grad_up,
    )

    tokens_pair = pair(tokens_own)
    tokens_over = across(tokens_own)
    send_mixer, keep_mixer = mixer_gradient(
        ids, rows, grad_mixed, grad_first, grad_out_gate, grad_third, gated
    )
    tap_rows = tap_grads[:, :3].transpose(1, 0, 2)
    tap_rows = jnp.roll(tap_rows, level, axis=1).reshape(3, model)
    small = jnp.concatenate([gain_one_grad, gain_two_grad, tap_rows, jnp.zeros((3, model), F32)])
    small = small + swapped(small, "tensor", 1)
    tokens_pair, tokens_over, send_mixer, keep_mixer, hidden, grad_gate, grad_up, small, down0, down1, down2 = together(
        tokens_pair, tokens_over, send_mixer, keep_mixer, hidden, grad_gate, grad_up, small, down0, down1, down2
    )

    mixed_pair1 = pair(jnp.where(end, down1, tokens_over))
    tokens_over_end = across(tokens_pair)
    core_mixer = to_core(send_mixer)
    send_gate, keep_gate = feedforward_gradient(ids, normed, grad_gate)
    send_up, keep_up = feedforward_gradient(ids, normed, grad_up)
    small = small + swapped(small, "tensor", 2)
    down_sum0 = added(down0, down_pair0)
    (
        mixed_pair1, tokens_over_end, core_mixer, send_gate, keep_gate, send_up, keep_up, small, down_sum0, hidden,
    ) = together(
        mixed_pair1, tokens_over_end, core_mixer, send_gate, keep_gate, send_up, keep_up, small, down_sum0, hidden,
    )

    mixed_pair2 = pair(jnp.where(end, down2, tokens_over_end))
    down_over0 = across(down_sum0)
    core_gate = to_core(send_gate)
    small = small + to_x(small)
    send_down, keep_down = feedforward_gradient(ids, cotangent.reshape(seqs * width, model), hidden)
    sum_mixer = added(keep_mixer, core_mixer)
    low, high = slice(None, part // 4), slice(part // 4, None)
    here_low, send_low = sum_mixer[0, :, :, :, low], sum_mixer[1, :, :, :, low]
    here_high, send_high = sum_mixer[:, 0, :, :, high], sum_mixer[:, 1, :, :, high]
    down_sum1 = added(down1, mixed_pair1)
    (
        mixed_pair2, down_over0, core_gate, send_up, send_down, keep_down, here_low, send_low, here_high,
        send_high, down_sum1, small, tokens_own,
    ) = together(
        mixed_pair2, down_over0, core_gate, send_up, send_down, keep_down, here_low, send_low, here_high,
        send_high, down_sum1, small, tokens_own,
    )

    down_pair3 = pair(added(down2, down_over0))
    down_over1 = across(down_sum1)
    y_low, x_high = to_y(send_low), to_x(send_high)
    grad_tokens = placed(
        tokens_own,
        (
            tokens_pair,
            jnp.where(end, mixed_pair1, tokens_over_end),
            jnp.where(end, mixed_pair2, tokens_over),
        ),
        F32,
    )
    sum_gate = added(keep_gate, core_gate)
    core_both = to_core(jnp.concatenate([send_up, send_down]))
    keep_both = jnp.concatenate([keep_up, keep_down])
    down_pair3, down_over1, y_low, x_high, grad_tokens, sum_gate, core_both, keep_both, small = together(
        down_pair3, down_over1, y_low, x_high, grad_tokens, sum_gate, core_both, keep_both, small
    )

    out_own = rounded(
        middle_own
        + down3.astype(F32)
        + jnp.where(end, down_pair3, mixed_pair2).astype(F32)
        + down_over1.astype(F32)
    )
    out_pair = pair(out_own)
    out_over = across(out_own)
    half_low = added(here_low, y_low)
    half_high = added(here_high, x_high)
    x_low, y_high = to_x(half_low[1]), to_y(half_high[1])
    mixer = jnp.concatenate([added(half_low[0], x_low), added(half_high[0], y_high)], axis=2)
    y_gate = to_y(sum_gate[1])
    sum_both = added(keep_both, core_both)
    send_both = jnp.concatenate([sum_both[1], sum_both[3]])
    here_both = jnp.concatenate([sum_both[0], sum_both[2]])
    out_pair, out_over, mixer, send_both, here_both, y_gate, small = together(
        out_pair, out_over, mixer, send_both, here_both, y_gate, small
    )

    out_over_end = across(out_pair)
    out_out2 = outward(out_over)
    mixer_in = inward(mixer[:3])
    y_both = to_y(send_both)
    mine_gate = rounded(added(sum_gate[0], y_gate))
    total_gate = mine_gate.astype(F32) + to_x(mine_gate).astype(F32)
    out_over_end, out_out2, mixer_in, y_both, total_gate, small = together(
        out_over_end, out_out2, mixer_in, y_both, total_gate, small
    )

    out_out3 = outward(out_over_end)
    mixer_over = across(added(mixer[:2], mixer_in[:2]))
    small = small + to_core(small)
    small = small + to_y(small)
    mixer_out = outward(added(mixer[2], mixer_over[0]))
    mine_both = rounded(added(here_both, y_both))
    total_both = mine_both.astype(F32) + to_x(mine_both).astype(F32)
    total_up, total_down = total_both[:part], total_both[part:].T
    mine = rounded(
        sum(value.astype(F32) for value in (mixer[3], mixer_out, mixer_in[2], mixer_over[1]))
    )
    other = to_x(mine)
    total = jnp.concatenate(
        [jnp.where(side == 0, mine, other), jnp.where(side == 0, other, mine)], axis=1
    ).astype(F32)
    total_taps = lax.dynamic_slice(small, (2, level * part), (3, part))
    block_out = placed(
        out_own,
        (out_pair, jnp.where(end, out_out2, out_over_end), jnp.where(end, out_out3, out_over)),
        BF16,
    )
    return (
        block_out, grad_tokens, small[0], total[:3], total_taps, total[3].T, small[1],
        total_gate, total_up, total_down,
    )


def from_behind(value, axis, steps):
    count = lax.axis_size(axis)
    initial, last = (max(0, -steps), min(count, count - steps))
    return lax.ppermute(value, axis, [(source, source + steps) for source in range(initial, last)])


def norm_backward_and_gain(grad_normed, plain, inverse, gain):
    grad_plain = grad_normed * gain
    grad_values = inverse * (
        grad_plain - plain * jnp.mean(grad_plain * plain, axis=-1, keepdims=True)
    )
    leading = tuple(range(grad_normed.ndim - 1))
    return (grad_values, jnp.sum(grad_normed * plain, axis=leading))


def local(
    tokens,
    norm_gain,
    w_in,
    conv_weight,
    convolution_out_weight,
    ffn_gain,
    w_gate,
    w_up,
    w_down,
    cotangent,
):
    input_rows = tokens.astype(jnp.float32)
    gain_one = norm_gain.astype(jnp.float32)
    gain_two = ffn_gain.astype(jnp.float32)
    taps = conv_weight.astype(jnp.float32)
    seqs, width, model = tokens.shape
    (
        complete_input_weight,
        complete_output_weight,
        feedforward_gate_weight,
        feedforward_up_weight,
        feedforward_down_weight,
    ) = (
        lax.all_gather(w_in, "shard", axis=1, tiled=True),
        lax.all_gather(convolution_out_weight, "shard", axis=1, tiled=True),
        lax.all_gather(w_gate, "shard", axis=0, tiled=True),
        lax.all_gather(w_up, "shard", axis=0, tiled=True),
        lax.all_gather(w_down, "shard", axis=1, tiled=True),
    )
    plain_one, inverse_one = norm_forward(input_rows)
    first_normalized = (plain_one * gain_one).astype(jnp.bfloat16)
    projection = jnp.einsum(
        "uiq,tqz->tuiz", first_normalized, complete_input_weight, preferred_element_type=jnp.float32
    )
    in_gate = projection[0]
    out_gate = projection[1]
    conv_input = projection[2]
    product = (in_gate * conv_input).astype(jnp.bfloat16)
    edge = from_behind(product[:, width - 2 :, :], "context", 1)
    extended = jnp.concatenate([edge, product], axis=1).astype(jnp.float32)
    recent = extended[:, 2:, :]
    previous = extended[:, 1 : width + 1, :]
    earlier = extended[:, :width, :]
    convolved = taps[0] * recent + taps[1] * previous + taps[2] * earlier
    gated_product = (out_gate * convolved).astype(jnp.bfloat16)
    partial_mixer_output = jnp.einsum(
        "zaw,wk->zak", gated_product, complete_output_weight, preferred_element_type=jnp.float32
    )
    residual_middle = input_rows + lax.psum(partial_mixer_output, "tensor")
    plain_two, inverse_two = norm_forward(residual_middle)
    second_normalized = (plain_two * gain_two).astype(jnp.bfloat16)
    gate_branch = jnp.einsum(
        "mut,tz->muz",
        second_normalized,
        feedforward_gate_weight,
        preferred_element_type=jnp.float32,
    )
    up_projection_branch = jnp.einsum(
        "mut,tz->muz", second_normalized, feedforward_up_weight, preferred_element_type=jnp.float32
    )
    sigmoid_gate = jax.nn.sigmoid(gate_branch)
    silu_gate = gate_branch * sigmoid_gate
    hidden_state = (silu_gate * up_projection_branch).astype(jnp.bfloat16)
    partial_feedforward = jnp.einsum(
        "eny,yv->env", hidden_state, feedforward_down_weight, preferred_element_type=jnp.float32
    )
    block_out = (
        residual_middle
        + lax.psum(partial_feedforward.astype(jnp.bfloat16), "tensor").astype(jnp.float32)
    ).astype(jnp.bfloat16)
    grad_out = cotangent.astype(jnp.float32)
    hidden_gradient = jnp.einsum(
        "qmn,pn->qmp", cotangent, feedforward_down_weight, preferred_element_type=jnp.float32
    )
    down_gradient = jnp.einsum(
        "eiu,eix->ux", hidden_state, cotangent, preferred_element_type=jnp.float32
    )
    gate_gradient = (
        hidden_gradient
        * up_projection_branch
        * sigmoid_gate
        * (1.0 + gate_branch * (1.0 - sigmoid_gate))
    ).astype(jnp.bfloat16)
    up_gradient = (hidden_gradient * silu_gate).astype(jnp.bfloat16)
    grad_w_gate = jnp.einsum(
        "rnj,rnt->jt", second_normalized, gate_gradient, preferred_element_type=jnp.float32
    )
    up_weight_gradient = jnp.einsum(
        "rnj,rnt->jt", second_normalized, up_gradient, preferred_element_type=jnp.float32
    )
    partial_normed_two = jnp.einsum(
        "wxo,qo->wxq", gate_gradient, feedforward_gate_weight, preferred_element_type=jnp.float32
    )
    partial_normed_two = partial_normed_two + jnp.einsum(
        "wxo,qo->wxq", up_gradient, feedforward_up_weight, preferred_element_type=jnp.float32
    )
    grad_normed_two = lax.psum(partial_normed_two, "tensor")
    grad_rows_two, gain_grad_two = norm_backward_and_gain(grad_normed_two, plain_two, inverse_two, gain_two)
    grad_middle = grad_out + grad_rows_two
    mixer_output_gradient = grad_middle.astype(jnp.bfloat16)
    grad_gated = jnp.einsum(
        "ymo,bo->ymb",
        mixer_output_gradient,
        complete_output_weight,
        preferred_element_type=jnp.float32,
    )
    out_weight_gradient = jnp.einsum(
        "miy,miq->yq", gated_product, mixer_output_gradient, preferred_element_type=jnp.float32
    )
    grad_convolved = (grad_gated * out_gate).astype(jnp.bfloat16)
    grad_out_gate = grad_gated * convolved
    grad_edge = from_behind(grad_convolved[:, :2, :], "context", -1)
    grad_extended = jnp.concatenate([grad_convolved, grad_edge], axis=1).astype(jnp.float32)
    grad_product = (
        taps[0] * grad_extended[:, :width, :]
        + taps[1] * grad_extended[:, 1 : width + 1, :]
        + taps[2] * grad_extended[:, 2:, :]
    )
    grad_local = grad_extended[:, :width, :]
    tap_grads = jnp.stack(
        [
            jnp.sum(grad_local * recent, axis=(0, 1)),
            jnp.sum(grad_local * previous, axis=(0, 1)),
            jnp.sum(grad_local * earlier, axis=(0, 1)),
        ]
    )
    projection_gradient = jnp.stack(
        [
            (grad_product * conv_input).astype(jnp.bfloat16),
            grad_out_gate.astype(jnp.bfloat16),
            (grad_product * in_gate).astype(jnp.bfloat16),
        ]
    )
    grad_w_in = jnp.einsum(
        "pxw,gpxt->gwt", first_normalized, projection_gradient, preferred_element_type=jnp.float32
    )
    partial_normed_one = jnp.einsum(
        "ireo,ivo->rev",
        projection_gradient,
        complete_input_weight,
        preferred_element_type=jnp.float32,
    )
    shard_in, shard_out, shard_gate, shard_up, shard_down = (
        lax.psum_scatter(
            grad_w_in.astype(jnp.bfloat16), "shard", scatter_dimension=1, tiled=True
        ).astype(jnp.float32),
        lax.psum_scatter(
            out_weight_gradient.astype(jnp.bfloat16), "shard", scatter_dimension=1, tiled=True
        ).astype(jnp.float32),
        lax.psum_scatter(
            grad_w_gate.astype(jnp.bfloat16), "shard", scatter_dimension=0, tiled=True
        ).astype(jnp.float32),
        lax.psum_scatter(
            up_weight_gradient.astype(jnp.bfloat16), "shard", scatter_dimension=0, tiled=True
        ).astype(jnp.float32),
        lax.psum_scatter(
            down_gradient.astype(jnp.bfloat16), "shard", scatter_dimension=1, tiled=True
        ).astype(jnp.float32),
    )
    total_in, total_out, total_gate, total_up, total_down = (
        lax.psum(shard_in.astype(jnp.bfloat16), "context").astype(jnp.float32),
        lax.psum(shard_out.astype(jnp.bfloat16), "context").astype(jnp.float32),
        lax.psum(shard_gate.astype(jnp.bfloat16), "context").astype(jnp.float32),
        lax.psum(shard_up.astype(jnp.bfloat16), "context").astype(jnp.float32),
        lax.psum(shard_down.astype(jnp.bfloat16), "context").astype(jnp.float32),
    )
    grad_normed_one = lax.psum(partial_normed_one.astype(jnp.bfloat16), "tensor").astype(
        jnp.float32
    )
    grad_rows_one, gain_grad_one = norm_backward_and_gain(grad_normed_one, plain_one, inverse_one, gain_one)
    grad_tokens = grad_middle + grad_rows_one
    total_gain_one, total_taps, total_gain_two = lax.psum(
        (gain_grad_one, tap_grads, gain_grad_two), ("shard", "context")
    )
    return (
        block_out,
        grad_tokens,
        total_gain_one,
        total_in,
        total_taps,
        total_out,
        total_gain_two,
        total_gate,
        total_up,
        total_down,
    )


def solution(mesh):
    in_specs = (
        P("shard", "context", None),
        P(),
        P(None, "shard", "tensor"),
        P(None, "tensor"),
        P("tensor", "shard"),
        P(),
        P("shard", "tensor"),
        P("shard", "tensor"),
        P("tensor", "shard"),
        P("shard", "context", None),
    )
    out_specs = (
        P("shard", "context", None),
        P("shard", "context", None),
        P(),
        P(None, "shard", "tensor"),
        P(None, "tensor"),
        P("tensor", "shard"),
        P(),
        P("shard", "tensor"),
        P("shard", "tensor"),
        P("tensor", "shard"),
    )
    sizes = mesh.shape
    by_links = (sizes["shard"], sizes["context"], sizes["tensor"]) == (4, 2, 4)
    body = local_by_links if by_links else local
    return jax.shard_map(body, mesh=mesh, in_specs=in_specs, out_specs=out_specs, check_vma=False)
```

```python
import functools

import jax
import jax.numpy as jnp
from jax import lax
from jax.experimental import pallas as pl
from jax.experimental.pallas import tpu as pltpu
from jax.sharding import PartitionSpec as P

EPSILON = 1e-05
F32 = jnp.float32
BF16 = jnp.bfloat16
MIB = 1024 * 1024
LEAD = 16


def norm_forward(values):
    inverse = lax.rsqrt(jnp.mean(values * values, axis=-1, keepdims=True) + EPSILON)
    return (values * inverse, inverse)


def norm_backward(grad_normed, plain, inverse, gain):
    grad_plain = grad_normed * gain
    return inverse * (
        grad_plain - plain * jnp.mean(grad_plain * plain, axis=-1, keepdims=True)
    )


def dot_nn(a, b):
    return lax.dot_general(a, b, (((1,), (0,)), ((), ())), preferred_element_type=F32)


def dot_nt(a, b):
    return lax.dot_general(a, b, (((1,), (1,)), ((), ())), preferred_element_type=F32)


def dot_tn(a, b):
    return lax.dot_general(a, b, (((0,), (0,)), ((), ())), preferred_element_type=F32)


def rounded(value):
    return lax.optimization_barrier(value.astype(BF16))


def shifted(value, steps):
    count = lax.axis_size("tensor")
    return lax.ppermute(value, "tensor", [(i, (i + steps) % count) for i in range(count)])


def swapped(value, axis, bit):
    count = lax.axis_size(axis)
    return lax.ppermute(value, axis, [(i, i ^ bit) for i in range(count)])


def to_core(value):
    return swapped(value, "shard", 1)


def to_y(value):
    return swapped(value, "shard", 2)


def to_x(value):
    return swapped(value, "context", 1)


def pair(value):
    return swapped(value, "tensor", 1)


def inward(value):
    return lax.ppermute(value, "tensor", [(0, 1), (3, 2)])


def outward(value):
    return lax.ppermute(value, "tensor", [(1, 0), (2, 3)])


def across(value):
    return lax.ppermute(value, "tensor", [(1, 2), (2, 1)])


def together(*values):
    return lax.optimization_barrier(values)


def added(*values):
    return sum(value.astype(F32) for value in values).astype(BF16)


def mixer_forward_kernel(ids, rows, mine, other, *rest):
    gated, weights, out_weights, own = rest[-4:]
    part = mine.shape[1]
    half = 2 * part + LEAD

    @pl.when(pl.program_id(0) == 0)
    def _():
        for bit, piece in enumerate((mine, other)):
            for far in range(2):
                start = pl.multiple_of((ids[0] ^ (bit + 2 * far)) * part, part)
                for side in range(2):
                    first = 2 * (ids[2] ^ side)
                    base = (2 * far + side) * half
                    lower = piece[base : base + part, :]
                    upper = piece[base + part : base + 2 * part, :]

                    @pl.when(first == 0)
                    def _(start=start, lower=lower, upper=upper):
                        weights[0, pl.ds(start, part), :part] = lower
                        weights[0, pl.ds(start, part), part : 2 * part] = upper

                    @pl.when(first == 2)
                    def _(start=start, lower=lower, upper=upper):
                        weights[0, pl.ds(start, part), 2 * part :] = lower
                        out_weights[pl.ds(start, part), :] = upper

    taps = mine[2 * part : half, :].astype(F32)
    values = rows[0]
    in_gate = dot_nn(values, weights[0, :, :part])
    conv_input = dot_nn(values, weights[0, :, 2 * part :])
    out_gate = dot_nn(values, weights[0, :, part : 2 * part])
    product = (in_gate * conv_input).astype(BF16).astype(F32)
    convolved = (
        taps[0:1] * product
        + taps[1:2] * pltpu.roll(product, 1, 0)
        + taps[2:3] * pltpu.roll(product, 2, 0)
    )[LEAD:]
    gated[0] = (out_gate[LEAD:] * convolved).astype(BF16)

    @pl.when(pl.program_id(0) == ids[1])
    def _():
        own[0] = in_gate.astype(BF16)
        own[1] = out_gate.astype(BF16)
        own[2] = conv_input.astype(BF16)


def mixer_forward(ids, rows, pieces, block, earlier):
    seqs, long, model = rows.shape
    width = long - LEAD
    part = pieces[0].shape[1]
    count = model // part
    specs = [pl.BlockSpec((1, long, model), lambda q, ids: (q, 0, 0))]
    specs += [pl.BlockSpec(piece.shape, lambda q, ids: (0, 0)) for piece in pieces]
    specs += [pl.BlockSpec(memory_space=pl.ANY)] * len(earlier)
    return pl.pallas_call(
        mixer_forward_kernel,
        grid_spec=pltpu.PrefetchScalarGridSpec(
            num_scalar_prefetch=1,
            grid=(seqs,),
            in_specs=specs,
            out_specs=[
                pl.BlockSpec((1, width, part), lambda q, ids: (q, 0, block)),
                pl.BlockSpec((1, model, 3 * part), lambda q, ids: (block, 0, 0)),
                pl.BlockSpec((model, part), lambda q, ids: (0, block)),
                pl.BlockSpec((3, long, part), lambda q, ids: (0, 0, block)),
            ],
        ),
        out_shape=[
            jax.ShapeDtypeStruct((seqs, width, model), BF16),
            jax.ShapeDtypeStruct((count, model, 3 * part), BF16),
            jax.ShapeDtypeStruct((model, model), BF16),
            jax.ShapeDtypeStruct((3, long, model), BF16),
        ],
        input_output_aliases={4: 0, 5: 1, 6: 2, 7: 3} if earlier else {},
        compiler_params=pltpu.CompilerParams(vmem_limit_bytes=36 * MIB),
        cost_estimate=pl.CostEstimate(flops=0, bytes_accessed=0, transcendentals=0),
        name="mixer_forward",
    )(ids, rows, *pieces, *earlier)


def feedforward_kernel(own, ids, gated, mixer, tokens, gain, cotangent, *rest):
    near, near_core, *rest = rest
    far, rest = rest[:6], rest[6:]
    outputs = rest[-8 - own : -2]
    weights, arrived = rest[-2:]
    normed, down, grad_normed, hidden, grad_gate, grad_up = outputs[:6]
    part = far[0].shape[0]
    first = pl.program_id(0) == 0

    def copies(which):
        rows = pl.ds(which * part, part)
        sources = (near.at[rows, :], near_core.at[rows, :], far[which], far[3 + which])
        for place, source in enumerate(sources):
            start = pl.multiple_of((ids[0] ^ place) * part, part)
            yield pltpu.make_async_copy(
                source,
                weights.at[which, pl.ds(start, part), :],
                arrived.at[which, place],
            )

    @pl.when(first)
    def _():
        for which in range(3):
            for copy in copies(which):
                copy.start()

    middle = tokens[0].astype(F32) + dot_nt(gated[0], mixer[...])
    if own:
        rest[-3][...] = middle
    values = (norm_forward(middle)[0] * gain[...].astype(F32)).astype(BF16)
    normed[0] = values

    @pl.when(first)
    def _():
        for which in range(3):
            for copy in copies(which):
                copy.wait()

    gate = dot_nn(values, weights[0])
    up = dot_nn(values, weights[1])
    grad_hidden = dot_nn(cotangent[0], weights[2])
    sigmoid = jax.nn.sigmoid(gate)
    silu = gate * sigmoid
    hidden_now = (silu * up).astype(BF16)
    hidden[0] = hidden_now
    gate_now = (grad_hidden * up * sigmoid * (1.0 + gate * (1.0 - sigmoid))).astype(BF16)
    up_now = (grad_hidden * silu).astype(BF16)
    grad_gate[0] = gate_now
    grad_up[0] = up_now
    grad_normed[...] = (dot_nt(gate_now, weights[0]) + dot_nt(up_now, weights[1])).astype(BF16)
    down[...] = dot_nt(hidden_now, weights[2]).astype(BF16)


def feedforward(ids, gated, mixer, tokens, gain, cotangent, places, which, earlier):
    seqs, width, model = tokens.shape
    units = places[0].shape[1]
    size = width // 2
    own = int(which == 3)

    def seq(i, ids):
        return (ids[3 + which], i, 0)

    def row(i, ids):
        return (i, 0)

    wide = jax.ShapeDtypeStruct((seqs, width, units), BF16)
    here = jax.ShapeDtypeStruct((width, model), BF16)
    first = 6 + len(places)
    return pl.pallas_call(
        functools.partial(feedforward_kernel, own),
        grid_spec=pltpu.PrefetchScalarGridSpec(
            num_scalar_prefetch=1,
            grid=(2,),
            in_specs=[
                pl.BlockSpec((1, size, model), seq),
                pl.BlockSpec((model, model), lambda i, ids: (0, 0), pipeline_mode=pl.Buffered(1)),
                pl.BlockSpec((1, size, model), seq),
                pl.BlockSpec((1, model), lambda i, ids: (0, 0)),
                pl.BlockSpec((1, size, model), seq),
            ]
            + [pl.BlockSpec(memory_space=pltpu.HBM)] * len(places)
            + [pl.BlockSpec(memory_space=pl.ANY)] * len(earlier),
            out_specs=[
                pl.BlockSpec((1, size, model), seq),
                pl.BlockSpec((size, model), row),
                pl.BlockSpec((size, model), row),
                pl.BlockSpec((1, size, units), seq),
                pl.BlockSpec((1, size, units), seq),
                pl.BlockSpec((1, size, units), seq),
            ]
            + [pl.BlockSpec((size, model), row)] * own,
            scratch_shapes=[
                pltpu.VMEM((3, model, units), BF16),
                pltpu.SemaphoreType.DMA((3, 4)),
            ],
        ),
        out_shape=[
            jax.ShapeDtypeStruct(tokens.shape, BF16),
            here,
            here,
            wide,
            wide,
            wide,
        ]
        + [jax.ShapeDtypeStruct((width, model), F32)] * own,
        input_output_aliases={first: 0, first + 1: 3, first + 2: 4, first + 3: 5} if earlier else {},
        compiler_params=pltpu.CompilerParams(vmem_limit_bytes=40 * MIB),
        cost_estimate=pl.CostEstimate(flops=0, bytes_accessed=0, transcendentals=0),
        name="feedforward",
    )(ids, gated, mixer, tokens, gain, cotangent, *places, *earlier)


def middle_gradient(parts, own, cotangent, gain):
    incoming = sum(part[...].astype(F32) for part in parts)
    plain, inverse = norm_forward(own[...])
    total = cotangent[0].astype(F32) + norm_backward(incoming, plain, inverse, gain[...].astype(F32))
    return total, jnp.sum(incoming * plain, axis=0, keepdims=True)


def edge_kernel(ids, part0, part1, part2, own, cotangent, gain, gate, out_weights, edge):
    mixed = middle_gradient((part0, part1, part2), own, cotangent, gain)[0].astype(BF16)
    edge[...] = (dot_nn(mixed, out_weights[...]) * gate[0].astype(F32)).astype(BF16)


def edge_gradient(ids, parts, own, cotangent, gain, gates, out_weights):
    width, model = own.shape
    rows = pl.BlockSpec((LEAD, model), lambda i, ids: (0, 0))
    return pl.pallas_call(
        edge_kernel,
        grid_spec=pltpu.PrefetchScalarGridSpec(
            num_scalar_prefetch=1,
            grid=(1,),
            in_specs=[
                rows, rows, rows, rows,
                pl.BlockSpec((1, LEAD, model), lambda i, ids: (ids[1], 0, 0)),
                pl.BlockSpec((1, model), lambda i, ids: (0, 0)),
                pl.BlockSpec((1, LEAD, model), lambda i, ids: (1, 1, 0)),
                pl.BlockSpec(out_weights.shape, lambda i, ids: (0, 0)),
            ],
            out_specs=rows,
        ),
        out_shape=jax.ShapeDtypeStruct((LEAD, model), BF16),
        compiler_params=pltpu.CompilerParams(vmem_limit_bytes=44 * MIB),
        cost_estimate=pl.CostEstimate(flops=0, bytes_accessed=0, transcendentals=0),
        name="edge_gradient",
    )(ids, *parts, own, cotangent, gain, gates, out_weights)


def mixer_backward_kernel(
    ids, part0, part1, part2, own, cotangent, gain, gates, out_weights, taps,
    grad_middle, grad_mixed, gain_grad, grad_convolved, grad_out_gate, tap_grads,
):
    @pl.when(pl.program_id(0) == 0)
    def _():
        here, gain_here = middle_gradient((part0, part1, part2), own, cotangent, gain)
        gain_grad[...] = gain_here
        grad_middle[...] = here
        grad_mixed[...] = here.astype(BF16)

    tap = taps[0].astype(F32)
    product = (gates[0].astype(F32) * gates[2].astype(F32)).astype(BF16).astype(F32)
    recent, previous, earlier = (
        product[LEAD:], pltpu.roll(product, 1, 0)[LEAD:], pltpu.roll(product, 2, 0)[LEAD:],
    )
    convolved = tap[0:1] * recent + tap[1:2] * previous + tap[2:3] * earlier
    grad_gated = dot_nn(grad_mixed[...], out_weights[...])
    grad_out_gate[...] = (grad_gated * convolved).astype(BF16)
    low = (grad_gated * gates[1, LEAD:, :].astype(F32)).astype(BF16)
    grad_convolved[...] = low
    low = low.astype(F32)
    tap_grads[0] = jnp.concatenate(
        [
            jnp.sum(low * recent, axis=0, keepdims=True),
            jnp.sum(low * previous, axis=0, keepdims=True),
            jnp.sum(low * earlier, axis=0, keepdims=True),
            jnp.zeros((5, low.shape[1]), F32),
        ]
    )


def mixer_backward(ids, parts, own, cotangent, gain, gates, out_weights, taps):
    width, model = own.shape
    long = gates.shape[1]
    count = taps.shape[0]
    part = model // count
    whole = pl.BlockSpec((width, model), lambda j, ids: (0, 0))
    once = pl.BlockSpec((width, model), lambda j, ids: (0, 0), pipeline_mode=pl.Buffered(1))
    line = pl.BlockSpec((1, model), lambda j, ids: (0, 0))
    column = pl.BlockSpec((width, part), lambda j, ids: (0, j))
    matrix = jax.ShapeDtypeStruct((width, model), BF16)
    return pl.pallas_call(
        mixer_backward_kernel,
        grid_spec=pltpu.PrefetchScalarGridSpec(
            num_scalar_prefetch=1,
            grid=(count,),
            in_specs=[
                once, once, once, once,
                pl.BlockSpec((1, width, model), lambda j, ids: (ids[1], 0, 0), pipeline_mode=pl.Buffered(1)),
                line,
                pl.BlockSpec((3, long, part), lambda j, ids: (0, 0, j)),
                pl.BlockSpec((model, part), lambda j, ids: (0, j)),
                pl.BlockSpec((1, LEAD, part), lambda j, ids: (j, 0, 0)),
            ],
            out_specs=[
                whole, whole, line, column, column,
                pl.BlockSpec((1, 8, part), lambda j, ids: (j, 0, 0)),
            ],
        ),
        out_shape=[
            jax.ShapeDtypeStruct((width, model), F32), matrix, jax.ShapeDtypeStruct((1, model), F32),
            matrix, matrix, jax.ShapeDtypeStruct((count, 8, part), F32),
        ],
        compiler_params=pltpu.CompilerParams(vmem_limit_bytes=44 * MIB),
        cost_estimate=pl.CostEstimate(flops=0, bytes_accessed=0, transcendentals=0),
        name="mixer_backward",
    )(ids, *parts, own, cotangent, gain, gates, out_weights, taps)


def input_backward_kernel(
    ids, grad_convolved, edge, gates, grad_out_gate, taps, weights, grad_middle, tokens, gain,
    grad_first, grad_third, grad_tokens, gain_grad, total,
):
    block = pl.program_id(0)
    width = grad_convolved.shape[0]
    tap = taps[0].astype(F32)
    longer = jnp.concatenate([grad_convolved[...], edge[...]]).astype(F32)
    count = longer.shape[0]
    grad_product = (
        tap[0:1] * longer
        + tap[1:2] * pltpu.roll(longer, count - 1, 0)
        + tap[2:3] * pltpu.roll(longer, count - 2, 0)
    )[:width]
    first = (grad_product * gates[2, LEAD:, :].astype(F32)).astype(BF16)
    third = (grad_product * gates[0, LEAD:, :].astype(F32)).astype(BF16)
    grad_first[...] = first
    grad_third[...] = third
    here = dot_nt(jnp.concatenate([first, grad_out_gate[...], third], axis=1), weights[0])

    @pl.when(block == 0)
    def _():
        total[...] = here

    @pl.when(block > 0)
    def _():
        total[...] += here

    @pl.when(block == pl.num_programs(0) - 1)
    def _():
        incoming = total[...]
        plain, inverse = norm_forward(tokens[0].astype(F32))
        gain_grad[...] = jnp.sum(incoming * plain, axis=0, keepdims=True)
        grad_tokens[...] = (
            grad_middle[...] + norm_backward(incoming, plain, inverse, gain[...].astype(F32))
        ).astype(BF16)


def input_backward(ids, grad_convolved, edge, gates, grad_out_gate, taps, weights, grad_middle, tokens, gain):
    width, model = grad_middle.shape
    long = gates.shape[1]
    count = taps.shape[0]
    part = model // count
    once = pl.BlockSpec((width, model), lambda j, ids: (0, 0), pipeline_mode=pl.Buffered(1))
    whole = pl.BlockSpec((width, model), lambda j, ids: (0, 0))
    line = pl.BlockSpec((1, model), lambda j, ids: (0, 0))
    column = pl.BlockSpec((width, part), lambda j, ids: (0, j))
    matrix = jax.ShapeDtypeStruct((width, model), BF16)
    return pl.pallas_call(
        input_backward_kernel,
        grid_spec=pltpu.PrefetchScalarGridSpec(
            num_scalar_prefetch=1,
            grid=(count,),
            in_specs=[
                column,
                pl.BlockSpec((LEAD, part), lambda j, ids: (0, j)),
                pl.BlockSpec((3, long, part), lambda j, ids: (0, 0, j)),
                column,
                pl.BlockSpec((1, LEAD, part), lambda j, ids: (j, 0, 0)),
                pl.BlockSpec((1, model, 3 * part), lambda j, ids: (j, 0, 0)),
                once,
                pl.BlockSpec((1, width, model), lambda j, ids: (ids[1], 0, 0), pipeline_mode=pl.Buffered(1)),
                line,
            ],
            out_specs=[column, column, whole, line],
            scratch_shapes=[pltpu.VMEM((width, model), F32)],
        ),
        out_shape=[matrix, matrix, matrix, jax.ShapeDtypeStruct((1, model), F32)],
        compiler_params=pltpu.CompilerParams(vmem_limit_bytes=44 * MIB),
        cost_estimate=pl.CostEstimate(flops=0, bytes_accessed=0, transcendentals=0),
        name="input_backward",
    )(ids, grad_convolved, edge, gates, grad_out_gate, taps, weights, grad_middle, tokens, gain)


def split_rows(ids, g):
    return ids[7 + g]


def feedforward_gradient_kernel(ids, left, right, send, keep):
    result = dot_tn(left[...], right[...]).astype(BF16)

    @pl.when(pl.program_id(0) < 2)
    def _():
        send[0] = result

    @pl.when(pl.program_id(0) >= 2)
    def _():
        keep[0] = result


def feedforward_gradient(ids, left, right):
    tokens, model = left.shape
    units = right.shape[1]
    part = model // 4
    shape = jax.ShapeDtypeStruct((2, part, units), BF16)
    return pl.pallas_call(
        feedforward_gradient_kernel,
        grid_spec=pltpu.PrefetchScalarGridSpec(
            num_scalar_prefetch=1,
            grid=(4,),
            in_specs=[
                pl.BlockSpec((tokens, part), lambda g, ids: (0, split_rows(ids, g))),
                pl.BlockSpec((tokens, units), lambda g, ids: (0, 0), pipeline_mode=pl.Buffered(1)),
            ],
            out_specs=[
                pl.BlockSpec((1, part, units), lambda g, ids: (jnp.minimum(g, 1), 0, 0)),
                pl.BlockSpec((1, part, units), lambda g, ids: (jnp.maximum(g - 2, 0), 0, 0)),
            ],
        ),
        out_shape=[shape, shape],
        compiler_params=pltpu.CompilerParams(vmem_limit_bytes=32 * MIB),
        cost_estimate=pl.CostEstimate(flops=0, bytes_accessed=0, transcendentals=0),
        name="feedforward_gradient",
    )(ids, left, right)


def mixer_gradient_kernel(ids, rows, mixed, first, second, third, gated, send, keep):
    part = mixed.shape[1]
    here = []
    for left, right in (
        (rows[0, LEAD:], first[...]),
        (rows[0, LEAD:], second[...]),
        (rows[0, LEAD:], third[...]),
        (mixed[...], gated[0]),
    ):
        here.append(dot_tn(left, right).astype(BF16))

    def store(out):
        for matrix, value in enumerate(here):
            for block in range(4):
                for upper in range(2):
                    out[0, ids[2] ^ upper, ids[11 + block], matrix] = value[
                        upper * part // 2 : (upper + 1) * part // 2, block * part : (block + 1) * part
                    ]

    @pl.when(pl.program_id(0) < 2)
    def _():
        store(send)

    @pl.when(pl.program_id(0) >= 2)
    def _():
        store(keep)


def mixer_gradient(ids, rows, mixed, first, second, third, gated):
    width, model = mixed.shape
    long = rows.shape[1]
    part = model // 4
    shape = jax.ShapeDtypeStruct((2, 2, 4, 4, part // 2, part), BF16)
    block = (1, 2, 4, 4, part // 2, part)
    whole = pl.BlockSpec((width, model), lambda g, ids: (0, 0))
    return pl.pallas_call(
        mixer_gradient_kernel,
        grid_spec=pltpu.PrefetchScalarGridSpec(
            num_scalar_prefetch=1,
            grid=(4,),
            in_specs=[
                pl.BlockSpec((1, long, part), lambda g, ids: (ids[1], 0, split_rows(ids, g))),
                pl.BlockSpec((width, part), lambda g, ids: (0, split_rows(ids, g))),
                whole, whole, whole,
                pl.BlockSpec((1, width, model), lambda g, ids: (ids[1], 0, 0)),
            ],
            out_specs=[
                pl.BlockSpec(block, lambda g, ids: (jnp.minimum(g, 1), 0, 0, 0, 0, 0)),
                pl.BlockSpec(block, lambda g, ids: (jnp.maximum(g - 2, 0), 0, 0, 0, 0, 0)),
            ],
        ),
        out_shape=[shape, shape],
        compiler_params=pltpu.CompilerParams(vmem_limit_bytes=40 * MIB),
        cost_estimate=pl.CostEstimate(flops=0, bytes_accessed=0, transcendentals=0),
        name="mixer_gradient",
    )(ids, rows, mixed, first, second, third, gated)


def local_by_links(
    tokens, norm_gain, w_in, conv_weight, convolution_out_weight, ffn_gain, w_gate, w_up, w_down, cotangent
):
    seqs, width, model = tokens.shape
    part = w_in.shape[1]
    units = w_gate.shape[1]
    shard, side, level = (lax.axis_index(name) for name in ("shard", "context", "tensor"))
    end = jnp.logical_or(level == 0, level == 3)
    order = [
        jnp.where(level < 2, 3, 0), jnp.where(level < 2, 2, 1), level ^ 1, level,
    ]
    place = [sum(jnp.where((level + block) % 4 == order[k], k, 0) for k in range(4)) for block in range(4)]
    ids = jnp.stack(
        [shard, level, side] + order + [shard ^ 1, shard ^ 3, shard, shard ^ 2] + place
    ).astype(jnp.int32)
    gain_one = norm_gain.reshape(1, model)
    gain_two = ffn_gain.reshape(1, model)
    def placed(own, others, dtype):
        out = jnp.zeros((seqs, width, model), dtype)
        for bits, block in enumerate((own,) + others):
            out = lax.dynamic_update_slice(out, block.astype(dtype)[None], (level ^ bits, 0, 0))
        return out

    taps_near = jnp.concatenate([conv_weight, jnp.zeros((LEAD - 3, part), BF16)])
    near = jnp.concatenate(
        [w_in[0], w_in[1], taps_near, w_in[2], convolution_out_weight.T, taps_near]
    )
    half = near.shape[0] // 2

    def sides(value):
        return [lax.dynamic_slice_in_dim(value, (side ^ bit) * half, half, 0) for bit in range(2)]

    near, near_side, near_else = together(near, *sides(near))
    far = to_y(near)
    near_right, near_left = shifted(near_side, -1), shifted(near_side, 1)
    edge = lax.ppermute(tokens[:, width - 2 :, :], "context", [(0, 1)])
    w_down = w_down.T
    feed = jnp.concatenate([w_gate, w_up, w_down])
    far, near_right, near_left, edge, feed, near_side, near_else, w_gate, w_up, w_down = together(
        far, near_right, near_left, edge, feed, near_side, near_else, w_gate, w_up, w_down
    )

    far_side, far_else = sides(far)
    far_right, far_left = shifted(far_side, -1), shifted(far_side, 1)
    near_over = to_x(jnp.concatenate([near_right, near_left]))
    far_gate = to_y(w_gate)
    mine = together(jnp.concatenate([near_side, near_else, far_side, far_else]))[0]
    other = to_core(mine)
    rows = jnp.concatenate([jnp.zeros((seqs, LEAD - 2, model), BF16), edge, tokens], axis=1).astype(F32)
    rows = (norm_forward(rows)[0] * gain_one.astype(F32)).astype(BF16)
    state = mixer_forward(ids, rows, (mine, other), 0, ())
    far_right, far_left, near_over, near_right, near_left, rows, feed, w_up, w_down, far_gate, *state = together(
        far_right, far_left, near_over, near_right, near_left, rows, feed, w_up, w_down, far_gate, *state
    )

    near_far, far_far = shifted(near_right, -1), shifted(far_left, 1)
    far_over = to_x(jnp.concatenate([far_right, far_left]))
    far_up = to_y(w_up)
    feed_core = to_core(feed)
    near_far, far_far, far_over, feed_core, far_up, w_down, *state = together(
        near_far, far_far, far_over, feed_core, far_up, w_down, *state
    )

    last_over = to_x(jnp.concatenate([near_far, far_far]))
    far_down = to_y(w_down)
    for block, rows_of, (a, b) in (
        (1, slice(None, half), (near_right, far_right)),
        (3, slice(half, None), (near_left, far_left)),
    ):
        mine = together(jnp.concatenate([a, near_over[rows_of], b, far_over[rows_of]]))[0]
        state = mixer_forward(ids, rows, (mine, to_core(mine)), block, state)
    last_over, far_down, far_gate, far_up, *state = together(
        last_over, far_down, far_gate, far_up, *state
    )

    mine = together(jnp.concatenate([near_far, last_over[:half], far_far, last_over[half:]]))[0]
    state = mixer_forward(ids, rows, (mine, to_core(mine)), 2, state)
    gated, weights, out_weights, gates = state
    far_all = (far_gate, far_up, far_down)
    core_all = [to_core(value) for value in far_all]
    gated, weights, out_weights, gates, *core_all = together(gated, weights, out_weights, gates, *core_all)
    places = (feed, feed_core, *far_all, *core_all)
    taps = jnp.stack([near_side[2 * part :], near_right[2 * part :], near_far[2 * part :], near_left[2 * part :]])

    def forward(which, earlier):
        normed, down, grad, *wide = feedforward(
            ids, gated, out_weights, tokens, gain_two, cotangent, places, which, earlier
        )
        return down, grad, (normed, *wide[:3]), wide[3:]

    down0, grad0, done, _ = forward(0, ())
    down0, grad0, *done = together(down0, grad0, *done)

    grad_pair0 = pair(grad0)
    down1, grad1, done, _ = forward(1, tuple(done))
    grad_pair0, down1, grad1, *done = together(grad_pair0, down1, grad1, *done)

    grad_pair1 = pair(grad1)
    grad_over0 = across(added(grad0, grad_pair0))
    down2, grad2, done, _ = forward(2, tuple(done))
    grad_pair1, grad_over0, down2, grad2, *done = together(grad_pair1, grad_over0, down2, grad2, *done)

    grad_pair2 = pair(added(grad2, grad_over0))
    grad_over1 = across(added(grad1, grad_pair1))
    down3, grad3, done, (middle_own,) = forward(3, tuple(done))
    normed, hidden, grad_gate, grad_up = (v.reshape(seqs * width, v.shape[2]) for v in done)
    grad_pair2, grad_over1, grad3, normed, hidden, grad_gate, grad_up, down0 = together(
        grad_pair2, grad_over1, grad3, normed, hidden, grad_gate, grad_up, down0
    )

    down_pair0 = pair(down0)
    grad_parts = (grad3, grad_pair2, grad_over1)
    edge = edge_gradient(ids, grad_parts, middle_own, cotangent, gain_two, gates, out_weights)
    edge = lax.ppermute(edge, "context", [(1, 0)])
    grad_middle, grad_mixed, gain_two_grad, grad_convolved, grad_out_gate, tap_grads = mixer_backward(
        ids, grad_parts, middle_own, cotangent, gain_two, gates, out_weights, taps
    )
    edge, grad_convolved = together(edge, grad_convolved)
    grad_first, grad_third, tokens_own, gain_one_grad = input_backward(
        ids, grad_convolved, edge, gates, grad_out_gate, taps, weights, grad_middle, tokens, gain_one
    )
    (
        down_pair0, tokens_own, grad_first, grad_third, grad_mixed, gain_one_grad, normed, hidden, grad_gate, grad_up,
    ) = together(
        down_pair0, tokens_own, grad_first, grad_third, grad_mixed, gain_one_grad, normed, hidden, grad_gate, grad_up,
    )

    tokens_pair = pair(tokens_own)
    tokens_over = across(tokens_own)
    send_mixer, keep_mixer = mixer_gradient(
        ids, rows, grad_mixed, grad_first, grad_out_gate, grad_third, gated
    )
    tap_rows = tap_grads[:, :3].transpose(1, 0, 2)
    tap_rows = jnp.roll(tap_rows, level, axis=1).reshape(3, model)
    small = jnp.concatenate([gain_one_grad, gain_two_grad, tap_rows, jnp.zeros((3, model), F32)])
    small = small + swapped(small, "tensor", 1)
    tokens_pair, tokens_over, send_mixer, keep_mixer, hidden, grad_gate, grad_up, small, down0, down1, down2 = together(
        tokens_pair, tokens_over, send_mixer, keep_mixer, hidden, grad_gate, grad_up, small, down0, down1, down2
    )

    mixed_pair1 = pair(jnp.where(end, down1, tokens_over))
    tokens_over_end = across(tokens_pair)
    core_mixer = to_core(send_mixer)
    send_gate, keep_gate = feedforward_gradient(ids, normed, grad_gate)
    send_up, keep_up = feedforward_gradient(ids, normed, grad_up)
    small = small + swapped(small, "tensor", 2)
    down_sum0 = added(down0, down_pair0)
    (
        mixed_pair1, tokens_over_end, core_mixer, send_gate, keep_gate, send_up, keep_up, small, down_sum0, hidden,
    ) = together(
        mixed_pair1, tokens_over_end, core_mixer, send_gate, keep_gate, send_up, keep_up, small, down_sum0, hidden,
    )

    mixed_pair2 = pair(jnp.where(end, down2, tokens_over_end))
    down_over0 = across(down_sum0)
    core_gate = to_core(send_gate)
    small = small + to_x(small)
    send_down, keep_down = feedforward_gradient(ids, cotangent.reshape(seqs * width, model), hidden)
    sum_mixer = added(keep_mixer, core_mixer)
    low, high = slice(None, part // 4), slice(part // 4, None)
    here_low, send_low = sum_mixer[0, :, :, :, low], sum_mixer[1, :, :, :, low]
    here_high, send_high = sum_mixer[:, 0, :, :, high], sum_mixer[:, 1, :, :, high]
    down_sum1 = added(down1, mixed_pair1)
    (
        mixed_pair2, down_over0, core_gate, send_up, send_down, keep_down, here_low, send_low, here_high,
        send_high, down_sum1, small, tokens_own,
    ) = together(
        mixed_pair2, down_over0, core_gate, send_up, send_down, keep_down, here_low, send_low, here_high,
        send_high, down_sum1, small, tokens_own,
    )

    down_pair3 = pair(added(down2, down_over0))
    down_over1 = across(down_sum1)
    y_low, x_high = to_y(send_low), to_x(send_high)
    grad_tokens = placed(
        tokens_own,
        (
            tokens_pair,
            jnp.where(end, mixed_pair1, tokens_over_end),
            jnp.where(end, mixed_pair2, tokens_over),
        ),
        F32,
    )
    sum_gate = added(keep_gate, core_gate)
    core_both = to_core(jnp.concatenate([send_up, send_down]))
    keep_both = jnp.concatenate([keep_up, keep_down])
    down_pair3, down_over1, y_low, x_high, grad_tokens, sum_gate, core_both, keep_both, small = together(
        down_pair3, down_over1, y_low, x_high, grad_tokens, sum_gate, core_both, keep_both, small
    )

    out_own = rounded(
        middle_own
        + down3.astype(F32)
        + jnp.where(end, down_pair3, mixed_pair2).astype(F32)
        + down_over1.astype(F32)
    )
    out_pair = pair(out_own)
    out_over = across(out_own)
    half_low = added(here_low, y_low)
    half_high = added(here_high, x_high)
    x_low, y_high = to_x(half_low[1]), to_y(half_high[1])
    mixer = jnp.concatenate([added(half_low[0], x_low), added(half_high[0], y_high)], axis=2)
    y_gate = to_y(sum_gate[1])
    sum_both = added(keep_both, core_both)
    send_both = jnp.concatenate([sum_both[1], sum_both[3]])
    here_both = jnp.concatenate([sum_both[0], sum_both[2]])
    out_pair, out_over, mixer, send_both, here_both, y_gate, small = together(
        out_pair, out_over, mixer, send_both, here_both, y_gate, small
    )

    out_over_end = across(out_pair)
    out_out2 = outward(out_over)
    mixer_in = inward(mixer[:3])
    y_both = to_y(send_both)
    mine_gate = rounded(added(sum_gate[0], y_gate))
    total_gate = mine_gate.astype(F32) + to_x(mine_gate).astype(F32)
    out_over_end, out_out2, mixer_in, y_both, total_gate, small = together(
        out_over_end, out_out2, mixer_in, y_both, total_gate, small
    )

    out_out3 = outward(out_over_end)
    mixer_over = across(added(mixer[:2], mixer_in[:2]))
    small = small + to_core(small)
    small = small + to_y(small)
    mixer_out = outward(added(mixer[2], mixer_over[0]))
    mine_both = rounded(added(here_both, y_both))
    total_both = mine_both.astype(F32) + to_x(mine_both).astype(F32)
    total_up, total_down = total_both[:part], total_both[part:].T
    mine = rounded(
        sum(value.astype(F32) for value in (mixer[3], mixer_out, mixer_in[2], mixer_over[1]))
    )
    other = to_x(mine)
    total = jnp.concatenate(
        [jnp.where(side == 0, mine, other), jnp.where(side == 0, other, mine)], axis=1
    ).astype(F32)
    total_taps = lax.dynamic_slice(small, (2, level * part), (3, part))
    block_out = placed(
        out_own,
        (out_pair, jnp.where(end, out_out2, out_over_end), jnp.where(end, out_out3, out_over)),
        BF16,
    )
    return (
        block_out, grad_tokens, small[0], total[:3], total_taps, total[3].T, small[1],
        total_gate, total_up, total_down,
    )


def from_behind(value, axis, steps):
    count = lax.axis_size(axis)
    initial, last = (max(0, -steps), min(count, count - steps))
    return lax.ppermute(value, axis, [(source, source + steps) for source in range(initial, last)])


def norm_backward_and_gain(grad_normed, plain, inverse, gain):
    grad_plain = grad_normed * gain
    grad_values = inverse * (
        grad_plain - plain * jnp.mean(grad_plain * plain, axis=-1, keepdims=True)
    )
    leading = tuple(range(grad_normed.ndim - 1))
    return (grad_values, jnp.sum(grad_normed * plain, axis=leading))


def local(
    tokens,
    norm_gain,
    w_in,
    conv_weight,
    convolution_out_weight,
    ffn_gain,
    w_gate,
    w_up,
    w_down,
    cotangent,
):
    input_rows = tokens.astype(jnp.float32)
    gain_one = norm_gain.astype(jnp.float32)
    gain_two = ffn_gain.astype(jnp.float32)
    taps = conv_weight.astype(jnp.float32)
    seqs, width, model = tokens.shape
    (
        complete_input_weight,
        complete_output_weight,
        feedforward_gate_weight,
        feedforward_up_weight,
        feedforward_down_weight,
    ) = (
        lax.all_gather(w_in, "shard", axis=1, tiled=True),
        lax.all_gather(convolution_out_weight, "shard", axis=1, tiled=True),
        lax.all_gather(w_gate, "shard", axis=0, tiled=True),
        lax.all_gather(w_up, "shard", axis=0, tiled=True),
        lax.all_gather(w_down, "shard", axis=1, tiled=True),
    )
    plain_one, inverse_one = norm_forward(input_rows)
    first_normalized = (plain_one * gain_one).astype(jnp.bfloat16)
    projection = jnp.einsum(
        "uiq,tqz->tuiz", first_normalized, complete_input_weight, preferred_element_type=jnp.float32
    )
    in_gate = projection[0]
    out_gate = projection[1]
    conv_input = projection[2]
    product = (in_gate * conv_input).astype(jnp.bfloat16)
    edge = from_behind(product[:, width - 2 :, :], "context", 1)
    extended = jnp.concatenate([edge, product], axis=1).astype(jnp.float32)
    recent = extended[:, 2:, :]
    previous = extended[:, 1 : width + 1, :]
    earlier = extended[:, :width, :]
    convolved = taps[0] * recent + taps[1] * previous + taps[2] * earlier
    gated_product = (out_gate * convolved).astype(jnp.bfloat16)
    partial_mixer_output = jnp.einsum(
        "zaw,wk->zak", gated_product, complete_output_weight, preferred_element_type=jnp.float32
    )
    residual_middle = input_rows + lax.psum(partial_mixer_output, "tensor")
    plain_two, inverse_two = norm_forward(residual_middle)
    second_normalized = (plain_two * gain_two).astype(jnp.bfloat16)
    gate_branch = jnp.einsum(
        "mut,tz->muz",
        second_normalized,
        feedforward_gate_weight,
        preferred_element_type=jnp.float32,
    )
    up_projection_branch = jnp.einsum(
        "mut,tz->muz", second_normalized, feedforward_up_weight, preferred_element_type=jnp.float32
    )
    sigmoid_gate = jax.nn.sigmoid(gate_branch)
    silu_gate = gate_branch * sigmoid_gate
    hidden_state = (silu_gate * up_projection_branch).astype(jnp.bfloat16)
    partial_feedforward = jnp.einsum(
        "eny,yv->env", hidden_state, feedforward_down_weight, preferred_element_type=jnp.float32
    )
    block_out = (
        residual_middle
        + lax.psum(partial_feedforward.astype(jnp.bfloat16), "tensor").astype(jnp.float32)
    ).astype(jnp.bfloat16)
    grad_out = cotangent.astype(jnp.float32)
    hidden_gradient = jnp.einsum(
        "qmn,pn->qmp", cotangent, feedforward_down_weight, preferred_element_type=jnp.float32
    )
    down_gradient = jnp.einsum(
        "eiu,eix->ux", hidden_state, cotangent, preferred_element_type=jnp.float32
    )
    gate_gradient = (
        hidden_gradient
        * up_projection_branch
        * sigmoid_gate
        * (1.0 + gate_branch * (1.0 - sigmoid_gate))
    ).astype(jnp.bfloat16)
    up_gradient = (hidden_gradient * silu_gate).astype(jnp.bfloat16)
    grad_w_gate = jnp.einsum(
        "rnj,rnt->jt", second_normalized, gate_gradient, preferred_element_type=jnp.float32
    )
    up_weight_gradient = jnp.einsum(
        "rnj,rnt->jt", second_normalized, up_gradient, preferred_element_type=jnp.float32
    )
    partial_normed_two = jnp.einsum(
        "wxo,qo->wxq", gate_gradient, feedforward_gate_weight, preferred_element_type=jnp.float32
    )
    partial_normed_two = partial_normed_two + jnp.einsum(
        "wxo,qo->wxq", up_gradient, feedforward_up_weight, preferred_element_type=jnp.float32
    )
    grad_normed_two = lax.psum(partial_normed_two, "tensor")
    grad_rows_two, gain_grad_two = norm_backward_and_gain(grad_normed_two, plain_two, inverse_two, gain_two)
    grad_middle = grad_out + grad_rows_two
    mixer_output_gradient = grad_middle.astype(jnp.bfloat16)
    grad_gated = jnp.einsum(
        "ymo,bo->ymb",
        mixer_output_gradient,
        complete_output_weight,
        preferred_element_type=jnp.float32,
    )
    out_weight_gradient = jnp.einsum(
        "miy,miq->yq", gated_product, mixer_output_gradient, preferred_element_type=jnp.float32
    )
    grad_convolved = (grad_gated * out_gate).astype(jnp.bfloat16)
    grad_out_gate = grad_gated * convolved
    grad_edge = from_behind(grad_convolved[:, :2, :], "context", -1)
    grad_extended = jnp.concatenate([grad_convolved, grad_edge], axis=1).astype(jnp.float32)
    grad_product = (
        taps[0] * grad_extended[:, :width, :]
        + taps[1] * grad_extended[:, 1 : width + 1, :]
        + taps[2] * grad_extended[:, 2:, :]
    )
    grad_local = grad_extended[:, :width, :]
    tap_grads = jnp.stack(
        [
            jnp.sum(grad_local * recent, axis=(0, 1)),
            jnp.sum(grad_local * previous, axis=(0, 1)),
            jnp.sum(grad_local * earlier, axis=(0, 1)),
        ]
    )
    projection_gradient = jnp.stack(
        [
            (grad_product * conv_input).astype(jnp.bfloat16),
            grad_out_gate.astype(jnp.bfloat16),
            (grad_product * in_gate).astype(jnp.bfloat16),
        ]
    )
    grad_w_in = jnp.einsum(
        "pxw,gpxt->gwt", first_normalized, projection_gradient, preferred_element_type=jnp.float32
    )
    partial_normed_one = jnp.einsum(
        "ireo,ivo->rev",
        projection_gradient,
        complete_input_weight,
        preferred_element_type=jnp.float32,
    )
    shard_in, shard_out, shard_gate, shard_up, shard_down = (
        lax.psum_scatter(
            grad_w_in.astype(jnp.bfloat16), "shard", scatter_dimension=1, tiled=True
        ).astype(jnp.float32),
        lax.psum_scatter(
            out_weight_gradient.astype(jnp.bfloat16), "shard", scatter_dimension=1, tiled=True
        ).astype(jnp.float32),
        lax.psum_scatter(
            grad_w_gate.astype(jnp.bfloat16), "shard", scatter_dimension=0, tiled=True
        ).astype(jnp.float32),
        lax.psum_scatter(
            up_weight_gradient.astype(jnp.bfloat16), "shard", scatter_dimension=0, tiled=True
        ).astype(jnp.float32),
        lax.psum_scatter(
            down_gradient.astype(jnp.bfloat16), "shard", scatter_dimension=1, tiled=True
        ).astype(jnp.float32),
    )
    total_in, total_out, total_gate, total_up, total_down = (
        lax.psum(shard_in.astype(jnp.bfloat16), "context").astype(jnp.float32),
        lax.psum(shard_out.astype(jnp.bfloat16), "context").astype(jnp.float32),
        lax.psum(shard_gate.astype(jnp.bfloat16), "context").astype(jnp.float32),
        lax.psum(shard_up.astype(jnp.bfloat16), "context").astype(jnp.float32),
        lax.psum(shard_down.astype(jnp.bfloat16), "context").astype(jnp.float32),
    )
    grad_normed_one = lax.psum(partial_normed_one.astype(jnp.bfloat16), "tensor").astype(
        jnp.float32
    )
    grad_rows_one, gain_grad_one = norm_backward_and_gain(grad_normed_one, plain_one, inverse_one, gain_one)
    grad_tokens = grad_middle + grad_rows_one
    total_gain_one, total_taps, total_gain_two = lax.psum(
        (gain_grad_one, tap_grads, gain_grad_two), ("shard", "context")
    )
    return (
        block_out,
        grad_tokens,
        total_gain_one,
        total_in,
        total_taps,
        total_out,
        total_gain_two,
        total_gate,
        total_up,
        total_down,
    )


def solution(mesh):
    in_specs = (
        P("shard", "context", None),
        P(),
        P(None, "shard", "tensor"),
        P(None, "tensor"),
        P("tensor", "shard"),
        P(),
        P("shard", "tensor"),
        P("shard", "tensor"),
        P("tensor", "shard"),
        P("shard", "context", None),
    )
    out_specs = (
        P("shard", "context", None),
        P("shard", "context", None),
        P(),
        P(None, "shard", "tensor"),
        P(None, "tensor"),
        P("tensor", "shard"),
        P(),
        P("shard", "tensor"),
        P("shard", "tensor"),
        P("tensor", "shard"),
    )
    sizes = mesh.shape
    by_links = (sizes["shard"], sizes["context"], sizes["tensor"]) == (4, 2, 4)
    body = local_by_links if by_links else local
    return jax.shard_map(body, mesh=mesh, in_specs=in_specs, out_specs=out_specs, check_vma=False)
```

```python
import functools

import jax
import jax.numpy as jnp
from jax import lax
from jax.experimental import pallas as pl
from jax.experimental.pallas import tpu as pltpu
from jax.sharding import PartitionSpec as P

EPSILON = 1e-05
F32 = jnp.float32
BF16 = jnp.bfloat16
MIB = 1024 * 1024
LEAD = 16


def norm_forward(values):
    inverse = lax.rsqrt(jnp.mean(values * values, axis=-1, keepdims=True) + EPSILON)
    return (values * inverse, inverse)


def norm_backward(grad_normed, plain, inverse, gain):
    grad_plain = grad_normed * gain
    return inverse * (
        grad_plain - plain * jnp.mean(grad_plain * plain, axis=-1, keepdims=True)
    )


def dot_nn(a, b):
    return lax.dot_general(a, b, (((1,), (0,)), ((), ())), preferred_element_type=F32)


def dot_nt(a, b):
    return lax.dot_general(a, b, (((1,), (1,)), ((), ())), preferred_element_type=F32)


def dot_tn(a, b):
    return lax.dot_general(a, b, (((0,), (0,)), ((), ())), preferred_element_type=F32)


def rounded(value):
    return lax.optimization_barrier(value.astype(BF16))


def shifted(value, steps):
    count = lax.axis_size("tensor")
    return lax.ppermute(value, "tensor", [(i, (i + steps) % count) for i in range(count)])


def swapped(value, axis, bit):
    count = lax.axis_size(axis)
    return lax.ppermute(value, axis, [(i, i ^ bit) for i in range(count)])


def to_core(value):
    return swapped(value, "shard", 1)


def to_y(value):
    return swapped(value, "shard", 2)


def to_x(value):
    return swapped(value, "context", 1)


def pair(value):
    return swapped(value, "tensor", 1)


def inward(value):
    return lax.ppermute(value, "tensor", [(0, 1), (3, 2)])


def outward(value):
    return lax.ppermute(value, "tensor", [(1, 0), (2, 3)])


def across(value):
    return lax.ppermute(value, "tensor", [(1, 2), (2, 1)])


def together(*values):
    return lax.optimization_barrier(values)


def added(*values):
    return sum(value.astype(F32) for value in values).astype(BF16)


def mixer_forward_kernel(ids, rows, mine, other, *rest):
    gated, weights, out_weights, own = rest[-4:]
    part = mine.shape[1]
    half = 2 * part + LEAD

    @pl.when(pl.program_id(0) == 0)
    def _():
        for bit, piece in enumerate((mine, other)):
            for far in range(2):
                start = pl.multiple_of((ids[0] ^ (bit + 2 * far)) * part, part)
                for side in range(2):
                    first = 2 * (ids[2] ^ side)
                    base = (2 * far + side) * half
                    lower = piece[base : base + part, :]
                    upper = piece[base + part : base + 2 * part, :]

                    @pl.when(first == 0)
                    def _(start=start, lower=lower, upper=upper):
                        weights[0, pl.ds(start, part), :part] = lower
                        weights[0, pl.ds(start, part), part : 2 * part] = upper

                    @pl.when(first == 2)
                    def _(start=start, lower=lower, upper=upper):
                        weights[0, pl.ds(start, part), 2 * part :] = lower
                        out_weights[pl.ds(start, part), :] = upper

    taps = mine[2 * part : half, :].astype(F32)
    values = rows[0]
    in_gate = dot_nn(values, weights[0, :, :part])
    conv_input = dot_nn(values, weights[0, :, 2 * part :])
    out_gate = dot_nn(values, weights[0, :, part : 2 * part])
    product = (in_gate * conv_input).astype(BF16).astype(F32)
    convolved = (
        taps[0:1] * product
        + taps[1:2] * pltpu.roll(product, 1, 0)
        + taps[2:3] * pltpu.roll(product, 2, 0)
    )[LEAD:]
    gated[0] = (out_gate[LEAD:] * convolved).astype(BF16)

    @pl.when(pl.program_id(0) == ids[1])
    def _():
        own[0] = in_gate.astype(BF16)
        own[1] = out_gate.astype(BF16)
        own[2] = conv_input.astype(BF16)


def mixer_forward(ids, rows, pieces, block, earlier):
    seqs, long, model = rows.shape
    width = long - LEAD
    part = pieces[0].shape[1]
    count = model // part
    specs = [pl.BlockSpec((1, long, model), lambda q, ids: (q, 0, 0))]
    specs += [pl.BlockSpec(piece.shape, lambda q, ids: (0, 0)) for piece in pieces]
    specs += [pl.BlockSpec(memory_space=pl.ANY)] * len(earlier)
    return pl.pallas_call(
        mixer_forward_kernel,
        grid_spec=pltpu.PrefetchScalarGridSpec(
            num_scalar_prefetch=1,
            grid=(seqs,),
            in_specs=specs,
            out_specs=[
                pl.BlockSpec((1, width, part), lambda q, ids: (q, 0, block)),
                pl.BlockSpec((1, model, 3 * part), lambda q, ids: (block, 0, 0)),
                pl.BlockSpec((model, part), lambda q, ids: (0, block)),
                pl.BlockSpec((3, long, part), lambda q, ids: (0, 0, block)),
            ],
        ),
        out_shape=[
            jax.ShapeDtypeStruct((seqs, width, model), BF16),
            jax.ShapeDtypeStruct((count, model, 3 * part), BF16),
            jax.ShapeDtypeStruct((model, model), BF16),
            jax.ShapeDtypeStruct((3, long, model), BF16),
        ],
        input_output_aliases={4: 0, 5: 1, 6: 2, 7: 3} if earlier else {},
        compiler_params=pltpu.CompilerParams(vmem_limit_bytes=36 * MIB),
        cost_estimate=pl.CostEstimate(flops=0, bytes_accessed=0, transcendentals=0),
        name="mixer_forward",
    )(ids, rows, *pieces, *earlier)


def feedforward_kernel(own, ids, gated, mixer, tokens, gain, cotangent, *rest):
    near, near_core, *rest = rest
    far, rest = rest[:6], rest[6:]
    outputs = rest[-8 - own : -2]
    weights, arrived = rest[-2:]
    normed, down, grad_normed, hidden, grad_gate, grad_up = outputs[:6]
    part = far[0].shape[0]
    first = pl.program_id(0) == 0

    def copies(which):
        rows = pl.ds(which * part, part)
        sources = (near.at[rows, :], near_core.at[rows, :], far[which], far[3 + which])
        for place, source in enumerate(sources):
            start = pl.multiple_of((ids[0] ^ place) * part, part)
            yield pltpu.make_async_copy(
                source,
                weights.at[which, pl.ds(start, part), :],
                arrived.at[which, place],
            )

    @pl.when(first)
    def _():
        for which in range(3):
            for copy in copies(which):
                copy.start()

    middle = tokens[0].astype(F32) + dot_nt(gated[0], mixer[...])
    if own:
        rest[-3][...] = middle
    values = (norm_forward(middle)[0] * gain[...].astype(F32)).astype(BF16)
    normed[0] = values

    @pl.when(first)
    def _():
        for which in range(3):
            for copy in copies(which):
                copy.wait()

    gate = dot_nn(values, weights[0])
    up = dot_nn(values, weights[1])
    grad_hidden = dot_nn(cotangent[0], weights[2])
    sigmoid = jax.nn.sigmoid(gate)
    silu = gate * sigmoid
    hidden_now = (silu * up).astype(BF16)
    hidden[0] = hidden_now
    gate_now = (grad_hidden * up * sigmoid * (1.0 + gate * (1.0 - sigmoid))).astype(BF16)
    up_now = (grad_hidden * silu).astype(BF16)
    grad_gate[0] = gate_now
    grad_up[0] = up_now
    grad_normed[...] = (dot_nt(gate_now, weights[0]) + dot_nt(up_now, weights[1])).astype(BF16)
    down[...] = dot_nt(hidden_now, weights[2]).astype(BF16)


def feedforward(ids, gated, mixer, tokens, gain, cotangent, places, which, earlier):
    seqs, width, model = tokens.shape
    units = places[0].shape[1]
    size = width // 2
    own = int(which == 3)

    def seq(i, ids):
        return (ids[3 + which], i, 0)

    def row(i, ids):
        return (i, 0)

    wide = jax.ShapeDtypeStruct((seqs, width, units), BF16)
    here = jax.ShapeDtypeStruct((width, model), BF16)
    first = 6 + len(places)
    return pl.pallas_call(
        functools.partial(feedforward_kernel, own),
        grid_spec=pltpu.PrefetchScalarGridSpec(
            num_scalar_prefetch=1,
            grid=(2,),
            in_specs=[
                pl.BlockSpec((1, size, model), seq),
                pl.BlockSpec((model, model), lambda i, ids: (0, 0), pipeline_mode=pl.Buffered(1)),
                pl.BlockSpec((1, size, model), seq),
                pl.BlockSpec((1, model), lambda i, ids: (0, 0)),
                pl.BlockSpec((1, size, model), seq),
            ]
            + [pl.BlockSpec(memory_space=pltpu.HBM)] * len(places)
            + [pl.BlockSpec(memory_space=pl.ANY)] * len(earlier),
            out_specs=[
                pl.BlockSpec((1, size, model), seq),
                pl.BlockSpec((size, model), row),
                pl.BlockSpec((size, model), row),
                pl.BlockSpec((1, size, units), seq),
                pl.BlockSpec((1, size, units), seq),
                pl.BlockSpec((1, size, units), seq),
            ]
            + [pl.BlockSpec((size, model), row)] * own,
            scratch_shapes=[
                pltpu.VMEM((3, model, units), BF16),
                pltpu.SemaphoreType.DMA((3, 4)),
            ],
        ),
        out_shape=[
            jax.ShapeDtypeStruct(tokens.shape, BF16),
            here,
            here,
            wide,
            wide,
            wide,
        ]
        + [jax.ShapeDtypeStruct((width, model), F32)] * own,
        input_output_aliases={first: 0, first + 1: 3, first + 2: 4, first + 3: 5} if earlier else {},
        compiler_params=pltpu.CompilerParams(vmem_limit_bytes=40 * MIB),
        cost_estimate=pl.CostEstimate(flops=0, bytes_accessed=0, transcendentals=0),
        name="feedforward",
    )(ids, gated, mixer, tokens, gain, cotangent, *places, *earlier)


def middle_gradient(parts, own, cotangent, gain):
    incoming = sum(part[...].astype(F32) for part in parts)
    plain, inverse = norm_forward(own[...])
    total = cotangent[0].astype(F32) + norm_backward(incoming, plain, inverse, gain[...].astype(F32))
    return total, jnp.sum(incoming * plain, axis=0, keepdims=True)


def edge_kernel(ids, part0, part1, part2, own, cotangent, gain, gate, out_weights, edge):
    mixed = middle_gradient((part0, part1, part2), own, cotangent, gain)[0].astype(BF16)
    edge[...] = (dot_nn(mixed, out_weights[...]) * gate[0].astype(F32)).astype(BF16)


def edge_gradient(ids, parts, own, cotangent, gain, gates, out_weights):
    width, model = own.shape
    rows = pl.BlockSpec((LEAD, model), lambda i, ids: (0, 0))
    return pl.pallas_call(
        edge_kernel,
        grid_spec=pltpu.PrefetchScalarGridSpec(
            num_scalar_prefetch=1,
            grid=(1,),
            in_specs=[
                rows, rows, rows, rows,
                pl.BlockSpec((1, LEAD, model), lambda i, ids: (ids[1], 0, 0)),
                pl.BlockSpec((1, model), lambda i, ids: (0, 0)),
                pl.BlockSpec((1, LEAD, model), lambda i, ids: (1, 1, 0)),
                pl.BlockSpec(out_weights.shape, lambda i, ids: (0, 0)),
            ],
            out_specs=rows,
        ),
        out_shape=jax.ShapeDtypeStruct((LEAD, model), BF16),
        compiler_params=pltpu.CompilerParams(vmem_limit_bytes=44 * MIB),
        cost_estimate=pl.CostEstimate(flops=0, bytes_accessed=0, transcendentals=0),
        name="edge_gradient",
    )(ids, *parts, own, cotangent, gain, gates, out_weights)


def mixer_backward_kernel(
    ids, part0, part1, part2, own, cotangent, gain, gates, out_weights, taps,
    grad_middle, grad_mixed, gain_grad, grad_convolved, grad_out_gate, tap_grads,
):
    @pl.when(pl.program_id(0) == 0)
    def _():
        here, gain_here = middle_gradient((part0, part1, part2), own, cotangent, gain)
        gain_grad[...] = gain_here
        grad_middle[...] = here
        grad_mixed[...] = here.astype(BF16)

    tap = taps[0].astype(F32)
    product = (gates[0].astype(F32) * gates[2].astype(F32)).astype(BF16).astype(F32)
    recent, previous, earlier = (
        product[LEAD:], pltpu.roll(product, 1, 0)[LEAD:], pltpu.roll(product, 2, 0)[LEAD:],
    )
    convolved = tap[0:1] * recent + tap[1:2] * previous + tap[2:3] * earlier
    grad_gated = dot_nn(grad_mixed[...], out_weights[...])
    grad_out_gate[...] = (grad_gated * convolved).astype(BF16)
    low = (grad_gated * gates[1, LEAD:, :].astype(F32)).astype(BF16)
    grad_convolved[...] = low
    low = low.astype(F32)
    tap_grads[0] = jnp.concatenate(
        [
            jnp.sum(low * recent, axis=0, keepdims=True),
            jnp.sum(low * previous, axis=0, keepdims=True),
            jnp.sum(low * earlier, axis=0, keepdims=True),
            jnp.zeros((5, low.shape[1]), F32),
        ]
    )


def mixer_backward(ids, parts, own, cotangent, gain, gates, out_weights, taps):
    width, model = own.shape
    long = gates.shape[1]
    count = taps.shape[0]
    part = model // count
    whole = pl.BlockSpec((width, model), lambda j, ids: (0, 0))
    once = pl.BlockSpec((width, model), lambda j, ids: (0, 0), pipeline_mode=pl.Buffered(1))
    line = pl.BlockSpec((1, model), lambda j, ids: (0, 0))
    column = pl.BlockSpec((width, part), lambda j, ids: (0, j))
    matrix = jax.ShapeDtypeStruct((width, model), BF16)
    return pl.pallas_call(
        mixer_backward_kernel,
        grid_spec=pltpu.PrefetchScalarGridSpec(
            num_scalar_prefetch=1,
            grid=(count,),
            in_specs=[
                once, once, once, once,
                pl.BlockSpec((1, width, model), lambda j, ids: (ids[1], 0, 0), pipeline_mode=pl.Buffered(1)),
                line,
                pl.BlockSpec((3, long, part), lambda j, ids: (0, 0, j)),
                pl.BlockSpec((model, part), lambda j, ids: (0, j)),
                pl.BlockSpec((1, LEAD, part), lambda j, ids: (j, 0, 0)),
            ],
            out_specs=[
                whole, whole, line, column, column,
                pl.BlockSpec((1, 8, part), lambda j, ids: (j, 0, 0)),
            ],
        ),
        out_shape=[
            jax.ShapeDtypeStruct((width, model), F32), matrix, jax.ShapeDtypeStruct((1, model), F32),
            matrix, matrix, jax.ShapeDtypeStruct((count, 8, part), F32),
        ],
        compiler_params=pltpu.CompilerParams(vmem_limit_bytes=44 * MIB),
        cost_estimate=pl.CostEstimate(flops=0, bytes_accessed=0, transcendentals=0),
        name="mixer_backward",
    )(ids, *parts, own, cotangent, gain, gates, out_weights, taps)


def input_backward_kernel(
    ids, grad_convolved, edge, gates, grad_out_gate, taps, weights, grad_middle, tokens, gain,
    grad_first, grad_third, grad_tokens, gain_grad, total,
):
    block = pl.program_id(0)
    width = grad_convolved.shape[0]
    tap = taps[0].astype(F32)
    longer = jnp.concatenate([grad_convolved[...], edge[...]]).astype(F32)
    count = longer.shape[0]
    grad_product = (
        tap[0:1] * longer
        + tap[1:2] * pltpu.roll(longer, count - 1, 0)
        + tap[2:3] * pltpu.roll(longer, count - 2, 0)
    )[:width]
    first = (grad_product * gates[2, LEAD:, :].astype(F32)).astype(BF16)
    third = (grad_product * gates[0, LEAD:, :].astype(F32)).astype(BF16)
    grad_first[...] = first
    grad_third[...] = third
    here = dot_nt(jnp.concatenate([first, grad_out_gate[...], third], axis=1), weights[0])

    @pl.when(block == 0)
    def _():
        total[...] = here

    @pl.when(block > 0)
    def _():
        total[...] += here

    @pl.when(block == pl.num_programs(0) - 1)
    def _():
        incoming = total[...]
        plain, inverse = norm_forward(tokens[0].astype(F32))
        gain_grad[...] = jnp.sum(incoming * plain, axis=0, keepdims=True)
        grad_tokens[...] = (
            grad_middle[...] + norm_backward(incoming, plain, inverse, gain[...].astype(F32))
        ).astype(BF16)


def input_backward(ids, grad_convolved, edge, gates, grad_out_gate, taps, weights, grad_middle, tokens, gain):
    width, model = grad_middle.shape
    long = gates.shape[1]
    count = taps.shape[0]
    part = model // count
    once = pl.BlockSpec((width, model), lambda j, ids: (0, 0), pipeline_mode=pl.Buffered(1))
    whole = pl.BlockSpec((width, model), lambda j, ids: (0, 0))
    line = pl.BlockSpec((1, model), lambda j, ids: (0, 0))
    column = pl.BlockSpec((width, part), lambda j, ids: (0, j))
    matrix = jax.ShapeDtypeStruct((width, model), BF16)
    return pl.pallas_call(
        input_backward_kernel,
        grid_spec=pltpu.PrefetchScalarGridSpec(
            num_scalar_prefetch=1,
            grid=(count,),
            in_specs=[
                column,
                pl.BlockSpec((LEAD, part), lambda j, ids: (0, j)),
                pl.BlockSpec((3, long, part), lambda j, ids: (0, 0, j)),
                column,
                pl.BlockSpec((1, LEAD, part), lambda j, ids: (j, 0, 0)),
                pl.BlockSpec((1, model, 3 * part), lambda j, ids: (j, 0, 0)),
                once,
                pl.BlockSpec((1, width, model), lambda j, ids: (ids[1], 0, 0), pipeline_mode=pl.Buffered(1)),
                line,
            ],
            out_specs=[column, column, whole, line],
            scratch_shapes=[pltpu.VMEM((width, model), F32)],
        ),
        out_shape=[matrix, matrix, matrix, jax.ShapeDtypeStruct((1, model), F32)],
        compiler_params=pltpu.CompilerParams(vmem_limit_bytes=44 * MIB),
        cost_estimate=pl.CostEstimate(flops=0, bytes_accessed=0, transcendentals=0),
        name="input_backward",
    )(ids, grad_convolved, edge, gates, grad_out_gate, taps, weights, grad_middle, tokens, gain)


def split_rows(ids, g):
    return ids[7 + g]


def feedforward_gradient_kernel(ids, left, right, send, keep):
    result = dot_tn(left[...], right[...]).astype(BF16)

    @pl.when(pl.program_id(0) < 2)
    def _():
        send[0] = result

    @pl.when(pl.program_id(0) >= 2)
    def _():
        keep[0] = result


def feedforward_gradient(ids, left, right):
    tokens, model = left.shape
    units = right.shape[1]
    part = model // 4
    shape = jax.ShapeDtypeStruct((2, part, units), BF16)
    return pl.pallas_call(
        feedforward_gradient_kernel,
        grid_spec=pltpu.PrefetchScalarGridSpec(
            num_scalar_prefetch=1,
            grid=(4,),
            in_specs=[
                pl.BlockSpec((tokens, part), lambda g, ids: (0, split_rows(ids, g))),
                pl.BlockSpec((tokens, units), lambda g, ids: (0, 0), pipeline_mode=pl.Buffered(1)),
            ],
            out_specs=[
                pl.BlockSpec((1, part, units), lambda g, ids: (jnp.minimum(g, 1), 0, 0)),
                pl.BlockSpec((1, part, units), lambda g, ids: (jnp.maximum(g - 2, 0), 0, 0)),
            ],
        ),
        out_shape=[shape, shape],
        compiler_params=pltpu.CompilerParams(vmem_limit_bytes=32 * MIB),
        cost_estimate=pl.CostEstimate(flops=0, bytes_accessed=0, transcendentals=0),
        name="feedforward_gradient",
    )(ids, left, right)


def mixer_gradient_kernel(ids, rows, mixed, first, second, third, gated, send, keep):
    part = mixed.shape[1]
    here = []
    for left, right in (
        (rows[0, LEAD:], first[...]),
        (rows[0, LEAD:], second[...]),
        (rows[0, LEAD:], third[...]),
        (mixed[...], gated[0]),
    ):
        here.append(dot_tn(left, right).astype(BF16))

    def store(out):
        for matrix, value in enumerate(here):
            for block in range(4):
                for upper in range(2):
                    out[0, ids[2] ^ upper, ids[11 + block], matrix] = value[
                        upper * part // 2 : (upper + 1) * part // 2, block * part : (block + 1) * part
                    ]

    @pl.when(pl.program_id(0) < 2)
    def _():
        store(send)

    @pl.when(pl.program_id(0) >= 2)
    def _():
        store(keep)


def mixer_gradient(ids, rows, mixed, first, second, third, gated):
    width, model = mixed.shape
    long = rows.shape[1]
    part = model // 4
    shape = jax.ShapeDtypeStruct((2, 2, 4, 4, part // 2, part), BF16)
    block = (1, 2, 4, 4, part // 2, part)
    whole = pl.BlockSpec((width, model), lambda g, ids: (0, 0))
    return pl.pallas_call(
        mixer_gradient_kernel,
        grid_spec=pltpu.PrefetchScalarGridSpec(
            num_scalar_prefetch=1,
            grid=(4,),
            in_specs=[
                pl.BlockSpec((1, long, part), lambda g, ids: (ids[1], 0, split_rows(ids, g))),
                pl.BlockSpec((width, part), lambda g, ids: (0, split_rows(ids, g))),
                whole, whole, whole,
                pl.BlockSpec((1, width, model), lambda g, ids: (ids[1], 0, 0)),
            ],
            out_specs=[
                pl.BlockSpec(block, lambda g, ids: (jnp.minimum(g, 1), 0, 0, 0, 0, 0)),
                pl.BlockSpec(block, lambda g, ids: (jnp.maximum(g - 2, 0), 0, 0, 0, 0, 0)),
            ],
        ),
        out_shape=[shape, shape],
        compiler_params=pltpu.CompilerParams(vmem_limit_bytes=40 * MIB),
        cost_estimate=pl.CostEstimate(flops=0, bytes_accessed=0, transcendentals=0),
        name="mixer_gradient",
    )(ids, rows, mixed, first, second, third, gated)


def local_by_links(
    tokens, norm_gain, w_in, conv_weight, convolution_out_weight, ffn_gain, w_gate, w_up, w_down, cotangent
):
    seqs, width, model = tokens.shape
    part = w_in.shape[1]
    units = w_gate.shape[1]
    shard, side, level = (lax.axis_index(name) for name in ("shard", "context", "tensor"))
    end = jnp.logical_or(level == 0, level == 3)
    order = [
        jnp.where(level < 2, 3, 0), jnp.where(level < 2, 2, 1), level ^ 1, level,
    ]
    place = [sum(jnp.where((level + block) % 4 == order[k], k, 0) for k in range(4)) for block in range(4)]
    ids = jnp.stack(
        [shard, level, side] + order + [shard ^ 1, shard ^ 3, shard, shard ^ 2] + place
    ).astype(jnp.int32)
    gain_one = norm_gain.reshape(1, model)
    gain_two = ffn_gain.reshape(1, model)
    def placed(own, others, dtype):
        out = jnp.zeros((seqs, width, model), dtype)
        for bits, block in enumerate((own,) + others):
            out = lax.dynamic_update_slice(out, block.astype(dtype)[None], (level ^ bits, 0, 0))
        return out

    taps_near = jnp.concatenate([conv_weight, jnp.zeros((LEAD - 3, part), BF16)])
    near = jnp.concatenate(
        [w_in[0], w_in[1], taps_near, w_in[2], convolution_out_weight.T, taps_near]
    )
    half = near.shape[0] // 2

    def sides(value):
        return [lax.dynamic_slice_in_dim(value, (side ^ bit) * half, half, 0) for bit in range(2)]

    near, near_side, near_else = together(near, *sides(near))
    far = to_y(near)
    near_right, near_left = shifted(near_side, -1), shifted(near_side, 1)
    edge = lax.ppermute(tokens[:, width - 2 :, :], "context", [(0, 1)])
    w_down = w_down.T
    feed = jnp.concatenate([w_gate, w_up, w_down])
    far, near_right, near_left, edge, feed, near_side, near_else, w_gate, w_up, w_down = together(
        far, near_right, near_left, edge, feed, near_side, near_else, w_gate, w_up, w_down
    )

    far_side, far_else = sides(far)
    far_right, far_left = shifted(far_side, -1), shifted(far_side, 1)
    near_over = to_x(jnp.concatenate([near_right, near_left]))
    far_gate = to_y(w_gate)
    mine = together(jnp.concatenate([near_side, near_else, far_side, far_else]))[0]
    other = to_core(mine)
    rows = jnp.concatenate([jnp.zeros((seqs, LEAD - 2, model), BF16), edge, tokens], axis=1).astype(F32)
    rows = (norm_forward(rows)[0] * gain_one.astype(F32)).astype(BF16)
    state = mixer_forward(ids, rows, (mine, other), 0, ())
    far_right, far_left, near_over, near_right, near_left, rows, feed, w_up, w_down, far_gate, *state = together(
        far_right, far_left, near_over, near_right, near_left, rows, feed, w_up, w_down, far_gate, *state
    )

    near_far, far_far = shifted(near_right, -1), shifted(far_left, 1)
    far_over = to_x(jnp.concatenate([far_right, far_left]))
    far_up = to_y(w_up)
    feed_core = to_core(feed)
    near_far, far_far, far_over, feed_core, far_up, w_down, *state = together(
        near_far, far_far, far_over, feed_core, far_up, w_down, *state
    )

    last_over = to_x(jnp.concatenate([near_far, far_far]))
    far_down = to_y(w_down)
    for block, rows_of, (a, b) in (
        (1, slice(None, half), (near_right, far_right)),
        (3, slice(half, None), (near_left, far_left)),
    ):
        mine = together(jnp.concatenate([a, near_over[rows_of], b, far_over[rows_of]]))[0]
        state = mixer_forward(ids, rows, (mine, to_core(mine)), block, state)
    last_over, far_down, far_gate, far_up, *state = together(
        last_over, far_down, far_gate, far_up, *state
    )

    mine = together(jnp.concatenate([near_far, last_over[:half], far_far, last_over[half:]]))[0]
    state = mixer_forward(ids, rows, (mine, to_core(mine)), 2, state)
    gated, weights, out_weights, gates = state
    far_all = (far_gate, far_up, far_down)
    core_all = [to_core(value) for value in far_all]
    gated, weights, out_weights, gates, *core_all = together(gated, weights, out_weights, gates, *core_all)
    places = (feed, feed_core, *far_all, *core_all)
    taps = jnp.stack([near_side[2 * part :], near_right[2 * part :], near_far[2 * part :], near_left[2 * part :]])

    def forward(which, earlier):
        normed, down, grad, *wide = feedforward(
            ids, gated, out_weights, tokens, gain_two, cotangent, places, which, earlier
        )
        return down, grad, (normed, *wide[:3]), wide[3:]

    down0, grad0, done, _ = forward(0, ())
    down0, grad0, *done = together(down0, grad0, *done)

    grad_pair0 = pair(grad0)
    down1, grad1, done, _ = forward(1, tuple(done))
    grad_pair0, down1, grad1, *done = together(grad_pair0, down1, grad1, *done)

    grad_pair1 = pair(grad1)
    grad_over0 = across(added(grad0, grad_pair0))
    down2, grad2, done, _ = forward(2, tuple(done))
    grad_pair1, grad_over0, down2, grad2, *done = together(grad_pair1, grad_over0, down2, grad2, *done)

    grad_pair2 = pair(added(grad2, grad_over0))
    grad_over1 = across(added(grad1, grad_pair1))
    down3, grad3, done, (middle_own,) = forward(3, tuple(done))
    normed, hidden, grad_gate, grad_up = (v.reshape(seqs * width, v.shape[2]) for v in done)
    grad_pair2, grad_over1, grad3, normed, hidden, grad_gate, grad_up, down0 = together(
        grad_pair2, grad_over1, grad3, normed, hidden, grad_gate, grad_up, down0
    )

    down_pair0 = pair(down0)
    grad_parts = (grad3, grad_pair2, grad_over1)
    edge = edge_gradient(ids, grad_parts, middle_own, cotangent, gain_two, gates, out_weights)
    edge = lax.ppermute(edge, "context", [(1, 0)])
    grad_middle, grad_mixed, gain_two_grad, grad_convolved, grad_out_gate, tap_grads = mixer_backward(
        ids, grad_parts, middle_own, cotangent, gain_two, gates, out_weights, taps
    )
    edge, grad_convolved = together(edge, grad_convolved)
    grad_first, grad_third, tokens_own, gain_one_grad = input_backward(
        ids, grad_convolved, edge, gates, grad_out_gate, taps, weights, grad_middle, tokens, gain_one
    )
    (
        down_pair0, tokens_own, grad_first, grad_third, grad_mixed, gain_one_grad, normed, hidden, grad_gate, grad_up,
    ) = together(
        down_pair0, tokens_own, grad_first, grad_third, grad_mixed, gain_one_grad, normed, hidden, grad_gate, grad_up,
    )

    tokens_pair = pair(tokens_own)
    tokens_over = across(tokens_own)
    send_mixer, keep_mixer = mixer_gradient(
        ids, rows, grad_mixed, grad_first, grad_out_gate, grad_third, gated
    )
    tap_rows = tap_grads[:, :3].transpose(1, 0, 2)
    tap_rows = jnp.roll(tap_rows, level, axis=1).reshape(3, model)
    small = jnp.concatenate([gain_one_grad, gain_two_grad, tap_rows, jnp.zeros((3, model), F32)])
    small = small + swapped(small, "tensor", 1)
    tokens_pair, tokens_over, send_mixer, keep_mixer, hidden, grad_gate, grad_up, small, down0, down1, down2 = together(
        tokens_pair, tokens_over, send_mixer, keep_mixer, hidden, grad_gate, grad_up, small, down0, down1, down2
    )

    mixed_pair1 = pair(jnp.where(end, down1, tokens_over))
    tokens_over_end = across(tokens_pair)
    core_mixer = to_core(send_mixer)
    send_gate, keep_gate = feedforward_gradient(ids, normed, grad_gate)
    send_up, keep_up = feedforward_gradient(ids, normed, grad_up)
    small = small + swapped(small, "tensor", 2)
    down_sum0 = added(down0, down_pair0)
    (
        mixed_pair1, tokens_over_end, core_mixer, send_gate, keep_gate, send_up, keep_up, small, down_sum0, hidden,
    ) = together(
        mixed_pair1, tokens_over_end, core_mixer, send_gate, keep_gate, send_up, keep_up, small, down_sum0, hidden,
    )

    mixed_pair2 = pair(jnp.where(end, down2, tokens_over_end))
    down_over0 = across(down_sum0)
    core_gate = to_core(send_gate)
    small = small + to_x(small)
    send_down, keep_down = feedforward_gradient(ids, cotangent.reshape(seqs * width, model), hidden)
    sum_mixer = added(keep_mixer, core_mixer)
    low, high = slice(None, part // 4), slice(part // 4, None)
    here_low, send_low = sum_mixer[0, :, :, :, low], sum_mixer[1, :, :, :, low]
    here_high, send_high = sum_mixer[:, 0, :, :, high], sum_mixer[:, 1, :, :, high]
    down_sum1 = added(down1, mixed_pair1)
    (
        mixed_pair2, down_over0, core_gate, send_up, send_down, keep_down, here_low, send_low, here_high,
        send_high, down_sum1, small, tokens_own,
    ) = together(
        mixed_pair2, down_over0, core_gate, send_up, send_down, keep_down, here_low, send_low, here_high,
        send_high, down_sum1, small, tokens_own,
    )

    down_pair3 = pair(added(down2, down_over0))
    down_over1 = across(down_sum1)
    y_low, x_high = to_y(send_low), to_x(send_high)
    grad_tokens = placed(
        tokens_own,
        (
            tokens_pair,
            jnp.where(end, mixed_pair1, tokens_over_end),
            jnp.where(end, mixed_pair2, tokens_over),
        ),
        F32,
    )
    sum_gate = added(keep_gate, core_gate)
    core_both = to_core(jnp.concatenate([send_up, send_down]))
    keep_both = jnp.concatenate([keep_up, keep_down])
    down_pair3, down_over1, y_low, x_high, grad_tokens, sum_gate, core_both, keep_both, small = together(
        down_pair3, down_over1, y_low, x_high, grad_tokens, sum_gate, core_both, keep_both, small
    )

    out_own = rounded(
        middle_own
        + down3.astype(F32)
        + jnp.where(end, down_pair3, mixed_pair2).astype(F32)
        + down_over1.astype(F32)
    )
    out_pair = pair(out_own)
    out_over = across(out_own)
    half_low = added(here_low, y_low)
    half_high = added(here_high, x_high)
    x_low, y_high = to_x(half_low[1]), to_y(half_high[1])
    mixer = jnp.concatenate([added(half_low[0], x_low), added(half_high[0], y_high)], axis=2)
    y_gate = to_y(sum_gate[1])
    sum_both = added(keep_both, core_both)
    send_both = jnp.concatenate([sum_both[1], sum_both[3]])
    here_both = jnp.concatenate([sum_both[0], sum_both[2]])
    out_pair, out_over, mixer, send_both, here_both, y_gate, small = together(
        out_pair, out_over, mixer, send_both, here_both, y_gate, small
    )

    out_over_end = across(out_pair)
    out_out2 = outward(out_over)
    mixer_in = inward(mixer[:3])
    y_both = to_y(send_both)
    mine_gate = rounded(added(sum_gate[0], y_gate))
    total_gate = mine_gate.astype(F32) + to_x(mine_gate).astype(F32)
    out_over_end, out_out2, mixer_in, y_both, total_gate, small = together(
        out_over_end, out_out2, mixer_in, y_both, total_gate, small
    )

    out_out3 = outward(out_over_end)
    mixer_over = across(added(mixer[:2], mixer_in[:2]))
    small = small + to_core(small)
    small = small + to_y(small)
    mixer_out = outward(added(mixer[2], mixer_over[0]))
    y_both, mixer_over = together(y_both, mixer_over)
    mine_both = rounded(added(here_both, y_both))
    total_both = mine_both.astype(F32) + to_x(mine_both).astype(F32)
    total_up, total_down = total_both[:part], total_both[part:].T
    mine = rounded(
        sum(value.astype(F32) for value in (mixer[3], mixer_out, mixer_in[2], mixer_over[1]))
    )
    other = to_x(mine)
    total = jnp.concatenate(
        [jnp.where(side == 0, mine, other), jnp.where(side == 0, other, mine)], axis=1
    ).astype(F32)
    total_taps = lax.dynamic_slice(small, (2, level * part), (3, part))
    block_out = placed(
        out_own,
        (out_pair, jnp.where(end, out_out2, out_over_end), jnp.where(end, out_out3, out_over)),
        BF16,
    )
    return (
        block_out, grad_tokens, small[0], total[:3], total_taps, total[3].T, small[1],
        total_gate, total_up, total_down,
    )


def from_behind(value, axis, steps):
    count = lax.axis_size(axis)
    initial, last = (max(0, -steps), min(count, count - steps))
    return lax.ppermute(value, axis, [(source, source + steps) for source in range(initial, last)])


def norm_backward_and_gain(grad_normed, plain, inverse, gain):
    grad_plain = grad_normed * gain
    grad_values = inverse * (
        grad_plain - plain * jnp.mean(grad_plain * plain, axis=-1, keepdims=True)
    )
    leading = tuple(range(grad_normed.ndim - 1))
    return (grad_values, jnp.sum(grad_normed * plain, axis=leading))


def local(
    tokens,
    norm_gain,
    w_in,
    conv_weight,
    convolution_out_weight,
    ffn_gain,
    w_gate,
    w_up,
    w_down,
    cotangent,
):
    input_rows = tokens.astype(jnp.float32)
    gain_one = norm_gain.astype(jnp.float32)
    gain_two = ffn_gain.astype(jnp.float32)
    taps = conv_weight.astype(jnp.float32)
    seqs, width, model = tokens.shape
    (
        complete_input_weight,
        complete_output_weight,
        feedforward_gate_weight,
        feedforward_up_weight,
        feedforward_down_weight,
    ) = (
        lax.all_gather(w_in, "shard", axis=1, tiled=True),
        lax.all_gather(convolution_out_weight, "shard", axis=1, tiled=True),
        lax.all_gather(w_gate, "shard", axis=0, tiled=True),
        lax.all_gather(w_up, "shard", axis=0, tiled=True),
        lax.all_gather(w_down, "shard", axis=1, tiled=True),
    )
    plain_one, inverse_one = norm_forward(input_rows)
    first_normalized = (plain_one * gain_one).astype(jnp.bfloat16)
    projection = jnp.einsum(
        "uiq,tqz->tuiz", first_normalized, complete_input_weight, preferred_element_type=jnp.float32
    )
    in_gate = projection[0]
    out_gate = projection[1]
    conv_input = projection[2]
    product = (in_gate * conv_input).astype(jnp.bfloat16)
    edge = from_behind(product[:, width - 2 :, :], "context", 1)
    extended = jnp.concatenate([edge, product], axis=1).astype(jnp.float32)
    recent = extended[:, 2:, :]
    previous = extended[:, 1 : width + 1, :]
    earlier = extended[:, :width, :]
    convolved = taps[0] * recent + taps[1] * previous + taps[2] * earlier
    gated_product = (out_gate * convolved).astype(jnp.bfloat16)
    partial_mixer_output = jnp.einsum(
        "zaw,wk->zak", gated_product, complete_output_weight, preferred_element_type=jnp.float32
    )
    residual_middle = input_rows + lax.psum(partial_mixer_output, "tensor")
    plain_two, inverse_two = norm_forward(residual_middle)
    second_normalized = (plain_two * gain_two).astype(jnp.bfloat16)
    gate_branch = jnp.einsum(
        "mut,tz->muz",
        second_normalized,
        feedforward_gate_weight,
        preferred_element_type=jnp.float32,
    )
    up_projection_branch = jnp.einsum(
        "mut,tz->muz", second_normalized, feedforward_up_weight, preferred_element_type=jnp.float32
    )
    sigmoid_gate = jax.nn.sigmoid(gate_branch)
    silu_gate = gate_branch * sigmoid_gate
    hidden_state = (silu_gate * up_projection_branch).astype(jnp.bfloat16)
    partial_feedforward = jnp.einsum(
        "eny,yv->env", hidden_state, feedforward_down_weight, preferred_element_type=jnp.float32
    )
    block_out = (
        residual_middle
        + lax.psum(partial_feedforward.astype(jnp.bfloat16), "tensor").astype(jnp.float32)
    ).astype(jnp.bfloat16)
    grad_out = cotangent.astype(jnp.float32)
    hidden_gradient = jnp.einsum(
        "qmn,pn->qmp", cotangent, feedforward_down_weight, preferred_element_type=jnp.float32
    )
    down_gradient = jnp.einsum(
        "eiu,eix->ux", hidden_state, cotangent, preferred_element_type=jnp.float32
    )
    gate_gradient = (
        hidden_gradient
        * up_projection_branch
        * sigmoid_gate
        * (1.0 + gate_branch * (1.0 - sigmoid_gate))
    ).astype(jnp.bfloat16)
    up_gradient = (hidden_gradient * silu_gate).astype(jnp.bfloat16)
    grad_w_gate = jnp.einsum(
        "rnj,rnt->jt", second_normalized, gate_gradient, preferred_element_type=jnp.float32
    )
    up_weight_gradient = jnp.einsum(
        "rnj,rnt->jt", second_normalized, up_gradient, preferred_element_type=jnp.float32
    )
    partial_normed_two = jnp.einsum(
        "wxo,qo->wxq", gate_gradient, feedforward_gate_weight, preferred_element_type=jnp.float32
    )
    partial_normed_two = partial_normed_two + jnp.einsum(
        "wxo,qo->wxq", up_gradient, feedforward_up_weight, preferred_element_type=jnp.float32
    )
    grad_normed_two = lax.psum(partial_normed_two, "tensor")
    grad_rows_two, gain_grad_two = norm_backward_and_gain(grad_normed_two, plain_two, inverse_two, gain_two)
    grad_middle = grad_out + grad_rows_two
    mixer_output_gradient = grad_middle.astype(jnp.bfloat16)
    grad_gated = jnp.einsum(
        "ymo,bo->ymb",
        mixer_output_gradient,
        complete_output_weight,
        preferred_element_type=jnp.float32,
    )
    out_weight_gradient = jnp.einsum(
        "miy,miq->yq", gated_product, mixer_output_gradient, preferred_element_type=jnp.float32
    )
    grad_convolved = (grad_gated * out_gate).astype(jnp.bfloat16)
    grad_out_gate = grad_gated * convolved
    grad_edge = from_behind(grad_convolved[:, :2, :], "context", -1)
    grad_extended = jnp.concatenate([grad_convolved, grad_edge], axis=1).astype(jnp.float32)
    grad_product = (
        taps[0] * grad_extended[:, :width, :]
        + taps[1] * grad_extended[:, 1 : width + 1, :]
        + taps[2] * grad_extended[:, 2:, :]
    )
    grad_local = grad_extended[:, :width, :]
    tap_grads = jnp.stack(
        [
            jnp.sum(grad_local * recent, axis=(0, 1)),
            jnp.sum(grad_local * previous, axis=(0, 1)),
            jnp.sum(grad_local * earlier, axis=(0, 1)),
        ]
    )
    projection_gradient = jnp.stack(
        [
            (grad_product * conv_input).astype(jnp.bfloat16),
            grad_out_gate.astype(jnp.bfloat16),
            (grad_product * in_gate).astype(jnp.bfloat16),
        ]
    )
    grad_w_in = jnp.einsum(
        "pxw,gpxt->gwt", first_normalized, projection_gradient, preferred_element_type=jnp.float32
    )
    partial_normed_one = jnp.einsum(
        "ireo,ivo->rev",
        projection_gradient,
        complete_input_weight,
        preferred_element_type=jnp.float32,
    )
    shard_in, shard_out, shard_gate, shard_up, shard_down = (
        lax.psum_scatter(
            grad_w_in.astype(jnp.bfloat16), "shard", scatter_dimension=1, tiled=True
        ).astype(jnp.float32),
        lax.psum_scatter(
            out_weight_gradient.astype(jnp.bfloat16), "shard", scatter_dimension=1, tiled=True
        ).astype(jnp.float32),
        lax.psum_scatter(
            grad_w_gate.astype(jnp.bfloat16), "shard", scatter_dimension=0, tiled=True
        ).astype(jnp.float32),
        lax.psum_scatter(
            up_weight_gradient.astype(jnp.bfloat16), "shard", scatter_dimension=0, tiled=True
        ).astype(jnp.float32),
        lax.psum_scatter(
            down_gradient.astype(jnp.bfloat16), "shard", scatter_dimension=1, tiled=True
        ).astype(jnp.float32),
    )
    total_in, total_out, total_gate, total_up, total_down = (
        lax.psum(shard_in.astype(jnp.bfloat16), "context").astype(jnp.float32),
        lax.psum(shard_out.astype(jnp.bfloat16), "context").astype(jnp.float32),
        lax.psum(shard_gate.astype(jnp.bfloat16), "context").astype(jnp.float32),
        lax.psum(shard_up.astype(jnp.bfloat16), "context").astype(jnp.float32),
        lax.psum(shard_down.astype(jnp.bfloat16), "context").astype(jnp.float32),
    )
    grad_normed_one = lax.psum(partial_normed_one.astype(jnp.bfloat16), "tensor").astype(
        jnp.float32
    )
    grad_rows_one, gain_grad_one = norm_backward_and_gain(grad_normed_one, plain_one, inverse_one, gain_one)
    grad_tokens = grad_middle + grad_rows_one
    total_gain_one, total_taps, total_gain_two = lax.psum(
        (gain_grad_one, tap_grads, gain_grad_two), ("shard", "context")
    )
    return (
        block_out,
        grad_tokens,
        total_gain_one,
        total_in,
        total_taps,
        total_out,
        total_gain_two,
        total_gate,
        total_up,
        total_down,
    )


def solution(mesh):
    in_specs = (
        P("shard", "context", None),
        P(),
        P(None, "shard", "tensor"),
        P(None, "tensor"),
        P("tensor", "shard"),
        P(),
        P("shard", "tensor"),
        P("shard", "tensor"),
        P("tensor", "shard"),
        P("shard", "context", None),
    )
    out_specs = (
        P("shard", "context", None),
        P("shard", "context", None),
        P(),
        P(None, "shard", "tensor"),
        P(None, "tensor"),
        P("tensor", "shard"),
        P(),
        P("shard", "tensor"),
        P("shard", "tensor"),
        P("tensor", "shard"),
    )
    sizes = mesh.shape
    by_links = (sizes["shard"], sizes["context"], sizes["tensor"]) == (4, 2, 4)
    body = local_by_links if by_links else local
    return jax.shard_map(body, mesh=mesh, in_specs=in_specs, out_specs=out_specs, check_vma=False)
```
